32 devices in a mesh: seq: 4 (over y, core), batch: 8 (over z, x).
Axes of the slice: x: 2, y: 2, z: 4, core: 2. Of those that a mesh axis runs over, the one named last changes fastest.
Arguments:
- tokens: bfloat16 [24, 1024, 768], P('batch', 'seq'), may hold values from -6 to 6
- cotangent: bfloat16 [24, 1024, 768], P('batch', 'seq'), may hold values from -6 to 6
- lengths: int32 [24], P('batch'), may hold values from 512 to 1024, as said below
- norm1_gain: float32 [768], replicated, may hold values from 0.1 to 1.9
- norm1_shift: float32 [768], replicated, may hold values from -3 to 3
- in_weight: bfloat16 [768, 2304], replicated, may hold values from -0.21875 to 0.21875
- in_bias: float32 [2304], replicated, may hold values from -3 to 3
- conv_weight: float32 [3, 2304], replicated, may hold values from -3.5 to 3.5
- conv_bias: float32 [2304], replicated, may hold values from -3 to 3
- filter_in: float32 [33, 64], replicated, may hold values from -1 to 1
- filter_in_bias: float32 [64], replicated, may hold values from -4 to 4
- filter_mid: float32 [64, 64], replicated, may hold values from -0.75 to 0.75
- filter_mid_bias: float32 [64], replicated, may hold values from -4 to 4
- filter_last: float32 [64, 64], replicated, may hold values from -0.75 to 0.75
- filter_last_bias: float32 [64], replicated, may hold values from -4 to 4
- filter_out: float32 [64, 768], replicated, may hold values from -0.046875 to 0.046875
- decay_rate: float32 [768], replicated, may hold values from 0.3 to 30
- skip_gain: float32 [768], replicated, may hold values from -4 to 4
- out_weight: bfloat16 [768, 768], replicated, may hold values from -0.21875 to 0.21875
- out_bias: float32 [768], replicated, may hold values from -2 to 2
- norm2_gain: float32 [768], replicated, may hold values from 0.1 to 1.9
- norm2_shift: float32 [768], replicated, may hold values from -3 to 3
- up_weight: bfloat16 [768, 3072], replicated, may hold values from -0.21875 to 0.21875
- up_bias: float32 [3072], replicated, may hold values from -3 to 3
- down_weight: bfloat16 [3072, 768], replicated, may hold values from -0.109375 to 0.109375
- down_bias: float32 [768], replicated, may hold values from -2 to 2
Outputs:
- block_out: bfloat16 [24, 1024, 768], P('batch', 'seq')
- grad_tokens: float32 [24, 1024, 768], P('batch', 'seq')
- grad_norm1_gain: float32 [768], replicated
- grad_norm1_shift: float32 [768], replicated
- grad_in_weight: float32 [768, 2304], replicated
- grad_in_bias: float32 [2304], replicated
- grad_conv_weight: float32 [3, 2304], replicated
- grad_conv_bias: float32 [2304], replicated
- grad_filter_in: float32 [33, 64], replicated
- grad_filter_in_bias: float32 [64], replicated
- grad_filter_mid: float32 [64, 64], replicated
- grad_filter_mid_bias: float32 [64], replicated
- grad_filter_last: float32 [64, 64], replicated
- grad_filter_last_bias: float32 [64], replicated
- grad_filter_out: float32 [64, 768], replicated
- grad_decay_rate: float32 [768], replicated
- grad_skip_gain: float32 [768], replicated
- grad_out_weight: float32 [768, 768], replicated
- grad_out_bias: float32 [768], replicated
- grad_norm2_gain: float32 [768], replicated
- grad_norm2_shift: float32 [768], replicated
- grad_up_weight: float32 [768, 3072], replicated
- grad_up_bias: float32 [3072], replicated
- grad_down_weight: float32 [3072, 768], replicated
- grad_down_bias: float32 [768], replicated
The draws below stay inside these ranges and needn't reach their ends.
Inputs may be any that keep to these rules, and one draw needn't show every extreme that they name: `lengths`: on each index of batch, one of its 3 buckets, chosen by the seed, has length 1024.
All inputs are finite; a program needn't handle non-finite values.
Results may differ from the reference program's by a relative error of at most 0.011.
Values may be sent and summed in bfloat16 or wider, within the bound.
No kernel may reach another device: no remote copies, remote signals or barrier semaphores. Data moves between devices by JAX's collectives and lax.ppermute only.
A program may use at most 320 MiB of HBM per device.

```python
import math
import jax
import jax.numpy as jnp
from jax import lax

D = 768
FF = 3072
FILT = 64
EMB = 33
BUCKETS = 3
SEQ_LEN = 1024
NBUCK = 24
LEN_MIN = 512


def draw_lengths(key, part):
    key = jax.random.fold_in(key, 17)
    first_key, second_key = jax.random.split(key)
    spread_len = jax.random.randint(first_key, (NBUCK,), LEN_MIN, SEQ_LEN + 1)
    chosen = jax.random.randint(second_key, (NBUCK // BUCKETS,), 0, BUCKETS)
    slot_index = jnp.arange(NBUCK, dtype=jnp.int32) % BUCKETS
    full_len = slot_index == jnp.repeat(chosen, BUCKETS)
    return jnp.where(full_len, SEQ_LEN, spread_len).astype(jnp.int32)


def block_scale(key, dims, shards, low, high):
    factor_of, own = 1.0, jax.random.fold_in(key, 6)
    for dim, shards_of in shards:
        steps = jnp.exp(jax.random.uniform(jax.random.fold_in(own, dim), (shards_of,), jnp.float32, low / len(shards), high / len(shards)))
        factor_of = factor_of * jnp.repeat(steps, dims[dim] // shards_of).reshape([-1 if axis == dim else 1 for axis in range(len(dims))])
    return factor_of


def centred(key, shape, scale, limit, cuts=(), held_as=jnp.bfloat16):
    factor_of = block_scale(key, shape, cuts, -0.22, 0.18) if cuts else 1.0
    drawn = jax.random.normal(key, shape, jnp.float32) * scale * factor_of
    return jnp.minimum(jnp.maximum(drawn, -limit), limit).astype(held_as)


def setup_inputs(seed: int = 0) -> dict:
    keys = jax.random.split(jax.random.key(seed), 27)
    return {
        "tokens": centred(keys[0], (NBUCK, SEQ_LEN, D), 1.0, 6.0, ((0, 8), (1, 4))),
        "cotangent": centred(keys[1], (NBUCK, SEQ_LEN, D), 1.0, 6.0, ((0, 8), (1, 4))),
        "lengths": draw_lengths(jax.random.fold_in(keys[26], 71), 0),
        "norm1_gain": jnp.clip(1.0 + 0.18 * jax.random.normal(keys[3], (D,), jnp.float32), 0.1, 1.9),
        "norm1_shift": centred(keys[4], (D,), 0.5, 3.0, (), jnp.float32),
        "in_weight": centred(keys[5], (D, 3 * D), D ** -0.5, 0.21875),
        "in_bias": centred(keys[6], (3 * D,), 0.5, 3.0, (), jnp.float32),
        "conv_weight": centred(keys[7], (3, 3 * D), 3 ** -0.5, 3.5, (), jnp.float32),
        "conv_bias": centred(keys[8], (3 * D,), 0.5, 3.0, (), jnp.float32),
        "filter_in": centred(keys[9], (EMB, FILT), EMB ** -0.5, 1.0, (), jnp.float32),
        "filter_in_bias": centred(keys[10], (FILT,), 1.0, 4.0, (), jnp.float32),
        "filter_mid": centred(keys[11], (FILT, FILT), FILT ** -0.5, 0.75, (), jnp.float32),
        "filter_mid_bias": centred(keys[12], (FILT,), 1.0, 4.0, (), jnp.float32),
        "filter_last": centred(keys[13], (FILT, FILT), FILT ** -0.5, 0.75, (), jnp.float32),
        "filter_last_bias": centred(keys[14], (FILT,), 1.0, 4.0, (), jnp.float32),
        "filter_out": centred(keys[15], (FILT, D), (16 * SEQ_LEN) ** -0.5, 0.046875, (), jnp.float32),
        "decay_rate": jnp.clip(jnp.exp(jax.random.uniform(keys[16], (D,), jnp.float32, math.log(0.3), math.log(30.0))), 0.3, 30.0),
        "skip_gain": centred(keys[17], (D,), 1.0, 4.0, (), jnp.float32),
        "out_weight": centred(keys[18], (D, D), D ** -0.5, 0.21875),
        "out_bias": centred(keys[19], (D,), 0.3, 2.0, (), jnp.float32),
        "norm2_gain": jnp.clip(1.0 + 0.18 * jax.random.normal(keys[20], (D,), jnp.float32), 0.1, 1.9),
        "norm2_shift": centred(keys[21], (D,), 0.5, 3.0, (), jnp.float32),
        "up_weight": centred(keys[22], (D, FF), D ** -0.5, 0.21875),
        "up_bias": centred(keys[23], (FF,), 0.5, 3.0, (), jnp.float32),
        "down_weight": centred(keys[24], (FF, D), FF ** -0.5, 0.109375),
        "down_bias": centred(keys[25], (D,), 0.3, 2.0, (), jnp.float32),
    }


@jax.custom_vjp
def low(v):
    return lax.optimization_barrier(v.astype(jnp.bfloat16)).astype(jnp.float32)

@jax.custom_vjp
def low_back(v):
    return v

def low_keep(v):
    return (low(v), None)

def low_pass(kept, grad):
    return (grad,)

def back_keep(v):
    return (v, None)

def back_low(kept, grad):
    return (low(grad),)
low.defvjp(low_keep, low_pass)
low_back.defvjp(back_keep, back_low)
norm_eps = 1e-05
window_floor = 0.05
highest = lax.Precision.HIGHEST

def layer_norm(values, scales, offset):
    center = values - lax.optimization_barrier(jnp.mean(values, axis=-1, keepdims=True))
    spread = lax.optimization_barrier(jnp.mean(center * center, axis=-1, keepdims=True))
    return center * lax.rsqrt(spread + norm_eps) * scales + offset

def features(seq_total, emb_width):
    band_count = (emb_width - 1) // 2
    steps_int = jnp.arange(seq_total, dtype=jnp.int32)
    harmonic = jnp.arange(1, band_count + 1, dtype=jnp.int32)
    phases = steps_int[:, None] * harmonic[None, :] % seq_total
    angles = phases.astype(jnp.float32) * (2.0 * math.pi / seq_total)
    time_ramp = steps_int.astype(jnp.float32) / seq_total
    table = jnp.concatenate([time_ramp[:, None], jnp.cos(angles), jnp.sin(angles)], axis=1)
    return (table, time_ramp)

def filter_taps(seq_total, filter_in, filter_in_bias, filter_mid, filter_mid_bias, filter_last, filter_last_bias, filter_out, decay_rate):
    table, time_ramp = features(seq_total, filter_in.shape[0])
    hidden = jnp.sin(jnp.dot(table, filter_in, precision=highest) + filter_in_bias)
    hidden = jnp.sin(jnp.dot(hidden, filter_mid, precision=highest) + filter_mid_bias)
    hidden = jnp.sin(jnp.dot(hidden, filter_last, precision=highest) + filter_last_bias)
    shaped = jnp.dot(hidden, filter_out, precision=highest)
    window = jnp.exp(-time_ramp[:, None] * decay_rate[None, :]) + window_floor
    return shaped * window

def project(values, matrix):
    return jnp.einsum('gnd,de->gne', values, matrix, precision=highest)

def forward(params, tokens_f, mask_f):
    norm1_gain, norm1_shift, in_weight, in_bias, conv_weight, conv_bias, filter_in, filter_in_bias, filter_mid, filter_mid_bias, filter_last, filter_last_bias, filter_out, decay_rate, skip_gain, out_weight, out_bias, norm2_gain, norm2_shift, up_weight, up_bias, down_weight, down_bias = params
    seq_total = tokens_f.shape[1]
    width = tokens_f.shape[2]
    normed = low(layer_norm(tokens_f, norm1_gain, norm1_shift))
    mixed_in = low(low_back(project(normed, in_weight) + in_bias))
    padded = jnp.pad(mixed_in, ((0, 0), (2, 0), (0, 0)))
    shorted = conv_weight[0] * padded[:, :-2] + conv_weight[1] * padded[:, 1:-1] + conv_weight[2] * padded[:, 2:] + conv_bias
    gate_out = shorted[:, :, :width]
    gate_in = shorted[:, :, width:2 * width]
    values = shorted[:, :, 2 * width:]
    product = low(values * gate_in * mask_f)
    taps = filter_taps(seq_total, filter_in, filter_in_bias, filter_mid, filter_mid_bias, filter_last, filter_last_bias, filter_out, decay_rate)
    span = 2 * seq_total
    spectrum = jnp.fft.rfft(product, n=span, axis=1) * jnp.fft.rfft(taps, n=span, axis=0)[None]
    convolved = low_back(jnp.fft.irfft(spectrum, n=span, axis=1)[:, :seq_total])
    gated = low((convolved + skip_gain * product) * gate_out)
    mixer = low_back(project(gated, out_weight) + out_bias)
    resid = tokens_f + mask_f * mixer
    normed2 = low(layer_norm(resid, norm2_gain, norm2_shift))
    upward = low_back(project(normed2, up_weight) + up_bias)
    active = low(jax.nn.gelu(upward, approximate=False))
    downward = low_back(project(active, down_weight) + down_bias)
    return resid + mask_f * downward

def reference(tokens, cotangent, lengths, norm1_gain, norm1_shift, in_weight, in_bias, conv_weight, conv_bias, filter_in, filter_in_bias, filter_mid, filter_mid_bias, filter_last, filter_last_bias, filter_out, decay_rate, skip_gain, out_weight, out_bias, norm2_gain, norm2_shift, up_weight, up_bias, down_weight, down_bias):
    weights = (norm1_gain, norm1_shift, in_weight, in_bias, conv_weight, conv_bias, filter_in, filter_in_bias, filter_mid, filter_mid_bias, filter_last, filter_last_bias, filter_out, decay_rate, skip_gain, out_weight, out_bias, norm2_gain, norm2_shift, up_weight, up_bias, down_weight, down_bias)
    params = tuple((tensor.astype(jnp.float32) for tensor in weights))
    bucket_total, seq_total, width = tokens.shape
    group_size = math.gcd(bucket_total, max(1, 4096 // seq_total))
    step_count = bucket_total // group_size
    places = jnp.arange(seq_total, dtype=jnp.int32)
    mask_all = (places[None, :] < lengths[:, None]).astype(jnp.float32)[:, :, None]
    tokens_g = tokens.astype(jnp.float32).reshape(step_count, group_size, seq_total, width)
    cot_g = cotangent.astype(jnp.float32).reshape(step_count, group_size, seq_total, width)
    mask_g = mask_all.reshape(step_count, group_size, seq_total, 1)

    def one_group(totals, inputs):
        tokens_f, cot_f, mask_f = inputs

        def apply_all(param_set, tokens_in):
            return forward(param_set, tokens_in, mask_f)
        result, pullback = jax.vjp(apply_all, params, tokens_f)
        grad_params, grad_in = pullback(cot_f)
        totals = jax.tree.map(jnp.add, totals, grad_params)
        return (totals, (result.astype(jnp.bfloat16), grad_in))
    zero_set = jax.tree.map(jnp.zeros_like, params)
    totals, (results, grads_in) = lax.scan(one_group, zero_set, (tokens_g, cot_g, mask_g))
    block_out = results.reshape(bucket_total, seq_total, width)
    grad_tokens = grads_in.reshape(bucket_total, seq_total, width)
    return (block_out, grad_tokens, totals[0], totals[1], totals[2], totals[3], totals[4], totals[5], totals[6], totals[7], totals[8], totals[9], totals[10], totals[11], totals[12], totals[13], totals[14], totals[15], totals[16], totals[17], totals[18], totals[19], totals[20], totals[21], totals[22])
```

```python
from functools import partial
import math

import jax
import jax.numpy as jnp
import numpy as np
from jax import lax
from jax.experimental import pallas as pl
from jax.experimental.pallas import tpu as pltpu
from jax.sharding import PartitionSpec as P

norm_eps = 1e-05
window_floor = 0.05
highest = lax.Precision.HIGHEST
HALO = 16
bf16 = jnp.bfloat16
f32 = jnp.float32


def dot(a, b, ca=1, cb=0, precision=None):
    return lax.dot_general(
        a, b, (((ca,), (cb,)), ((), ())), precision=precision, preferred_element_type=f32
    )


def xor_permute(array, axis, bit):
    count = lax.axis_size(axis)
    return lax.ppermute(array, axis, [(i, i ^ bit) for i in range(count)])


def exchange_seq(array):
    count = lax.axis_size("seq")
    held = {0: array}
    bit = count // 2
    while bit:
        held.update({k ^ bit: xor_permute(a, "seq", bit) for k, a in list(held.items())})
        bit //= 2
    return [held[k] for k in range(count)]


def block_tables(rows):
    phase = (2 * np.arange(rows)[:, None] + 1) * np.arange(rows)[None, :] % (4 * rows)
    angle = phase * (2.0 * math.pi / (4 * rows))
    table = np.concatenate([np.cos(angle), -np.sin(angle)], axis=0)
    high = table.astype(jnp.bfloat16)
    low = (table - high.astype(np.float64)).astype(jnp.bfloat16)
    return high, low


def features(seq_total, emb_width):
    bands = (emb_width - 1) // 2
    steps = np.arange(seq_total)
    phases = steps[:, None] * np.arange(1, bands + 1)[None, :] % seq_total
    angles = phases * (2.0 * math.pi / seq_total)
    ramp = steps / seq_total
    return np.concatenate([ramp[:, None], np.cos(angles), np.sin(angles)], axis=1).astype(np.float32)


def filter_hidden(table, filter_in, in_bias, filter_mid, mid_bias, filter_last, last_bias):
    hidden = jnp.sin(jnp.dot(table, filter_in, precision=highest) + in_bias)
    hidden = jnp.sin(jnp.dot(hidden, filter_mid, precision=highest) + mid_bias)
    return jnp.sin(jnp.dot(hidden, filter_last, precision=highest) + last_bias)


def normalized(values):
    center = values - jnp.mean(values, axis=-1, keepdims=True)
    scale = lax.rsqrt(jnp.mean(center * center, axis=-1, keepdims=True) + norm_eps)
    return center * scale, scale


def live_rows(meta, bucket, rows):
    place = meta[0] * rows + lax.broadcasted_iota(jnp.int32, (rows, 1), 0)
    return (place < meta[1 + bucket]).astype(f32)


def params(mib, count=1):
    return pltpu.CompilerParams(
        dimension_semantics=("arbitrary",) * count, vmem_limit_bytes=mib * 1024 * 1024
    )


SMEM = pl.BlockSpec(memory_space=pltpu.SMEM)


def whole(shape):
    zeros = (0,) * len(shape)
    return pl.BlockSpec(tuple(shape), lambda *_: zeros)


def cost(flops, read):
    return pl.CostEstimate(flops=flops, bytes_accessed=read, transcendentals=0)


def front_body(buckets, rows, meta, tok, halo, gain, shift, w0, w1, w2, bias, cw, cb,
               normed, mixed, product, gate_out, taps_in):
    ext = rows + HALO

    @pl.when(pl.program_id(0) == 0)
    def _():
        for b in range(buckets):
            hat, _ = normalized(halo[b].astype(f32))
            normed[b * ext : b * ext + HALO] = (hat * gain[...] + shift[...]).astype(bf16)
            hat, _ = normalized(tok[b].astype(f32))
            normed[b * ext + HALO : (b + 1) * ext] = (hat * gain[...] + shift[...]).astype(bf16)

    inner = meta[0] > 0
    for b in range(buckets):
        parts = []
        for t, w in enumerate((w0, w1, w2)):
            m = (dot(normed[b * ext : (b + 1) * ext], w[...]) + bias[t : t + 1]).astype(bf16)
            head = jnp.where(inner, m[:HALO].astype(f32), 0.0)
            mixed[t, b, :HALO] = head.astype(bf16)
            mixed[t, b, HALO:] = m[HALO:]
            taps_in[t, :HALO] = head
            taps_in[t, HALO:] = m[HALO:].astype(f32)
            s = cb[t : t + 1]
            for i in range(3):
                s = s + cw[i, t : t + 1] * taps_in[t, HALO - 2 + i : HALO - 2 + i + rows]
            parts.append(s)
        gate_out[b] = parts[0]
        product[b] = (parts[2] * parts[1] * live_rows(meta, b, rows)).astype(bf16)


def front(meta, tok, halo, gain, shift, in_weight, in_bias, conv_weight, conv_bias):
    buckets, rows, width = tok.shape
    ext = rows + HALO
    tile = 256
    steps = width // tile
    columns = [pl.BlockSpec((width, tile), lambda c, t=t: (0, t * steps + c)) for t in range(3)]
    return pl.pallas_call(
        partial(front_body, buckets, rows),
        grid=(steps,),
        in_specs=[
            SMEM, whole(tok.shape), whole(halo.shape), whole((1, width)), whole((1, width)), *columns,
            pl.BlockSpec((3, tile), lambda c: (0, c)),
            pl.BlockSpec((3, 3, tile), lambda c: (0, 0, c)),
            pl.BlockSpec((3, tile), lambda c: (0, c)),
        ],
        out_specs=[
            whole((buckets * ext, width)),
            pl.BlockSpec((3, buckets, ext, tile), lambda c: (0, 0, 0, c)),
            pl.BlockSpec((buckets, rows, tile), lambda c: (0, 0, c)),
            pl.BlockSpec((buckets, rows, tile), lambda c: (0, 0, c)),
        ],
        out_shape=[
            jax.ShapeDtypeStruct((buckets * ext, width), bf16),
            jax.ShapeDtypeStruct((3, buckets, ext, width), bf16),
            jax.ShapeDtypeStruct((buckets, rows, width), bf16),
            jax.ShapeDtypeStruct((buckets, rows, width), f32),
        ],
        scratch_shapes=[pltpu.VMEM((3, ext, tile), f32)],
        compiler_params=params(48),
        cost_estimate=cost(6 * buckets * ext * width * width, 16 << 20),
        name="front",
    )(meta, tok, halo, gain, shift, in_weight, in_weight, in_weight, in_bias, conv_weight, conv_bias)


def alternating(rows):
    parity = lax.broadcasted_iota(jnp.int32, (rows, 1), 0) % 2
    return (1 - 2 * parity).astype(f32)


def window_of(first, rows, total, decay):
    ramp = (first + lax.broadcasted_iota(jnp.int32, (rows, 1), 0)).astype(f32) * (1.0 / total)
    return ramp, jnp.exp(-ramp * decay)


def filter_body(blocks, rows, hidden, out, decay, high, low, shaped, spectrum):
    sign = alternating(rows)
    last = None
    for m in range(blocks):
        here = slice(m * rows, (m + 1) * rows)
        plain = dot(hidden[here], out[...], precision=highest)
        shaped[here] = plain
        _, fall = window_of(m * rows, rows, blocks * rows, decay[...])
        taps = plain * (fall + window_floor)
        upper = taps.astype(bf16)
        rest = (taps - upper.astype(f32)).astype(bf16)
        full = dot(high[...], upper) + (dot(high[...], rest) + dot(low[...], upper))
        re, im = full[:rows], full[rows:]
        if last is None:
            spectrum[m, :rows] = re
            spectrum[m, rows:] = im
        else:
            spectrum[m, :rows] = re - sign * last[1]
            spectrum[m, rows:] = im + sign * last[0]
        last = (re, im)


def filter_spectra(hidden, filter_out, decay, high, low, blocks):
    total, inner = hidden.shape
    width = filter_out.shape[1]
    rows = total // blocks
    tile = 256
    return pl.pallas_call(
        partial(filter_body, blocks, rows),
        grid=(width // tile,),
        in_specs=[
            whole(hidden.shape),
            pl.BlockSpec((inner, tile), lambda c: (0, c)),
            pl.BlockSpec((1, tile), lambda c: (0, c)),
            whole(high.shape), whole(low.shape),
        ],
        out_specs=[
            pl.BlockSpec((total, tile), lambda c: (0, c)),
            pl.BlockSpec((blocks, 2 * rows, tile), lambda c: (0, 0, c)),
        ],
        out_shape=[
            jax.ShapeDtypeStruct((total, width), f32),
            jax.ShapeDtypeStruct((blocks, 2 * rows, width), f32),
        ],
        compiler_params=params(48),
        cost_estimate=cost(20 * total * width * rows, 10 << 20),
        name="filter_spectra",
    )(hidden, filter_out, decay, high, low)


def conv_body(blocks, rows, meta, *refs):
    products = refs[:blocks]
    spectrum, gate_out, skip, high, back, mixture, gated, total = refs[blocks:]
    own = meta[0]
    for k in range(blocks):
        lag = own - (own ^ k)

        def add(k=k, lag=lag):
            full = dot(high[...], products[k][0])
            re, im = full[:rows], full[rows:]
            tap_re, tap_im = spectrum[lag, :rows], spectrum[lag, rows:]
            out_re = tap_re * re - tap_im * im
            out_im = tap_re * im + tap_im * re
            if k == 0:
                total[:rows] = out_re
                total[rows:] = out_im
            else:
                total[:rows] += out_re
                total[rows:] += out_im

        if k == 0:
            add()
        else:
            pl.when(lag >= 0)(add)
    convolved = dot(back[...], total[...].astype(bf16)) * (1.0 / rows)
    mixed = convolved + skip[...] * products[0][0].astype(f32)
    mixture[0] = mixed
    gated[0] = (mixed * gate_out[0]).astype(bf16)


def conv_forward(meta, products, spectrum, gate_out, skip, high, back):
    buckets, rows, width = gate_out.shape
    blocks = len(products)
    tile = 256
    piece = pl.BlockSpec((1, rows, tile), lambda c, b: (b, 0, c))
    return pl.pallas_call(
        partial(conv_body, blocks, rows),
        grid=(width // tile, buckets),
        in_specs=[SMEM] + [piece] * blocks + [
            pl.BlockSpec((blocks, 2 * rows, tile), lambda c, b: (0, 0, c)),
            piece,
            pl.BlockSpec((1, tile), lambda c, b: (0, c)),
            whole(high.shape), whole(back.shape),
        ],
        out_specs=[piece, piece],
        out_shape=[
            jax.ShapeDtypeStruct((buckets, rows, width), f32),
            jax.ShapeDtypeStruct((buckets, rows, width), bf16),
        ],
        scratch_shapes=[pltpu.VMEM((2 * rows, tile), f32)],
        compiler_params=params(48, 2),
        cost_estimate=cost(4 * (blocks + 1) * rows * rows * width * buckets, 16 << 20),
        name="conv_forward",
    )(meta, *products, spectrum, gate_out, skip, high, back)


def gelu_parts(u):
    cdf = 0.5 + 0.5 * lax.erf(u * (1.0 / math.sqrt(2.0)))
    pdf = jnp.exp(-0.5 * u * u) * (1.0 / math.sqrt(2.0 * math.pi))
    return u * cdf, cdf + u * pdf


def middle_body(buckets, rows, steps, meta, gated, out_w, out_b, tok, cot, gain, shift, up_w, up_b, down_w,
                gate_out, normed2, d_down, resid, active, d_up, g_up_bias, d_resid, d_mixer, d_gated, d_conv,
                g_gain, g_shift, g_out_bias, total):
    step = pl.program_id(0)

    @pl.when(step == 0)
    def _():
        for b in range(buckets):
            here = slice(b * rows, (b + 1) * rows)
            live = live_rows(meta, b, rows)
            mixer = dot(gated[here], out_w[...]) + out_b[...]
            r = tok[here].astype(f32) + live * mixer
            resid[here] = r
            hat, _ = normalized(r)
            normed2[here] = (hat * gain[...] + shift[...]).astype(bf16)
            d_down[here] = (live * cot[here].astype(f32)).astype(bf16)

    bias_sum = None
    for b in range(buckets):
        here = slice(b * rows, (b + 1) * rows)
        u = dot(normed2[here], up_w[...]) + up_b[...]
        d_active = dot(d_down[here], down_w[...], 1, 1)
        act, slope = gelu_parts(u)
        active[here] = act.astype(bf16)
        d_u = (d_active * slope).astype(bf16)
        d_up[here] = d_u
        part = jnp.sum(d_u.astype(f32), axis=0, keepdims=True)
        bias_sum = part if bias_sum is None else bias_sum + part
        back = dot(d_u, up_w[...], 1, 1)

        @pl.when(step == 0)
        def _(back=back, here=here):
            total[here] = back

        @pl.when(step > 0)
        def _(back=back, here=here):
            total[here] += back

    g_up_bias[...] = bias_sum

    @pl.when(step == steps - 1)
    def _():
        sums = [jnp.zeros((1, gain.shape[1]), f32)] * 3
        for b in range(buckets):
            here = slice(b * rows, (b + 1) * rows)
            live = live_rows(meta, b, rows)
            hat, scale = normalized(resid[here])
            d = total[here]
            sums[0] = sums[0] + jnp.sum(d * hat, axis=0, keepdims=True)
            sums[1] = sums[1] + jnp.sum(d, axis=0, keepdims=True)
            e = d * gain[...]
            mean_e = jnp.mean(e, axis=-1, keepdims=True)
            mean_eh = jnp.mean(e * hat, axis=-1, keepdims=True)
            d_r = cot[here].astype(f32) + (e - mean_e - hat * mean_eh) * scale
            d_resid[here] = d_r
            d_m = (live * d_r).astype(bf16)
            d_mixer[here] = d_m
            sums[2] = sums[2] + jnp.sum(d_m.astype(f32), axis=0, keepdims=True)
            d_g = dot(d_m, out_w[...], 1, 1)
            d_gated[here] = d_g
            d_conv[here] = (d_g * gate_out[here]).astype(bf16)
        g_gain[...] = sums[0]
        g_shift[...] = sums[1]
        g_out_bias[...] = sums[2]


def middle(meta, gated, out_w, out_b, tok, cot, gain, shift, up_w, up_b, down_w, gate_out, buckets):
    count, width = tok.shape
    hidden = up_w.shape[1]
    tile = 384
    steps = hidden // tile
    rows = count // buckets
    square = whole((count, width))
    line = whole((1, width))
    shape = jax.ShapeDtypeStruct
    return pl.pallas_call(
        partial(middle_body, buckets, rows, steps),
        grid=(steps,),
        in_specs=[
            SMEM, square, whole(out_w.shape), line, square, square, line, line,
            pl.BlockSpec((width, tile), lambda s: (0, s)),
            pl.BlockSpec((1, tile), lambda s: (0, s)),
            pl.BlockSpec((tile, width), lambda s: (s, 0)),
            square,
        ],
        out_specs=[
            square, square, square,
            pl.BlockSpec((count, tile), lambda s: (0, s)),
            pl.BlockSpec((count, tile), lambda s: (0, s)),
            pl.BlockSpec((1, tile), lambda s: (0, s)),
            square, square, square, square, line, line, line,
        ],
        out_shape=[
            shape((count, width), bf16), shape((count, width), bf16), shape((count, width), f32),
            shape((count, hidden), bf16), shape((count, hidden), bf16), shape((1, hidden), f32),
            shape((count, width), f32), shape((count, width), bf16), shape((count, width), f32),
            shape((count, width), bf16), shape((1, width), f32), shape((1, width), f32), shape((1, width), f32),
        ],
        scratch_shapes=[pltpu.VMEM((count, width), f32)],
        compiler_params=params(56),
        cost_estimate=cost(6 * count * width * hidden, 40 << 20),
        name="middle",
    )(meta, gated, out_w, out_b, tok, cot, gain, shift, up_w, up_b, down_w, gate_out)


def weights_body(buckets, rows, steps, meta, active, d_up, normed2, d_down, down_w, down_b, resid, gated, d_mixer,
                 block_out, g_down, g_up, g_out, g_down_bias, total):
    step = pl.program_id(0)
    part = dot(active[...], down_w[...])

    @pl.when(step == 0)
    def _():
        total[...] = part
        g_out[...] = dot(gated[...], d_mixer[...], 0, 0).astype(bf16)
        g_down_bias[...] = jnp.sum(d_down[...].astype(f32), axis=0, keepdims=True)

    @pl.when(step > 0)
    def _():
        total[...] += part

    g_down[...] = dot(active[...], d_down[...], 0, 0).astype(bf16)
    g_up[0] = dot(normed2[...], d_up[...], 0, 0).astype(bf16)

    @pl.when(step == steps - 1)
    def _():
        for b in range(buckets):
            here = slice(b * rows, (b + 1) * rows)
            live = live_rows(meta, b, rows)
            block_out[here] = (resid[here] + live * (total[here] + down_b[...])).astype(bf16)


def weight_grads(meta, active, d_up, normed2, d_down, down_w, down_b, resid, gated, d_mixer, buckets):
    count, width = normed2.shape
    hidden = down_w.shape[0]
    tile = 384
    steps = hidden // tile
    per = width // tile
    rows = count // buckets
    square = whole((count, width))
    shape = jax.ShapeDtypeStruct
    return pl.pallas_call(
        partial(weights_body, buckets, rows, steps),
        grid=(steps,),
        in_specs=[
            SMEM,
            pl.BlockSpec((count, tile), lambda s: (0, s)),
            pl.BlockSpec((count, tile), lambda s: (0, s)),
            square, square,
            pl.BlockSpec((tile, width), lambda s: (s, 0)),
            whole((1, width)), square, square, square,
        ],
        out_specs=[
            square,
            pl.BlockSpec((tile, width), lambda s: (s, 0)),
            pl.BlockSpec((1, width, tile), lambda s: (s // per, 0, s % per)),
            whole((width, width)),
            whole((1, width)),
        ],
        out_shape=[
            shape((count, width), bf16), shape((hidden, width), bf16),
            shape((hidden // width, width, width), bf16),
            shape((width, width), bf16), shape((1, width), f32),
        ],
        scratch_shapes=[pltpu.VMEM((count, width), f32)],
        compiler_params=params(56),
        cost_estimate=cost(6 * count * width * hidden, 40 << 20),
        name="weight_grads",
    )(meta, active, d_up, normed2, d_down, down_w, down_b, resid, gated, d_mixer)


def conv_back_body(blocks, rows, buckets, meta, *refs):
    grads = refs[:blocks]
    (product, spectrum, skip, high, back, hidden, filter_out, decay, shaped,
     d_product, g_hidden, g_filter_out, g_decay, g_skip, total, lags) = refs[blocks:]
    own = meta[0]
    tile_step, b = pl.program_id(0), pl.program_id(1)

    @pl.when(b == 0)
    def _():
        lags[...] = jnp.zeros_like(lags)
        g_skip[...] = jnp.zeros_like(g_skip)

    full = dot(high[...], product[0])
    prod_re, prod_im = full[:rows], full[rows:]
    for k in range(blocks):
        lag = (own ^ k) - own

        def add(k=k, lag=lag):
            grad = dot(high[...], grads[k][0])
            re, im = grad[:rows], grad[rows:]
            tap_re, tap_im = spectrum[lag, :rows], spectrum[lag, rows:]
            out_re = tap_re * re + tap_im * im
            out_im = tap_re * im - tap_im * re
            if k == 0:
                total[:rows] = out_re
                total[rows:] = out_im
            else:
                total[:rows] += out_re
                total[rows:] += out_im
            lags[lag, :rows] += re * prod_re + im * prod_im
            lags[lag, rows:] += im * prod_re - re * prod_im

        if k == 0:
            add()
        else:
            pl.when(lag >= 0)(add)
    d_own = grads[0][0].astype(f32)
    d_product[0] = dot(back[...], total[...].astype(bf16)) * (1.0 / rows) + skip[...] * d_own
    g_skip[...] += jnp.sum(d_own * product[0].astype(f32), axis=0, keepdims=True)

    @pl.when(b == buckets - 1)
    def _():
        sign = alternating(rows)
        sum_out = jnp.zeros(g_filter_out.shape, f32)
        sum_decay = jnp.zeros(g_decay.shape, f32)
        for m in range(blocks):
            here = slice(m * rows, (m + 1) * rows)
            re, im = lags[m, :rows], lags[m, rows:]
            if m + 1 < blocks:
                re, im = re + sign * lags[m + 1, rows:], im - sign * lags[m + 1, :rows]
            d_taps = (dot(back[:, :rows], re.astype(bf16)) + dot(back[:, rows:], im.astype(bf16))) * (1.0 / rows)
            ramp, fall = window_of(m * rows, rows, blocks * rows, decay[...])
            sum_decay = sum_decay - jnp.sum(d_taps * shaped[here] * ramp * fall, axis=0, keepdims=True)
            d_shaped = (d_taps * (fall + window_floor)).astype(bf16)
            sum_out = sum_out + dot(hidden[here], d_shaped, 0, 0)
            d_hidden = dot(d_shaped, filter_out[...], 1, 1)

            @pl.when(tile_step == 0)
            def _(d_hidden=d_hidden, here=here):
                g_hidden[here] = d_hidden

            @pl.when(tile_step > 0)
            def _(d_hidden=d_hidden, here=here):
                g_hidden[here] += d_hidden

        g_filter_out[...] = sum_out
        g_decay[...] = sum_decay


def conv_backward(meta, grads, product, spectrum, skip, high, back, hidden, filter_out, decay, shaped):
    buckets, rows, width = product.shape
    blocks = len(grads)
    total, inner = hidden.shape
    tile = 256
    piece = pl.BlockSpec((1, rows, tile), lambda c, b: (b, 0, c))
    line = pl.BlockSpec((1, tile), lambda c, b: (0, c))
    shape = jax.ShapeDtypeStruct
    return pl.pallas_call(
        partial(conv_back_body, blocks, rows, buckets),
        grid=(width // tile, buckets),
        in_specs=[SMEM] + [piece] * blocks + [
            piece,
            pl.BlockSpec((blocks, 2 * rows, tile), lambda c, b: (0, 0, c)),
            line, whole(high.shape), whole(back.shape), whole(hidden.shape),
            pl.BlockSpec((inner, tile), lambda c, b: (0, c)),
            line,
            pl.BlockSpec((total, tile), lambda c, b: (0, c)),
        ],
        out_specs=[
            piece, whole((total, inner)),
            pl.BlockSpec((inner, tile), lambda c, b: (0, c)),
            line, line,
        ],
        out_shape=[
            shape((buckets, rows, width), f32), shape((total, inner), f32), shape((inner, width), f32),
            shape((1, width), f32), shape((1, width), f32),
        ],
        scratch_shapes=[pltpu.VMEM((2 * rows, tile), f32), pltpu.VMEM((blocks, 2 * rows, tile), f32)],
        compiler_params=params(48, 2),
        cost_estimate=cost(4 * (2 * blocks + 2) * rows * rows * width * buckets, 20 << 20),
        name="conv_backward",
    )(meta, *grads, product, spectrum, skip, high, back, hidden, filter_out, decay, shaped)


def tail_body(buckets, rows, steps, meta, mixed, d_product, mixture, d_gated, normed, w0, w1, w2, cw, cb,
              tok, halo, gain, d_resid, g_tokens, d_halo, g_in, g_conv, g_conv_bias, g_bias, g_gain, g_shift,
              taps_in, d_pad, g_mixed, total):
    ext = rows + HALO
    step = pl.program_id(0)
    inner = meta[0] > 0
    tile = cb.shape[1]
    sums = [[jnp.zeros((1, tile), f32)] * 5 for _ in range(3)]
    for b in range(buckets):
        live = live_rows(meta, b, rows)
        short = []
        for t in range(3):
            taps_in[t] = mixed[t, b].astype(f32)
            s = cb[t : t + 1]
            if t:
                for i in range(3):
                    s = s + cw[i, t : t + 1] * taps_in[t, HALO - 2 + i : HALO - 2 + i + rows]
            short.append(s)
        d_prod = d_product[b] * live
        d_shorts = (d_gated[b] * mixture[b], d_prod * short[2], d_prod * short[1])
        for t in range(3):
            d_short = d_shorts[t]
            d_pad[t, :HALO] = jnp.zeros((HALO, tile), f32)
            d_pad[t, HALO : HALO + rows] = d_short
            d_pad[t, HALO + rows :] = jnp.zeros((8, tile), f32)
            for i in range(3):
                sums[t][i] = sums[t][i] + jnp.sum(
                    d_short * taps_in[t, HALO - 2 + i : HALO - 2 + i + rows], axis=0, keepdims=True)
            sums[t][3] = sums[t][3] + jnp.sum(d_short, axis=0, keepdims=True)
            g = (cw[2, t : t + 1] * d_pad[t, :ext] + cw[1, t : t + 1] * d_pad[t, 1 : ext + 1]
                 + cw[0, t : t + 1] * d_pad[t, 2 : ext + 2])
            head = jnp.where(inner, g[:HALO], 0.0).astype(bf16)
            body = g[HALO:].astype(bf16)
            g_mixed[t, b * ext : b * ext + HALO] = head
            g_mixed[t, b * ext + HALO : (b + 1) * ext] = body
            sums[t][4] = sums[t][4] + (jnp.sum(head.astype(f32), axis=0, keepdims=True)
                                       + jnp.sum(body.astype(f32), axis=0, keepdims=True))
    for t, w in enumerate((w0, w1, w2)):
        for i in range(3):
            g_conv[i, t : t + 1] = sums[t][i]
        g_conv_bias[t : t + 1] = sums[t][3]
        g_bias[t : t + 1] = sums[t][4]
        g_in[t] = dot(normed[...], g_mixed[t], 0, 0).astype(bf16)
    back = dot(g_mixed[0], w0[...], 1, 1) + dot(g_mixed[1], w1[...], 1, 1) + dot(g_mixed[2], w2[...], 1, 1)

    @pl.when(step == 0)
    def _():
        total[...] = back

    @pl.when(step > 0)
    def _():
        total[...] += back

    @pl.when(step == steps - 1)
    def _():
        add = [jnp.zeros((1, gain.shape[1]), f32)] * 2
        for b in range(buckets):
            for first, size, source in ((0, HALO, halo), (HALO, rows, tok)):
                d = total[b * ext + first : b * ext + first + size]
                hat, scale = normalized(source[b].astype(f32))
                add[0] = add[0] + jnp.sum(d * hat, axis=0, keepdims=True)
                add[1] = add[1] + jnp.sum(d, axis=0, keepdims=True)
                e = d * gain[...]
                mean_e = jnp.mean(e, axis=-1, keepdims=True)
                mean_eh = jnp.mean(e * hat, axis=-1, keepdims=True)
                d_v = (e - mean_e - hat * mean_eh) * scale
                if first:
                    g_tokens[b] = d_resid[b] + d_v
                else:
                    d_halo[b] = d_v
        g_gain[...] = add[0]
        g_shift[...] = add[1]


def tail(meta, mixed, d_product, mixture, d_gated, normed, in_weight, conv_weight, conv_bias, tok, halo, gain, d_resid):
    buckets, rows, width = tok.shape
    ext = rows + HALO
    tile = 256
    steps = width // tile
    columns = [pl.BlockSpec((width, tile), lambda c, t=t: (0, t * steps + c)) for t in range(3)]
    piece = pl.BlockSpec((buckets, rows, tile), lambda c: (0, 0, c))
    three = pl.BlockSpec((3, tile), lambda c: (0, c))
    nine = pl.BlockSpec((3, 3, tile), lambda c: (0, 0, c))
    shape = jax.ShapeDtypeStruct
    return pl.pallas_call(
        partial(tail_body, buckets, rows, steps),
        grid=(steps,),
        in_specs=[
            SMEM,
            pl.BlockSpec((3, buckets, ext, tile), lambda c: (0, 0, 0, c)),
            piece, piece, piece, whole(normed.shape), *columns, nine, three,
            whole(tok.shape), whole(halo.shape), whole((1, width)), whole(tok.shape),
        ],
        out_specs=[
            whole(tok.shape), whole(halo.shape),
            pl.BlockSpec((3, width, tile), lambda c: (0, 0, c)),
            nine, three, three, whole((1, width)), whole((1, width)),
        ],
        out_shape=[
            shape(tok.shape, f32), shape(halo.shape, f32), shape((3, width, width), bf16),
            shape((3, 3, width), f32), shape((3, width), f32), shape((3, width), f32),
            shape((1, width), f32), shape((1, width), f32),
        ],
        scratch_shapes=[
            pltpu.VMEM((3, ext, tile), f32),
            pltpu.VMEM((3, ext + 8, tile), f32),
            pltpu.VMEM((3, buckets * ext, tile), bf16),
            pltpu.VMEM((buckets * ext, width), f32),
        ],
        compiler_params=params(56),
        cost_estimate=cost(12 * buckets * ext * width * width, 30 << 20),
        name="tail",
    )(meta, mixed, d_product, mixture, d_gated, normed, in_weight, in_weight, in_weight, conv_weight, conv_bias,
      tok, halo, gain, d_resid)


def index_bits(axis):
    count = lax.axis_size(axis)
    return [(axis, 1 << i) for i in range(count.bit_length() - 1)]


def bit_of(axis, bit):
    return (lax.axis_index(axis) // bit) % 2


def scatter_sum(array, order):
    for axis, bit in order:
        half = array.shape[0] // 2
        mine = bit_of(axis, bit)
        sent = lax.dynamic_slice_in_dim(array, (1 - mine) * half, half, 0)
        kept = lax.dynamic_slice_in_dim(array, mine * half, half, 0)
        array = (kept.astype(f32) + xor_permute(sent, axis, bit).astype(f32)).astype(bf16)
    return array


def gather_rows(array, order):
    for axis, bit in reversed(order):
        other = xor_permute(array, axis, bit)
        high = bit_of(axis, bit) == 1
        array = jnp.concatenate([jnp.where(high, other, array), jnp.where(high, array, other)], axis=0)
    return array


def unscramble(gathered, order):
    names = [b for axis in ("seq", "batch") for b in reversed(index_bits(axis))]
    rows, width = gathered.shape[1:]
    cube = gathered.reshape([2] * len(names) + [rows, width])
    places = [names.index(b) for b in order] + [len(names), len(names) + 1]
    return cube.transpose(places).reshape(gathered.shape[0] * rows, width)


def shards(
    tokens, cotangent, lengths, norm1_gain, norm1_shift, in_weight, in_bias, conv_weight, conv_bias,
    filter_in, filter_in_bias, filter_mid, filter_mid_bias, filter_last, filter_last_bias, filter_out,
    decay_rate, skip_gain, out_weight, out_bias, norm2_gain, norm2_shift, up_weight, up_bias,
    down_weight, down_bias,
):
    buckets, rows, width = tokens.shape
    hidden_width = up_weight.shape[1]
    blocks = lax.axis_size("seq")
    devices = blocks * lax.axis_size("batch")
    count = buckets * rows
    meta = jnp.concatenate([lax.axis_index("seq")[None].astype(jnp.int32), lengths.astype(jnp.int32)])
    high_np, low_np = block_tables(rows)
    high, low = jnp.asarray(high_np), jnp.asarray(low_np)
    back = jnp.asarray(np.ascontiguousarray(high_np.T))
    line = lambda a: a.reshape(1, -1)

    halo = lax.ppermute(tokens[:, rows - HALO :], "seq", [(i, i + 1) for i in range(blocks - 1)])
    conv_w = conv_weight.reshape(3, 3, width)
    conv_b = conv_bias.reshape(3, width)
    normed, mixed, product, gate_out = front(
        meta, tokens, halo, line(norm1_gain), line(norm1_shift), in_weight, in_bias.reshape(3, width), conv_w, conv_b)
    products = exchange_seq(product)
    table = jnp.asarray(features(rows * blocks, filter_in.shape[0]))
    hidden, hidden_pull = jax.vjp(
        partial(filter_hidden, table), filter_in, filter_in_bias, filter_mid, filter_mid_bias,
        filter_last, filter_last_bias)
    shaped, spectrum = filter_spectra(hidden, filter_out, line(decay_rate), high, low, blocks)
    mixture, gated = conv_forward(meta, products, spectrum, gate_out, line(skip_gain), high, back)

    flat = lambda a: a.reshape(count, width)
    (normed2, d_down, resid, active, d_up, g_up_bias, d_resid, d_mixer, d_gated, d_conv,
     g_norm2_gain, g_norm2_shift, g_out_bias) = middle(
        meta, flat(gated), out_weight, line(out_bias), flat(tokens), flat(cotangent), line(norm2_gain),
        line(norm2_shift), up_weight, line(up_bias), down_weight, flat(gate_out), buckets)
    cube = lambda a: a.reshape(buckets, rows, width)
    grads = exchange_seq(cube(d_conv))
    block_out, g_down, g_up, g_out, g_down_bias = weight_grads(
        meta, active, d_up, normed2, d_down, down_weight, line(down_bias), resid, flat(gated), d_mixer, buckets)

    seq_bits, batch_bits = index_bits("seq"), index_bits("batch")
    order_a = [seq_bits[0], batch_bits[0], *seq_bits[1:], *batch_bits[1:]]
    order_b = [seq_bits[0], *batch_bits[1:], batch_bits[0], *seq_bits[1:]]
    down_part = scatter_sum(g_down, order_a)
    up_part = scatter_sum(g_up.reshape(hidden_width, width), order_b)

    d_product, g_hidden, g_filter_out, g_decay, g_skip = conv_backward(
        meta, grads, product, spectrum, line(skip_gain), high, back, hidden.astype(bf16), filter_out.astype(bf16),
        line(decay_rate), shaped)
    g_tokens, d_halo, g_in, g_conv, g_conv_bias, g_in_bias, g_norm1_gain, g_norm1_shift = tail(
        meta, mixed, d_product, mixture, cube(d_gated), normed, in_weight, conv_w, conv_b, tokens, halo,
        line(norm1_gain), cube(d_resid))
    arriving = lax.ppermute(d_halo[:, HALO - 2 :], "seq", [(i + 1, i) for i in range(blocks - 1)])
    g_tokens = g_tokens.at[:, rows - 2 :].add(arriving)
    (g_filter_in, g_filter_in_bias, g_filter_mid, g_filter_mid_bias, g_filter_last,
     g_filter_last_bias) = hidden_pull(g_hidden)

    gathered = lax.all_gather(jnp.stack([down_part, up_part]), ("seq", "batch"), axis=0)
    grad_down_weight = unscramble(gathered[:, 0], order_a).astype(f32)
    grad_up = unscramble(gathered[:, 1], order_b).reshape(hidden_width // width, width, width)
    grad_up_weight = grad_up.transpose(1, 0, 2).reshape(width, hidden_width).astype(f32)

    small = [
        g_norm1_gain, g_norm1_shift, g_in_bias, g_conv, g_conv_bias, g_filter_in, g_filter_in_bias,
        g_filter_mid, g_filter_mid_bias, g_filter_last, g_filter_last_bias, g_filter_out, g_decay, g_skip,
        g_out_bias, g_norm2_gain, g_norm2_shift, g_up_bias, g_down_bias,
    ]
    packed = jnp.concatenate([a.reshape(-1) for a in small]).astype(bf16)
    unit = width * 8 * devices
    padded = -(-packed.shape[0] // unit) * unit
    packed = jnp.pad(packed, (0, padded - packed.shape[0])).reshape(-1, width)
    last = jnp.concatenate([g_in.reshape(3 * width, width), g_out, packed], axis=0)
    last = gather_rows(scatter_sum(last, order_a), order_a).astype(f32)
    grad_in_weight = last[: 3 * width].reshape(3, width, width).transpose(1, 0, 2).reshape(width, 3 * width)
    grad_out_weight = last[3 * width : 4 * width]
    flat_small = last[4 * width :].reshape(-1)
    shapes = [
        (width,), (width,), (3 * width,), (3, 3 * width), (3 * width,), filter_in.shape, filter_in_bias.shape,
        filter_mid.shape, filter_mid_bias.shape, filter_last.shape, filter_last_bias.shape, filter_out.shape,
        (width,), (width,), (width,), (width,), (width,), (hidden_width,), (width,),
    ]
    outs, at = [], 0
    for s in shapes:
        size = math.prod(s)
        outs.append(flat_small[at : at + size].reshape(s))
        at += size
    (n1g, n1s, inb, cw, cb, fi, fib, fm, fmb, fl, flb, fo, dr, sg, ob, n2g, n2s, ub, db) = outs
    return (
        cube(block_out), g_tokens, n1g, n1s, grad_in_weight, inb, cw, cb, fi, fib, fm, fmb, fl, flb, fo, dr, sg,
        grad_out_weight, ob, n2g, n2s, grad_up_weight, ub, grad_down_weight, db,
    )


def solution(mesh):
    split = P("batch", "seq", None)
    return jax.shard_map(
        shards,
        mesh=mesh,
        in_specs=(split, split, P("batch")) + (P(),) * 23,
        out_specs=(split, split) + (P(),) * 23,
        check_vma=False,
    )
```

```python
from functools import partial
import math

import jax
import jax.numpy as jnp
import numpy as np
from jax import lax
from jax.experimental import pallas as pl
from jax.experimental.pallas import tpu as pltpu
from jax.sharding import PartitionSpec as P

norm_eps = 1e-05
window_floor = 0.05
highest = lax.Precision.HIGHEST
HALO = 16
bf16 = jnp.bfloat16
f32 = jnp.float32


def dot(a, b, ca=1, cb=0, precision=None):
    return lax.dot_general(
        a, b, (((ca,), (cb,)), ((), ())), precision=precision, preferred_element_type=f32
    )


def xor_permute(array, axis, bit):
    count = lax.axis_size(axis)
    return lax.ppermute(array, axis, [(i, i ^ bit) for i in range(count)])


def exchange_far(array):
    held = {0: array}
    bit = lax.axis_size("seq") // 2
    while bit > 1:
        held.update({k ^ bit: xor_permute(a, "seq", bit) for k, a in list(held.items())})
        bit //= 2
    return held


def exchange_near(held):
    held = {**held, **{k ^ 1: xor_permute(a, "seq", 1) for k, a in held.items()}}
    return [held[k] for k in range(len(held))]


def after(held, *others):
    keys = [k for k in held if k]
    flat, others = lax.optimization_barrier(([held[k] for k in keys], others))
    return {**held, **dict(zip(keys, flat))}, *others


def block_tables(rows):
    phase = (2 * np.arange(rows)[:, None] + 1) * np.arange(rows)[None, :] % (4 * rows)
    angle = phase * (2.0 * math.pi / (4 * rows))
    table = np.concatenate([np.cos(angle), -np.sin(angle)], axis=0)
    high = table.astype(jnp.bfloat16)
    low = (table - high.astype(np.float64)).astype(jnp.bfloat16)
    return high, low


def features(seq_total, emb_width):
    bands = (emb_width - 1) // 2
    steps = np.arange(seq_total)
    phases = steps[:, None] * np.arange(1, bands + 1)[None, :] % seq_total
    angles = phases * (2.0 * math.pi / seq_total)
    ramp = steps / seq_total
    return np.concatenate([ramp[:, None], np.cos(angles), np.sin(angles)], axis=1).astype(np.float32)


def filter_layers(table, filter_in, in_bias, filter_mid, mid_bias, filter_last, last_bias):
    sines, cosines, value = [], [], table
    for weight, bias in ((filter_in, in_bias), (filter_mid, mid_bias), (filter_last, last_bias)):
        phase = jnp.dot(value, weight, precision=highest) + bias
        value = jnp.sin(phase)
        sines.append(value)
        cosines.append(jnp.cos(phase))
    return sines, cosines


def normalized(values):
    center = values - jnp.mean(values, axis=-1, keepdims=True)
    scale = lax.rsqrt(jnp.mean(center * center, axis=-1, keepdims=True) + norm_eps)
    return center * scale, scale


def live_rows(meta, bucket, rows):
    place = meta[0] * rows + lax.broadcasted_iota(jnp.int32, (rows, 1), 0)
    return (place < meta[1 + bucket]).astype(f32)


def params(mib, count=1):
    return pltpu.CompilerParams(
        dimension_semantics=("arbitrary",) * count, vmem_limit_bytes=mib * 1024 * 1024
    )


SMEM = pl.BlockSpec(memory_space=pltpu.SMEM)


def whole(shape):
    zeros = (0,) * len(shape)
    return pl.BlockSpec(tuple(shape), lambda *_: zeros)


def cost(flops, read):
    return pl.CostEstimate(flops=flops, bytes_accessed=read, transcendentals=0)


def front_body(buckets, rows, meta, tok, halo, gain, shift, w0, w1, w2, bias, cw, cb,
               normed, mixed, product, gate_out, taps_in):
    ext = rows + HALO

    @pl.when(pl.program_id(0) == 0)
    def _():
        for b in range(buckets):
            hat, _ = normalized(halo[b].astype(f32))
            normed[b * ext : b * ext + HALO] = (hat * gain[...] + shift[...]).astype(bf16)
            hat, _ = normalized(tok[b].astype(f32))
            normed[b * ext + HALO : (b + 1) * ext] = (hat * gain[...] + shift[...]).astype(bf16)

    inner = meta[0] > 0
    for b in range(buckets):
        parts = []
        for t, w in enumerate((w0, w1, w2)):
            m = (dot(normed[b * ext : (b + 1) * ext], w[...]) + bias[t : t + 1]).astype(bf16)
            head = jnp.where(inner, m[:HALO].astype(f32), 0.0)
            mixed[t, b, :HALO] = head.astype(bf16)
            mixed[t, b, HALO:] = m[HALO:]
            taps_in[t, :HALO] = head
            taps_in[t, HALO:] = m[HALO:].astype(f32)
            s = cb[t : t + 1]
            for i in range(3):
                s = s + cw[i, t : t + 1] * taps_in[t, HALO - 2 + i : HALO - 2 + i + rows]
            parts.append(s)
        gate_out[b] = parts[0]
        product[b] = (parts[2] * parts[1] * live_rows(meta, b, rows)).astype(bf16)


def front(meta, tok, halo, gain, shift, in_weight, in_bias, conv_weight, conv_bias):
    buckets, rows, width = tok.shape
    ext = rows + HALO
    tile = 256
    steps = width // tile
    columns = [pl.BlockSpec((width, tile), lambda c, t=t: (0, t * steps + c)) for t in range(3)]
    return pl.pallas_call(
        partial(front_body, buckets, rows),
        grid=(steps,),
        in_specs=[
            SMEM, whole(tok.shape), whole(halo.shape), whole((1, width)), whole((1, width)), *columns,
            pl.BlockSpec((3, tile), lambda c: (0, c)),
            pl.BlockSpec((3, 3, tile), lambda c: (0, 0, c)),
            pl.BlockSpec((3, tile), lambda c: (0, c)),
        ],
        out_specs=[
            whole((buckets * ext, width)),
            pl.BlockSpec((3, buckets, ext, tile), lambda c: (0, 0, 0, c)),
            pl.BlockSpec((buckets, rows, tile), lambda c: (0, 0, c)),
            pl.BlockSpec((buckets, rows, tile), lambda c: (0, 0, c)),
        ],
        out_shape=[
            jax.ShapeDtypeStruct((buckets * ext, width), bf16),
            jax.ShapeDtypeStruct((3, buckets, ext, width), bf16),
            jax.ShapeDtypeStruct((buckets, rows, width), bf16),
            jax.ShapeDtypeStruct((buckets, rows, width), f32),
        ],
        scratch_shapes=[pltpu.VMEM((3, ext, tile), f32)],
        compiler_params=params(48),
        cost_estimate=cost(6 * buckets * ext * width * width, 16 << 20),
        name="front",
    )(meta, tok, halo, gain, shift, in_weight, in_weight, in_weight, in_bias, conv_weight, conv_bias)


def alternating(rows):
    parity = lax.broadcasted_iota(jnp.int32, (rows, 1), 0) % 2
    return (1 - 2 * parity).astype(f32)


def window_of(first, rows, total, decay):
    ramp = (first + lax.broadcasted_iota(jnp.int32, (rows, 1), 0)).astype(f32) * (1.0 / total)
    return ramp, jnp.exp(-ramp * decay)


def filter_body(blocks, rows, hidden, out, decay, high, low, shaped, spectrum):
    sign = alternating(rows)
    last = None
    for m in range(blocks):
        here = slice(m * rows, (m + 1) * rows)
        plain = dot(hidden[here], out[...], precision=highest)
        shaped[here] = plain
        _, fall = window_of(m * rows, rows, blocks * rows, decay[...])
        taps = plain * (fall + window_floor)
        upper = taps.astype(bf16)
        rest = (taps - upper.astype(f32)).astype(bf16)
        full = dot(high[...], upper) + (dot(high[...], rest) + dot(low[...], upper))
        re, im = full[:rows], full[rows:]
        if last is None:
            spectrum[m, :rows] = re
            spectrum[m, rows:] = im
        else:
            spectrum[m, :rows] = re - sign * last[1]
            spectrum[m, rows:] = im + sign * last[0]
        last = (re, im)
    spectrum[blocks] = jnp.zeros(spectrum.shape[1:], f32)


def filter_spectra(hidden, filter_out, decay, high, low, blocks):
    total, inner = hidden.shape
    width = filter_out.shape[1]
    rows = total // blocks
    tile = 256
    return pl.pallas_call(
        partial(filter_body, blocks, rows),
        grid=(width // tile,),
        in_specs=[
            whole(hidden.shape),
            pl.BlockSpec((inner, tile), lambda c: (0, c)),
            pl.BlockSpec((1, tile), lambda c: (0, c)),
            whole(high.shape), whole(low.shape),
        ],
        out_specs=[
            pl.BlockSpec((total, tile), lambda c: (0, c)),
            pl.BlockSpec((blocks + 1, 2 * rows, tile), lambda c: (0, 0, c)),
        ],
        out_shape=[
            jax.ShapeDtypeStruct((total, width), f32),
            jax.ShapeDtypeStruct((blocks + 1, 2 * rows, width), f32),
        ],
        compiler_params=params(48),
        cost_estimate=cost(20 * total * width * rows, 10 << 20),
        name="filter_spectra",
    )(hidden, filter_out, decay, high, low)


def conv_body(blocks, rows, tile, meta, *refs):
    products = refs[:blocks]
    spectrum, gate_out, skip, high, back, mixture, gated = refs[blocks:]
    own = meta[0]
    for c in range(products[0].shape[2] // tile):
        at = slice(c * tile, (c + 1) * tile)
        sum_re = sum_im = None
        for k in range(blocks):
            lag = own - (own ^ k)
            lag = jnp.where(lag < 0, blocks, lag)
            full = dot(high[...], products[k][0, :, at])
            re, im = full[:rows], full[rows:]
            tap_re, tap_im = spectrum[lag, :rows, at], spectrum[lag, rows:, at]
            out_re = tap_re * re - tap_im * im
            out_im = tap_re * im + tap_im * re
            sum_re = out_re if sum_re is None else sum_re + out_re
            sum_im = out_im if sum_im is None else sum_im + out_im
        convolved = dot(back[:, :rows], sum_re.astype(bf16)) + dot(back[:, rows:], sum_im.astype(bf16))
        mixed = convolved * (1.0 / rows) + skip[:, at] * products[0][0, :, at].astype(f32)
        mixture[0, :, at] = mixed
        gated[0, :, at] = (mixed * gate_out[0, :, at]).astype(bf16)


def conv_forward(meta, products, spectrum, gate_out, skip, high, back):
    buckets, rows, width = gate_out.shape
    blocks = len(products)
    piece = pl.BlockSpec((1, rows, width), lambda b: (b, 0, 0))
    return pl.pallas_call(
        partial(conv_body, blocks, rows, 256),
        grid=(buckets,),
        in_specs=[SMEM] + [piece] * blocks + [
            whole(spectrum.shape), piece, whole(skip.shape), whole(high.shape), whole(back.shape),
        ],
        out_specs=[piece, piece],
        out_shape=[
            jax.ShapeDtypeStruct((buckets, rows, width), f32),
            jax.ShapeDtypeStruct((buckets, rows, width), bf16),
        ],
        compiler_params=params(56),
        cost_estimate=cost(4 * (blocks + 1) * rows * rows * width * buckets, 16 << 20),
        name="conv_forward",
    )(meta, *products, spectrum, gate_out, skip, high, back)


def gelu_parts(u):
    cdf = 0.5 + 0.5 * lax.erf(u * (1.0 / math.sqrt(2.0)))
    pdf = jnp.exp(-0.5 * u * u) * (1.0 / math.sqrt(2.0 * math.pi))
    return u * cdf, cdf + u * pdf


def middle_body(buckets, rows, steps, meta, gated, out_w, out_b, tok, cot, gain, shift, up_w, up_b, down_w,
                gate_out, normed2, d_down, resid, active, d_up, g_up_bias, d_resid, d_mixer, d_gated, d_conv,
                g_gain, g_shift, g_out_bias, total):
    step = pl.program_id(0)

    @pl.when(step == 0)
    def _():
        for b in range(buckets):
            here = slice(b * rows, (b + 1) * rows)
            live = live_rows(meta, b, rows)
            mixer = dot(gated[here], out_w[...]) + out_b[...]
            r = tok[here].astype(f32) + live * mixer
            resid[here] = r
            hat, _ = normalized(r)
            normed2[here] = (hat * gain[...] + shift[...]).astype(bf16)
            d_down[here] = (live * cot[here].astype(f32)).astype(bf16)

    bias_sum = None
    for b in range(buckets):
        here = slice(b * rows, (b + 1) * rows)
        u = dot(normed2[here], up_w[...]) + up_b[...]
        d_active = dot(d_down[here], down_w[...], 1, 1)
        act, slope = gelu_parts(u)
        active[here] = act.astype(bf16)
        d_u = (d_active * slope).astype(bf16)
        d_up[here] = d_u
        part = jnp.sum(d_u.astype(f32), axis=0, keepdims=True)
        bias_sum = part if bias_sum is None else bias_sum + part
        back = dot(d_u, up_w[...], 1, 1)

        @pl.when(step == 0)
        def _(back=back, here=here):
            total[here] = back

        @pl.when(step > 0)
        def _(back=back, here=here):
            total[here] += back

    g_up_bias[...] = bias_sum

    @pl.when(step == steps - 1)
    def _():
        sums = [jnp.zeros((1, gain.shape[1]), f32)] * 3
        for b in range(buckets):
            here = slice(b * rows, (b + 1) * rows)
            live = live_rows(meta, b, rows)
            hat, scale = normalized(resid[here])
            d = total[here]
            sums[0] = sums[0] + jnp.sum(d * hat, axis=0, keepdims=True)
            sums[1] = sums[1] + jnp.sum(d, axis=0, keepdims=True)
            e = d * gain[...]
            mean_e = jnp.mean(e, axis=-1, keepdims=True)
            mean_eh = jnp.mean(e * hat, axis=-1, keepdims=True)
            d_r = cot[here].astype(f32) + (e - mean_e - hat * mean_eh) * scale
            d_resid[here] = d_r
            d_m = (live * d_r).astype(bf16)
            d_mixer[here] = d_m
            sums[2] = sums[2] + jnp.sum(d_m.astype(f32), axis=0, keepdims=True)
            d_g = dot(d_m, out_w[...], 1, 1)
            d_gated[here] = d_g
            d_conv[here] = (d_g * gate_out[here]).astype(bf16)
        g_gain[...] = sums[0]
        g_shift[...] = sums[1]
        g_out_bias[...] = sums[2]


def middle(meta, gated, out_w, out_b, tok, cot, gain, shift, up_w, up_b, down_w, gate_out, buckets):
    count, width = tok.shape
    hidden = up_w.shape[1]
    tile = 384
    steps = hidden // tile
    rows = count // buckets
    square = whole((count, width))
    line = whole((1, width))
    shape = jax.ShapeDtypeStruct
    return pl.pallas_call(
        partial(middle_body, buckets, rows, steps),
        grid=(steps,),
        in_specs=[
            SMEM, square, whole(out_w.shape), line, square, square, line, line,
            pl.BlockSpec((width, tile), lambda s: (0, s)),
            pl.BlockSpec((1, tile), lambda s: (0, s)),
            pl.BlockSpec((tile, width), lambda s: (s, 0)),
            square,
        ],
        out_specs=[
            square, square, square,
            pl.BlockSpec((count, tile), lambda s: (0, s)),
            pl.BlockSpec((count, tile), lambda s: (0, s)),
            pl.BlockSpec((1, tile), lambda s: (0, s)),
            square, square, square, square, line, line, line,
        ],
        out_shape=[
            shape((count, width), bf16), shape((count, width), bf16), shape((count, width), f32),
            shape((count, hidden), bf16), shape((count, hidden), bf16), shape((1, hidden), f32),
            shape((count, width), f32), shape((count, width), bf16), shape((count, width), f32),
            shape((count, width), bf16), shape((1, width), f32), shape((1, width), f32), shape((1, width), f32),
        ],
        scratch_shapes=[pltpu.VMEM((count, width), f32)],
        compiler_params=params(56),
        cost_estimate=cost(6 * count * width * hidden, 40 << 20),
        name="middle",
    )(meta, gated, out_w, out_b, tok, cot, gain, shift, up_w, up_b, down_w, gate_out)


def own_half(core, width, mine):
    half = width // 2
    return pl.ds(pl.multiple_of((core if mine else 1 - core) * half, half), half)


def weights_body(buckets, rows, steps, meta, active, d_up, normed2, d_down, down_w, down_b, resid, gated, d_mixer,
                 block_out, g_bias, *refs):
    *stacks, total = refs
    kept, sent = stacks[:3], stacks[3:]
    step = pl.program_id(0)
    core = lax.rem(meta[0], 2)
    width = normed2.shape[1]
    mine, theirs = own_half(core, width, True), own_half(core, width, False)

    @pl.when(step < steps)
    def _():
        part = dot(active[...], down_w[...])
        total[...] = jnp.where(step == 0, part, total[...] + part)
        down = [dot(active[:, at], d_down[...], 0, 0).astype(bf16) for at in (mine, theirs)]
        up = [dot(normed2[:, at], d_up[...], 0, 0).astype(bf16) for at in (mine, theirs)]
        for first, stop, source, stack in ((0, 3, down, 0), (3, 4, down, 1), (0, 2, up, 1), (2, 4, up, 2)):

            @pl.when((step >= first) & (step < stop))
            def _(source=source, stack=stack):
                kept[stack][0] = source[0]
                sent[stack][0] = source[1]

    @pl.when(step == 0)
    def _():
        g_bias[...] = jnp.sum(d_down[...].astype(f32), axis=0, keepdims=True)

    @pl.when(step == steps)
    def _():
        kept[2][0] = dot(gated[:, mine], d_mixer[...], 0, 0).astype(bf16)
        sent[2][0] = dot(gated[:, theirs], d_mixer[...], 0, 0).astype(bf16)
        for b in range(buckets):
            here = slice(b * rows, (b + 1) * rows)
            live = live_rows(meta, b, rows)
            block_out[here] = (resid[here] + live * (total[here] + down_b[...])).astype(bf16)


def weight_grads(meta, active, d_up, normed2, d_down, down_w, down_b, resid, gated, d_mixer, buckets):
    count, width = normed2.shape
    hidden = down_w.shape[0]
    steps = hidden // width
    assert steps == 4
    square = whole((count, width))
    shape = jax.ShapeDtypeStruct
    last = steps - 1
    columns = pl.BlockSpec((count, width), lambda s: (0, jnp.minimum(s, last)))
    half = (1, width // 2, width)
    stacks = [
        pl.BlockSpec(half, lambda s: (jnp.minimum(s, 2), 0, 0)),
        pl.BlockSpec(half, lambda s: (jnp.where(s > 2, 0, jnp.minimum(s + 1, 2)), 0, 0)),
        pl.BlockSpec(half, lambda s: (jnp.maximum(s - 2, 0), 0, 0)),
    ]
    return pl.pallas_call(
        partial(weights_body, buckets, count // buckets, steps),
        grid=(steps + 1,),
        in_specs=[
            SMEM, columns, columns, square, square,
            pl.BlockSpec((width, width), lambda s: (jnp.minimum(s, last), 0)),
            whole((1, width)), square, square, square,
        ],
        out_specs=[square, whole((1, width)), *stacks, *stacks],
        out_shape=[shape((count, width), bf16), shape((1, width), f32)] + [shape((3, width // 2, width), bf16)] * 6,
        scratch_shapes=[pltpu.VMEM((count, width), f32)],
        compiler_params=params(56),
        cost_estimate=cost(6 * count * width * hidden, 40 << 20),
        name="weight_grads",
    )(meta, active, d_up, normed2, d_down, down_w, down_b, resid, gated, d_mixer)


def conv_back_body(blocks, rows, buckets, tile, meta, *refs):
    grads = refs[:blocks]
    product, spectrum, skip, high, back, d_product, g_skip, g_lags, lags = refs[blocks:]
    own = meta[0]
    b = pl.program_id(0)
    width = product.shape[2]

    @pl.when(b == 0)
    def _():
        lags[...] = jnp.zeros_like(lags)
        g_skip[...] = jnp.zeros_like(g_skip)

    for c in range(width // tile):
        at = slice(c * tile, (c + 1) * tile)
        full = dot(high[...], product[0, :, at])
        prod_re, prod_im = full[:rows], full[rows:]
        sum_re = sum_im = None
        for k in range(blocks):
            lag = (own ^ k) - own
            lag = jnp.where(lag < 0, blocks, lag)
            grad = dot(high[...], grads[k][0, :, at])
            re, im = grad[:rows], grad[rows:]
            tap_re, tap_im = spectrum[lag, :rows, at], spectrum[lag, rows:, at]
            out_re = tap_re * re + tap_im * im
            out_im = tap_re * im - tap_im * re
            sum_re = out_re if sum_re is None else sum_re + out_re
            sum_im = out_im if sum_im is None else sum_im + out_im
            lags[lag, :rows, at] += re * prod_re + im * prod_im
            lags[lag, rows:, at] += im * prod_re - re * prod_im
        d_own = grads[0][0, :, at].astype(f32)
        full = dot(back[:, :rows], sum_re.astype(bf16)) + dot(back[:, rows:], sum_im.astype(bf16))
        d_product[0, :, at] = full * (1.0 / rows) + skip[:, at] * d_own
        g_skip[:, at] += jnp.sum(d_own * product[0, :, at].astype(f32), axis=0, keepdims=True)

    @pl.when(b == buckets - 1)
    def _():
        g_lags[...] = lags[:blocks].astype(bf16)


def conv_backward(meta, grads, product, spectrum, skip, high, back):
    buckets, rows, width = product.shape
    blocks = len(grads)
    piece = pl.BlockSpec((1, rows, width), lambda b: (b, 0, 0))
    line = whole((1, width))
    shape = jax.ShapeDtypeStruct
    return pl.pallas_call(
        partial(conv_back_body, blocks, rows, buckets, 256),
        grid=(buckets,),
        in_specs=[SMEM] + [piece] * blocks + [
            piece, whole(spectrum.shape), line, whole(high.shape), whole(back.shape),
        ],
        out_specs=[piece, line, whole((blocks, 2 * rows, width))],
        out_shape=[shape((buckets, rows, width), f32), shape((1, width), f32), shape((blocks, 2 * rows, width), bf16)],
        scratch_shapes=[pltpu.VMEM((blocks + 1, 2 * rows, width), f32)],
        compiler_params=params(60),
        cost_estimate=cost(4 * (2 * blocks + 2) * rows * rows * width * buckets, 20 << 20),
        name="conv_backward",
    )(meta, *grads, product, spectrum, skip, high, back)


def filter_back_body(blocks, rows, tile, lags, back, hidden, filter_out, decay, shaped, table, sin_a, sin_b, cos_a, cos_b,
                     cos_c, filter_mid, filter_last, g_filter_out, g_decay, g_in, g_in_bias, g_mid, g_mid_bias,
                     g_last, g_last_bias, g_hidden):
    sign = alternating(rows)
    for c in range(decay.shape[1] // tile):
        at = slice(c * tile, (c + 1) * tile)
        sum_out = sum_decay = None
        for m in range(blocks):
            here = slice(m * rows, (m + 1) * rows)
            re, im = lags[m, :rows, at].astype(f32), lags[m, rows:, at].astype(f32)
            if m + 1 < blocks:
                re = re + sign * lags[m + 1, rows:, at].astype(f32)
                im = im - sign * lags[m + 1, :rows, at].astype(f32)
            d_taps = dot(back[:, :rows], re.astype(bf16)) + dot(back[:, rows:], im.astype(bf16))
            d_taps = d_taps * (1.0 / rows)
            ramp, fall = window_of(m * rows, rows, blocks * rows, decay[:, at])
            g_d = -jnp.sum(d_taps * shaped[here, at] * ramp * fall, axis=0, keepdims=True)
            d_shaped = (d_taps * (fall + window_floor)).astype(bf16)
            g_o = dot(hidden[here], d_shaped, 0, 0)
            sum_out = g_o if sum_out is None else sum_out + g_o
            sum_decay = g_d if sum_decay is None else sum_decay + g_d
            d_hidden = dot(d_shaped, filter_out[:, at], 1, 1)
            g_hidden[here] = d_hidden if c == 0 else g_hidden[here] + d_hidden
        g_filter_out[:, at] = sum_out
        g_decay[:, at] = sum_decay
    d_c = g_hidden[...] * cos_c[...]
    g_last_bias[...] = jnp.sum(d_c, axis=0, keepdims=True)
    d_c = d_c.astype(bf16)
    g_last[...] = dot(sin_b[...].astype(bf16), d_c, 0, 0)
    d_b = dot(d_c, filter_last[...].astype(bf16), 1, 1) * cos_b[...]
    g_mid_bias[...] = jnp.sum(d_b, axis=0, keepdims=True)
    d_b = d_b.astype(bf16)
    g_mid[...] = dot(sin_a[...].astype(bf16), d_b, 0, 0)
    d_a = dot(d_b, filter_mid[...].astype(bf16), 1, 1) * cos_a[...]
    g_in[...] = dot(table[...].astype(bf16), d_a.astype(bf16), 0, 0)
    g_in_bias[...] = jnp.sum(d_a, axis=0, keepdims=True)


def filter_backward(lags, back, hidden, filter_out, decay, shaped, table, sines, cosines, filter_mid, filter_last):
    blocks, double_rows, width = lags.shape
    total, inner = hidden.shape
    shape = jax.ShapeDtypeStruct
    outs = [shape((inner, width), f32), shape((1, width), f32),
            shape((table.shape[1], inner), f32), shape((1, inner), f32), shape((inner, inner), f32),
            shape((1, inner), f32), shape((inner, inner), f32), shape((1, inner), f32)]
    arrays = [lags, back, hidden, filter_out, decay, shaped, table, sines[0], sines[1], *cosines, filter_mid, filter_last]
    return pl.pallas_call(
        partial(filter_back_body, blocks, double_rows // 2, 256),
        grid=(1,),
        in_specs=[whole(a.shape) for a in arrays],
        out_specs=[whole(a.shape) for a in outs],
        out_shape=outs,
        scratch_shapes=[pltpu.VMEM((total, inner), f32)],
        compiler_params=params(56),
        cost_estimate=cost(10 * total * width * double_rows, 10 << 20),
        name="filter_backward",
    )(*arrays)


PACK = 128


def pack_layout(width, shapes):
    out, narrow, row = [], 0, [64, 64]
    for shape in shapes:
        r, c = (1, shape[0]) if len(shape) == 1 else shape
        if c < width:
            out.append([((slice(0, r), slice(0, c)), 0, 0, narrow)])
            narrow += 128
        elif r > 32:
            out.append([((slice(0, r), slice(0, c)), 1, 0, 0)])
        else:
            entry = []
            for j in range(c // width):
                block = 0 if row[0] + r <= PACK else 1
                entry.append(((slice(0, r), slice(j * width, (j + 1) * width)), block, row[block], 0))
                row[block] += r
            out.append(entry)
    assert max(row) <= PACK and narrow <= width
    return out


def short_back_body(buckets, rows, first, meta, *refs):
    count = 1 if first else 2
    if first:
        mixture, d_gated, *refs = refs
    else:
        d_product, *refs = refs
    mixed, refs = refs[:count], refs[count:]
    normed, cw, cb, kept, sent, g_mixed, g_conv, g_conv_bias, g_bias, taps_in, d_pad = refs
    ext = rows + HALO
    inner = meta[0] > 0
    core = lax.rem(meta[0], 2)
    tile = cb.shape[1]
    width = normed.shape[1]
    sums = [[jnp.zeros((1, tile), f32)] * 5 for _ in range(count)]
    for b in range(buckets):
        short = []
        for t in range(count):
            k = t if first else t + 1
            taps_in[t] = mixed[t][0, b].astype(f32)
            s = cb[k : k + 1]
            if not first:
                for i in range(3):
                    s = s + cw[i, k : k + 1] * taps_in[t, HALO - 2 + i : HALO - 2 + i + rows]
            short.append(s)
        if first:
            d_shorts = (d_gated[b] * mixture[b],)
        else:
            d_prod = d_product[b] * live_rows(meta, b, rows)
            d_shorts = (d_prod * short[1], d_prod * short[0])
        for t in range(count):
            k = t if first else t + 1
            d_short = d_shorts[t]
            d_pad[t, :HALO] = jnp.zeros((HALO, tile), f32)
            d_pad[t, HALO : HALO + rows] = d_short
            d_pad[t, HALO + rows :] = jnp.zeros((8, tile), f32)
            for i in range(3):
                sums[t][i] = sums[t][i] + jnp.sum(
                    d_short * taps_in[t, HALO - 2 + i : HALO - 2 + i + rows], axis=0, keepdims=True)
            sums[t][3] = sums[t][3] + jnp.sum(d_short, axis=0, keepdims=True)
            g = (cw[2, k : k + 1] * d_pad[t, :ext] + cw[1, k : k + 1] * d_pad[t, 1 : ext + 1]
                 + cw[0, k : k + 1] * d_pad[t, 2 : ext + 2])
            head = jnp.where(inner, g[:HALO], 0.0).astype(bf16)
            body = g[HALO:].astype(bf16)
            g_mixed[t, b * ext : b * ext + HALO] = head
            g_mixed[t, b * ext + HALO : (b + 1) * ext] = body
            sums[t][4] = sums[t][4] + (jnp.sum(head.astype(f32), axis=0, keepdims=True)
                                       + jnp.sum(body.astype(f32), axis=0, keepdims=True))
    for t in range(count):
        for i in range(3):
            g_conv[i, t : t + 1] = sums[t][i]
        g_conv_bias[t : t + 1] = sums[t][3]
        g_bias[t : t + 1] = sums[t][4]
        kept[t] = dot(normed[:, own_half(core, width, True)], g_mixed[t], 0, 0).astype(bf16)
        sent[t] = dot(normed[:, own_half(core, width, False)], g_mixed[t], 0, 0).astype(bf16)


def short_backward(meta, sources, mixed, normed, conv_weight, conv_bias):
    _, buckets, ext, width = mixed.shape
    rows = ext - HALO
    tile = 256
    first = len(sources) == 2
    count = 1 if first else 2
    piece = pl.BlockSpec((buckets, rows, tile), lambda c: (0, 0, c))
    columns = [pl.BlockSpec((1, buckets, ext, tile), lambda c, t=t: (t, 0, 0, c)) for t in ([0] if first else [1, 2])]
    three = pl.BlockSpec((3, tile), lambda c: (0, c))
    nine = pl.BlockSpec((3, 3, tile), lambda c: (0, 0, c))
    line = pl.BlockSpec((count, tile), lambda c: (0, c))
    half = pl.BlockSpec((count, width // 2, tile), lambda c: (0, 0, c))
    shape = jax.ShapeDtypeStruct
    return pl.pallas_call(
        partial(short_back_body, buckets, rows, first),
        grid=(width // tile,),
        in_specs=[SMEM, *[piece] * len(sources), *columns, whole(normed.shape), nine, three],
        out_specs=[
            half, half, pl.BlockSpec((count, buckets * ext, tile), lambda c: (0, 0, c)),
            pl.BlockSpec((3, count, tile), lambda c: (0, 0, c)), line, line,
        ],
        out_shape=[
            shape((count, width // 2, width), bf16), shape((count, width // 2, width), bf16),
            shape((count, buckets * ext, width), bf16), shape((3, count, width), f32), shape((count, width), f32),
            shape((count, width), f32),
        ],
        scratch_shapes=[pltpu.VMEM((count, ext, tile), f32), pltpu.VMEM((count, ext + 8, tile), f32)],
        compiler_params=params(56),
        cost_estimate=cost(2 * count * buckets * ext * width * width, 10 << 20),
        name="short_backward",
    )(meta, *sources, *[mixed] * count, normed, conv_weight, conv_bias)


def token_body(buckets, rows, layout, others, meta, g_first, g_mixed, weight, tok, halo, gain, d_resid, *refs):
    parts, refs = refs[:6], refs[6:]
    smalls, (g_tokens, d_halo, kept, sent, total, pack) = refs[:others], refs[others:]
    ext = rows + HALO
    step = pl.program_id(0)
    core = lax.rem(meta[0], 2)

    @pl.when(step == 0)
    def _():
        total[...] = dot(g_first[0], weight[...], 1, 1)

    @pl.when(step > 0)
    def _():
        total[...] += dot(g_mixed[0], weight[...], 1, 1)

    @pl.when(step == 2)
    def _():
        add = [jnp.zeros((1, gain.shape[1]), f32)] * 2
        for b in range(buckets):
            for first, size, source in ((0, HALO, halo), (HALO, rows, tok)):
                d = total[b * ext + first : b * ext + first + size]
                hat, scale = normalized(source[b].astype(f32))
                add[0] = add[0] + jnp.sum(d * hat, axis=0, keepdims=True)
                add[1] = add[1] + jnp.sum(d, axis=0, keepdims=True)
                e = d * gain[...]
                mean_e = jnp.mean(e, axis=-1, keepdims=True)
                mean_eh = jnp.mean(e * hat, axis=-1, keepdims=True)
                d_v = (e - mean_e - hat * mean_eh) * scale
                if first:
                    g_tokens[b] = d_resid[b] + d_v
                else:
                    d_halo[b] = d_v
        pack[...] = jnp.zeros_like(pack)
        for source, entry in zip(add, layout[:2]):
            (_, block, row, _), = entry
            pack[block, row : row + 1] = source
        conv, conv_bias, bias = parts[0::3], parts[1::3], parts[2::3]
        for j in range(3):
            p, q = (0, 0) if j == 0 else (1, j - 1)
            _, block, row, _ = layout[2][j]
            pack[block, row : row + 1] = bias[p][q : q + 1]
            _, block, row, _ = layout[4][j]
            pack[block, row : row + 1] = conv_bias[p][q : q + 1]
            _, block, row, _ = layout[3][j]
            for i in range(3):
                pack[block, row + i : row + i + 1] = conv[p][i, q : q + 1]
        for source, entry in zip(smalls, layout[5:]):
            for (r, c), block, row, lane in entry:
                pack[block, row : row + r.stop - r.start, lane : lane + c.stop - c.start] = source[r, c]
        kept[...] = jnp.where(core == 0, pack[...], 0.0).astype(bf16)
        sent[...] = jnp.where(core == 0, 0.0, pack[...]).astype(bf16)


def token_grads(meta, g_first, g_mixed, in_weight, tok, halo, gain, d_resid, parts, smalls, layout):
    buckets, rows, width = tok.shape
    ext = rows + HALO
    shape = jax.ShapeDtypeStruct
    packed = (2, PACK, width)
    arrays = [tok, halo, gain, d_resid, *parts, *smalls]
    return pl.pallas_call(
        partial(token_body, buckets, rows, layout, len(smalls)),
        grid=(3,),
        in_specs=[
            SMEM, whole(g_first.shape), pl.BlockSpec((1, buckets * ext, width), lambda t: (jnp.maximum(t - 1, 0), 0, 0)),
            pl.BlockSpec((width, width), lambda t: (0, t)), *[whole(a.shape) for a in arrays],
        ],
        out_specs=[whole(tok.shape), whole(halo.shape), whole(packed), whole(packed)],
        out_shape=[shape(tok.shape, f32), shape(halo.shape, f32), shape(packed, bf16), shape(packed, bf16)],
        scratch_shapes=[pltpu.VMEM((buckets * ext, width), f32), pltpu.VMEM(packed, f32)],
        compiler_params=params(56),
        cost_estimate=cost(6 * buckets * ext * width * width, 30 << 20),
        name="token_grads",
    )(meta, g_first, g_mixed, in_weight, *arrays)


def index_bits(axis):
    count = lax.axis_size(axis)
    return [(axis, 1 << i) for i in range(count.bit_length() - 1)]


def bit_of(axis, bit):
    return (lax.axis_index(axis) // bit) % 2


def halve_parts(kept, come, axis, bit):
    half = kept.shape[1] // 2
    mine = bit_of(axis, bit)

    def part(which):
        a = lax.dynamic_slice_in_dim(kept, which * half, half, 1)
        b = lax.dynamic_slice_in_dim(come, which * half, half, 1)
        return (a.astype(f32) + b.astype(f32)).astype(bf16)

    return part(mine), part(1 - mine)


def halve(kept, come, axis, bit):
    kept, sent = halve_parts(kept, come, axis, bit)
    return kept, xor_permute(sent, axis, bit)


def add_up(kept, come):
    return (kept.astype(f32) + come.astype(f32)).astype(bf16)


def double(array, axis, bit):
    return side_of(array, xor_permute(array, axis, bit), axis, bit)


def side_of(array, other, axis, bit):
    high = bit_of(axis, bit) == 1
    return jnp.concatenate([jnp.where(high, other, array), jnp.where(high, array, other)], axis=1)


def device_of(order):
    names = [b for axis in ("seq", "batch") for b in reversed(index_bits(axis))]
    last = len(names) - 1

    def device(shard):
        return sum((shard // (1 << (last - i))) % 2 * (1 << (last - names.index(b))) for i, b in enumerate(order))

    return device


def restored(gathered, order):
    names = [b for axis in ("seq", "batch") for b in reversed(index_bits(axis))]
    _, n, rows, width = gathered.shape
    cube = gathered.reshape([2] * len(names) + [n, rows, width])
    k = len(names)
    cube = cube.transpose([k] + [names.index(b) for b in order] + [k + 1, k + 2])
    return cube.reshape(n, -1, width).astype(f32)


def spread_body(a, b, c, down, up, out):
    width = out.shape[1]
    for i in range(3):
        down[i] = a[0, i].astype(f32)
    down[3] = b[0, 0].astype(f32)
    for i, source in enumerate((b[0, 1], b[0, 2], c[0, 0], c[0, 1])):
        up[:, i * width : (i + 1) * width] = source.astype(f32)
    out[...] = c[0, 2].astype(f32)


def spread(gathered, orders):
    devices, stacked, rows, width = gathered.shape
    if rows % 8:
        a, b, c = (restored(gathered[:, 3 * i : 3 * i + 3], order) for i, order in enumerate(orders))
        return (jnp.concatenate([a, b[:1]]).reshape(4 * width, width),
                jnp.concatenate([b[1], b[2], c[0], c[1]], axis=1), c[2])
    places = [device_of(order) for order in orders]
    down, up, out = pl.pallas_call(
        spread_body,
        grid=(devices,),
        in_specs=[pl.BlockSpec((1, 3, rows, width), lambda s, i=i, p=p: (p(s), i, 0, 0)) for i, p in enumerate(places)],
        out_specs=[
            pl.BlockSpec((4, rows, width), lambda s: (0, s, 0)),
            pl.BlockSpec((rows, 4 * width), lambda s: (s, 0)),
            pl.BlockSpec((rows, width), lambda s: (s, 0)),
        ],
        out_shape=[
            jax.ShapeDtypeStruct((4, width, width), f32),
            jax.ShapeDtypeStruct((width, 4 * width), f32),
            jax.ShapeDtypeStruct((width, width), f32),
        ],
        compiler_params=params(32),
        cost_estimate=cost(0, 6 * devices * stacked * rows * width),
        name="spread",
    )(gathered, gathered, gathered)
    return down.reshape(4 * width, width), up, out


def in_final_body(half_shards, meta, first, kept, other, target):
    width = first.shape[3]
    own = (pl.program_id(0) // half_shards) == lax.rem(meta[0], 2)
    target[:, :width] = first[0, 0].astype(f32)
    for i in range(2):
        value = jnp.where(own, kept[i].astype(f32), other[i].astype(f32))
        target[:, (i + 1) * width : (i + 2) * width] = value


def in_final(meta, gathered, order, kept, other):
    devices, stacked, rows, width = gathered.shape
    if rows % 8:
        half = width // 2
        high = lax.axis_index("seq") % 2 == 1
        a, b = kept[:, :half].astype(f32), other[:, :half].astype(f32)
        rest = jnp.concatenate([jnp.where(high, b, a), jnp.where(high, a, b)], axis=1)
        return jnp.concatenate([restored(gathered[:, -1:], order)[0], rest[0], rest[1]], axis=1)
    place = device_of(order)
    half = devices // 2
    piece = pl.BlockSpec((2, rows, width), lambda s: (0, s % half, 0))
    return pl.pallas_call(
        partial(in_final_body, half),
        grid=(devices,),
        in_specs=[SMEM, pl.BlockSpec((1, 1, rows, width), lambda s: (place(s), stacked - 1, 0, 0)), piece, piece],
        out_specs=pl.BlockSpec((rows, 3 * width), lambda s: (s, 0)),
        out_shape=jax.ShapeDtypeStruct((width, 3 * width), f32),
        compiler_params=params(32),
        cost_estimate=cost(0, 18 * width * width),
        name="in_final",
    )(meta, gathered, kept, other)


def unpack_body(layout, meta, kept, other, *refs):
    *targets, rows = refs
    core = lax.rem(meta[0], 2)

    @pl.when(core == 0)
    def _():
        rows[...] = kept[...].astype(f32)

    @pl.when(core == 1)
    def _():
        rows[...] = other[...].astype(f32)

    for target, entry in zip(targets, layout):
        for (r, c), block, row, lane in entry:
            size, across = r.stop - r.start, c.stop - c.start
            part = rows[block, row : row + size, lane : lane + across]
            if len(target.shape) == 1:
                target[c] = part[0]
            else:
                target[r, c] = part


def unpack(meta, kept, other, layout, shapes):
    count, rows, width = kept.shape
    at = (rows - PACK) // PACK
    piece = pl.BlockSpec((count, PACK, width), lambda i: (0, at, 0))
    return pl.pallas_call(
        partial(unpack_body, layout),
        grid=(1,),
        in_specs=[SMEM, piece, piece],
        out_specs=[whole(s) for s in shapes],
        out_shape=[jax.ShapeDtypeStruct(s, f32) for s in shapes],
        scratch_shapes=[pltpu.VMEM((count, PACK, width), f32)],
        compiler_params=params(32),
        cost_estimate=cost(0, 2 << 20),
        name="unpack",
    )(meta, kept, other)


def shards(
    tokens, cotangent, lengths, norm1_gain, norm1_shift, in_weight, in_bias, conv_weight, conv_bias,
    filter_in, filter_in_bias, filter_mid, filter_mid_bias, filter_last, filter_last_bias, filter_out,
    decay_rate, skip_gain, out_weight, out_bias, norm2_gain, norm2_shift, up_weight, up_bias,
    down_weight, down_bias,
):
    buckets, rows, width = tokens.shape
    hidden_width = up_weight.shape[1]
    blocks = lax.axis_size("seq")
    devices = blocks * lax.axis_size("batch")
    count = buckets * rows
    meta = jnp.concatenate([lax.axis_index("seq")[None].astype(jnp.int32), lengths.astype(jnp.int32)])
    high_np, low_np = block_tables(rows)
    high, low = jnp.asarray(high_np), jnp.asarray(low_np)
    back = jnp.asarray(np.ascontiguousarray(high_np.T))
    line = lambda a: a.reshape(1, -1)

    halo = lax.ppermute(tokens[:, rows - HALO :], "seq", [(i, i + 1) for i in range(blocks - 1)])
    conv_w = conv_weight.reshape(3, 3, width)
    conv_b = conv_bias.reshape(3, width)
    normed, mixed, product, gate_out = front(
        meta, tokens, halo, line(norm1_gain), line(norm1_shift), in_weight, in_bias.reshape(3, width), conv_w, conv_b)
    far = exchange_far(product)
    table = jnp.asarray(features(rows * blocks, filter_in.shape[0]))
    sines, cosines = filter_layers(
        table, filter_in, filter_in_bias, filter_mid, filter_mid_bias, filter_last, filter_last_bias)
    hidden = sines[2]
    shaped, spectrum = filter_spectra(hidden, filter_out, line(decay_rate), high, low, blocks)
    far, spectrum = after(far, spectrum)
    products = exchange_near(far)
    mixture, gated = conv_forward(meta, products, spectrum, gate_out, line(skip_gain), high, back)

    flat = lambda a: a.reshape(count, width)
    (normed2, d_down, resid, active, d_up, g_up_bias, d_resid, d_mixer, d_gated, d_conv,
     g_norm2_gain, g_norm2_shift, g_out_bias) = middle(
        meta, flat(gated), out_weight, line(out_bias), flat(tokens), flat(cotangent), line(norm2_gain),
        line(norm2_shift), up_weight, line(up_bias), down_weight, flat(gate_out), buckets)
    cube = lambda a: a.reshape(buckets, rows, width)
    seq_bits, batch_bits = index_bits("seq"), index_bits("batch")
    core, far_seq, near_batch, far_batch = seq_bits[0], seq_bits[1:], batch_bits[:1], batch_bits[1:]
    orders = [near_batch + far_seq + far_batch, far_seq + far_batch + near_batch, far_batch + near_batch + far_seq]
    barrier = lax.optimization_barrier

    def wave(kept, come, at):
        pairs = [halve(k, c, *order[at]) for k, c, order in zip(kept, come, orders)]
        return [k for k, _ in pairs], [c for _, c in pairs]

    far = exchange_far(cube(d_conv))
    block_out, g_down_bias, *stacks = weight_grads(
        meta, active, d_up, normed2, d_down, down_weight, line(down_bias), resid, flat(gated), d_mixer, buckets)
    first_kept, first_sent, g_first, *first_parts = short_backward(
        meta, (mixture, cube(d_gated)), mixed, normed, conv_w, conv_b)
    kept, sent = stacks[:3], stacks[3:]
    far, sent, first_sent = after(far, sent, first_sent)
    grads = exchange_near(far)
    come = [xor_permute(a, *core) for a in sent]
    first_come = xor_permute(first_sent, *core)
    come, first_come, grads = barrier((come, first_come, grads))
    first_kept, first_sent = halve_parts(first_kept, first_come, *orders[0][0])
    kept_0, sent_0 = halve_parts(kept[0], come[0], *orders[0][0])
    pairs = [halve(k, c, *order[0]) for k, c, order in zip(kept[1:], come[1:], orders[1:])]
    come_0 = xor_permute(jnp.concatenate([sent_0, first_sent], axis=0), *orders[0][0])
    kept = [jnp.concatenate([kept_0, first_kept], axis=0)] + [k for k, _ in pairs]
    come = [come_0] + [c for _, c in pairs]
    d_product, g_skip, lags = conv_backward(meta, grads, product, spectrum, line(skip_gain), high, back)

    come, d_product, lags = barrier((come, d_product, lags))
    kept, come = wave(kept, come, 1)
    in_kept, in_sent, g_mixed, *other_parts = short_backward(meta, (d_product,), mixed, normed, conv_w, conv_b)
    (g_filter_out, g_decay, g_filter_in, g_filter_in_bias, g_filter_mid, g_filter_mid_bias,
     g_filter_last, g_filter_last_bias) = filter_backward(
        lags, back, hidden.astype(bf16), filter_out.astype(bf16), line(decay_rate), shaped, table, sines, cosines,
        filter_mid, filter_last)

    come, in_sent, g_filter_out, g_mixed = barrier((come, in_sent, g_filter_out, g_mixed))
    in_come = xor_permute(in_sent, *core)
    kept, come = wave(kept, come, 2)
    shapes = [
        (width,), (width,), (3 * width,), (3, 3 * width), (3 * width,), filter_in.shape, filter_in_bias.shape,
        filter_mid.shape, filter_mid_bias.shape, filter_last.shape, filter_last_bias.shape, filter_out.shape,
        (width,), (width,), (width,), (width,), (width,), (hidden_width,), (width,),
    ]
    layout = pack_layout(width, shapes)
    smalls = [
        g_filter_in, g_filter_in_bias, g_filter_mid, g_filter_mid_bias, g_filter_last, g_filter_last_bias,
        g_filter_out, g_decay, g_skip, g_out_bias, g_norm2_gain, g_norm2_shift, g_up_bias, g_down_bias,
    ]
    g_tokens, d_halo, pack_kept, pack_sent = token_grads(
        meta, g_first, g_mixed, in_weight, tokens, halo, line(norm1_gain), cube(d_resid), first_parts + other_parts,
        smalls, layout)

    come, in_come, pack_sent = barrier((come, in_come, pack_sent))
    pack_come = xor_permute(pack_sent, *core)
    for at in range(3, len(orders[0])):
        kept, come = wave(kept, come, at)
    arriving = lax.ppermute(d_halo[:, HALO - 2 :], "seq", [(i + 1, i) for i in range(blocks - 1)])
    g_tokens = g_tokens.at[:, rows - 2 :].add(arriving)
    come, pack_come = barrier((come, pack_come))
    in_kept = jnp.concatenate([in_kept, pack_kept], axis=1)
    in_come = jnp.concatenate([in_come, pack_come], axis=1)
    order = orders[0]
    in_kept, in_come = halve(in_kept, in_come, *order[0])
    both = jnp.concatenate([add_up(kept[0], come[0])[:3], add_up(kept[1], come[1]), add_up(kept[2], come[2]),
                            add_up(kept[0], come[0])[3:]], axis=0)
    gathered = lax.all_gather(both, ("seq", "batch"), axis=0)

    for step in order[1:]:
        in_kept, in_come = halve(in_kept, in_come, *step)
    in_kept = add_up(in_kept, in_come)
    for step in reversed(order[1:]):
        in_kept = double(in_kept, *step)
    in_come = xor_permute(in_kept, *order[0])
    grad_down_weight, grad_up_weight, grad_out_weight = spread(gathered, [[core, *o] for o in orders])
    in_come, grad_down_weight, g_tokens = barrier((in_come, grad_down_weight, g_tokens))
    in_kept = side_of(in_kept, in_come, *order[0])
    in_come = xor_permute(in_kept, *core)
    grad_in_weight = in_final(meta, gathered, [core, *orders[0]], in_kept, in_come)
    (n1g, n1s, inb, cw, cb, fi, fib, fm, fmb, fl, flb, fo, dr, sg, ob, n2g, n2s, ub, db) = unpack(
        meta, in_kept, in_come, layout, shapes)
    return (
        cube(block_out), g_tokens, n1g, n1s, grad_in_weight, inb, cw, cb, fi, fib, fm, fmb, fl, flb, fo, dr, sg,
        grad_out_weight, ob, n2g, n2s, grad_up_weight, ub, grad_down_weight, db,
    )


def solution(mesh):
    split = P("batch", "seq", None)
    return jax.shard_map(
        shards,
        mesh=mesh,
        in_specs=(split, split, P("batch")) + (P(),) * 23,
        out_specs=(split, split) + (P(),) * 23,
        check_vma=False,
    )
```

```python
from functools import partial
import math

import jax
import jax.numpy as jnp
import numpy as np
from jax import lax
from jax.experimental import pallas as pl
from jax.experimental.pallas import tpu as pltpu
from jax.sharding import PartitionSpec as P

norm_eps = 1e-05
window_floor = 0.05
highest = lax.Precision.HIGHEST
HALO = 16
CONV_TILE = 256
LAST_STEPS = 1
bf16 = jnp.bfloat16
f32 = jnp.float32


def dot(a, b, ca=1, cb=0, precision=None):
    return lax.dot_general(
        a, b, (((ca,), (cb,)), ((), ())), precision=precision, preferred_element_type=f32
    )


def xor_permute(array, axis, bit):
    count = lax.axis_size(axis)
    return lax.ppermute(array, axis, [(i, i ^ bit) for i in range(count)])


def exchange_far(array):
    held = {0: array}
    bit = lax.axis_size("seq") // 2
    while bit > 1:
        held.update({k ^ bit: xor_permute(a, "seq", bit) for k, a in list(held.items())})
        bit //= 2
    return held


def exchange_near(held):
    held = {**held, **{k ^ 1: xor_permute(a, "seq", 1) for k, a in held.items()}}
    return [held[k] for k in range(len(held))]


def after(held, *others):
    keys = [k for k in held if k]
    flat, others = lax.optimization_barrier(([held[k] for k in keys], others))
    return {**held, **dict(zip(keys, flat))}, *others


def block_tables(rows):
    phase = (2 * np.arange(rows)[:, None] + 1) * np.arange(rows)[None, :] % (4 * rows)
    angle = phase * (2.0 * math.pi / (4 * rows))
    table = np.concatenate([np.cos(angle), -np.sin(angle)], axis=0)
    high = table.astype(jnp.bfloat16)
    low = (table - high.astype(np.float64)).astype(jnp.bfloat16)
    return high, low


def features(seq_total, emb_width):
    bands = (emb_width - 1) // 2
    steps = np.arange(seq_total)
    phases = steps[:, None] * np.arange(1, bands + 1)[None, :] % seq_total
    angles = phases * (2.0 * math.pi / seq_total)
    ramp = steps / seq_total
    return np.concatenate([ramp[:, None], np.cos(angles), np.sin(angles)], axis=1).astype(np.float32)


def filter_layers(table, filter_in, in_bias, filter_mid, mid_bias, filter_last, last_bias):
    sines, cosines, value = [], [], table
    for weight, bias in ((filter_in, in_bias), (filter_mid, mid_bias), (filter_last, last_bias)):
        phase = jnp.dot(value, weight, precision=highest) + bias
        value = jnp.sin(phase)
        sines.append(value)
        cosines.append(jnp.cos(phase))
    return sines, cosines


def normalized(values):
    center = values - jnp.mean(values, axis=-1, keepdims=True)
    scale = lax.rsqrt(jnp.mean(center * center, axis=-1, keepdims=True) + norm_eps)
    return center * scale, scale


def live_rows(meta, bucket, rows):
    place = meta[0] * rows + lax.broadcasted_iota(jnp.int32, (rows, 1), 0)
    return (place < meta[1 + bucket]).astype(f32)


LIMIT = 0


def params(mib, count=1):
    return pltpu.CompilerParams(
        dimension_semantics=("arbitrary",) * count, vmem_limit_bytes=max(mib, LIMIT) * 1024 * 1024
    )


SMEM = pl.BlockSpec(memory_space=pltpu.SMEM)


def whole(shape):
    zeros = (0,) * len(shape)
    return pl.BlockSpec(tuple(shape), lambda *_: zeros)


def cost(flops, read):
    return pl.CostEstimate(flops=flops, bytes_accessed=read, transcendentals=0)


def front_body(buckets, rows, meta, tok, halo, gain, shift, w0, w1, w2, bias, cw, cb,
               normed, mixed, product, gate_out, taps_in):
    ext = rows + HALO

    @pl.when(pl.program_id(0) == 0)
    def _():
        for b in range(buckets):
            hat, _ = normalized(halo[b].astype(f32))
            normed[b * ext : b * ext + HALO] = (hat * gain[...] + shift[...]).astype(bf16)
            hat, _ = normalized(tok[b].astype(f32))
            normed[b * ext + HALO : (b + 1) * ext] = (hat * gain[...] + shift[...]).astype(bf16)

    inner = meta[0] > 0
    for b in range(buckets):
        parts = []
        for t, w in enumerate((w0, w1, w2)):
            m = (dot(normed[b * ext : (b + 1) * ext], w[...]) + bias[t : t + 1]).astype(bf16)
            head = jnp.where(inner, m[:HALO].astype(f32), 0.0)
            mixed[t, b, :HALO] = head.astype(bf16)
            mixed[t, b, HALO:] = m[HALO:]
            taps_in[t, :HALO] = head
            taps_in[t, HALO:] = m[HALO:].astype(f32)
            s = cb[t : t + 1]
            for i in range(3):
                s = s + cw[i, t : t + 1] * taps_in[t, HALO - 2 + i : HALO - 2 + i + rows]
            parts.append(s)
        gate_out[b] = parts[0]
        product[b] = (parts[2] * parts[1] * live_rows(meta, b, rows)).astype(bf16)


def front(meta, tok, halo, gain, shift, in_weight, in_bias, conv_weight, conv_bias):
    buckets, rows, width = tok.shape
    ext = rows + HALO
    tile = 256
    steps = width // tile
    columns = [pl.BlockSpec((width, tile), lambda c, t=t: (0, t * steps + c)) for t in range(3)]
    return pl.pallas_call(
        partial(front_body, buckets, rows),
        grid=(steps,),
        in_specs=[
            SMEM, whole(tok.shape), whole(halo.shape), whole((1, width)), whole((1, width)), *columns,
            pl.BlockSpec((3, tile), lambda c: (0, c)),
            pl.BlockSpec((3, 3, tile), lambda c: (0, 0, c)),
            pl.BlockSpec((3, tile), lambda c: (0, c)),
        ],
        out_specs=[
            whole((buckets * ext, width)),
            pl.BlockSpec((3, buckets, ext, tile), lambda c: (0, 0, 0, c)),
            pl.BlockSpec((buckets, rows, tile), lambda c: (0, 0, c)),
            pl.BlockSpec((buckets, rows, tile), lambda c: (0, 0, c)),
        ],
        out_shape=[
            jax.ShapeDtypeStruct((buckets * ext, width), bf16),
            jax.ShapeDtypeStruct((3, buckets, ext, width), bf16),
            jax.ShapeDtypeStruct((buckets, rows, width), bf16),
            jax.ShapeDtypeStruct((buckets, rows, width), f32),
        ],
        scratch_shapes=[pltpu.VMEM((3, ext, tile), f32)],
        compiler_params=params(48),
        cost_estimate=cost(6 * buckets * ext * width * width, 16 << 20),
        name="front",
    )(meta, tok, halo, gain, shift, in_weight, in_weight, in_weight, in_bias, conv_weight, conv_bias)


def alternating(rows):
    parity = lax.broadcasted_iota(jnp.int32, (rows, 1), 0) % 2
    return (1 - 2 * parity).astype(f32)


def window_of(first, rows, total, decay):
    ramp = (first + lax.broadcasted_iota(jnp.int32, (rows, 1), 0)).astype(f32) * (1.0 / total)
    return ramp, jnp.exp(-ramp * decay)


def filter_body(blocks, rows, hidden, out, decay, high, low, shaped, spectrum):
    sign = alternating(rows)
    last = None
    for m in range(blocks):
        here = slice(m * rows, (m + 1) * rows)
        plain = dot(hidden[here], out[...], precision=highest)
        shaped[here] = plain
        _, fall = window_of(m * rows, rows, blocks * rows, decay[...])
        taps = plain * (fall + window_floor)
        upper = taps.astype(bf16)
        rest = (taps - upper.astype(f32)).astype(bf16)
        full = dot(high[...], upper) + (dot(high[...], rest) + dot(low[...], upper))
        re, im = full[:rows], full[rows:]
        if last is None:
            spectrum[m, :rows] = re
            spectrum[m, rows:] = im
        else:
            spectrum[m, :rows] = re - sign * last[1]
            spectrum[m, rows:] = im + sign * last[0]
        last = (re, im)
    spectrum[blocks] = jnp.zeros(spectrum.shape[1:], f32)


def filter_spectra(hidden, filter_out, decay, high, low, blocks):
    total, inner = hidden.shape
    width = filter_out.shape[1]
    rows = total // blocks
    tile = 256
    return pl.pallas_call(
        partial(filter_body, blocks, rows),
        grid=(width // tile,),
        in_specs=[
            whole(hidden.shape),
            pl.BlockSpec((inner, tile), lambda c: (0, c)),
            pl.BlockSpec((1, tile), lambda c: (0, c)),
            whole(high.shape), whole(low.shape),
        ],
        out_specs=[
            pl.BlockSpec((total, tile), lambda c: (0, c)),
            pl.BlockSpec((blocks + 1, 2 * rows, tile), lambda c: (0, 0, c)),
        ],
        out_shape=[
            jax.ShapeDtypeStruct((total, width), f32),
            jax.ShapeDtypeStruct((blocks + 1, 2 * rows, width), f32),
        ],
        compiler_params=params(48),
        cost_estimate=cost(20 * total * width * rows, 10 << 20),
        name="filter_spectra",
    )(hidden, filter_out, decay, high, low)


def conv_body(blocks, rows, meta, *refs):
    products = refs[:blocks]
    spectrum, gate_out, skip, high, back, mixture, gated = refs[blocks:]
    own = meta[0]
    for c in range(products[0].shape[2] // CONV_TILE):
        at = slice(c * CONV_TILE, (c + 1) * CONV_TILE)
        sum_re = sum_im = None
        for k in range(blocks):
            lag = own - (own ^ k)
            lag = jnp.where(lag < 0, blocks, lag)
            full = dot(high[...], products[k][0, :, at])
            re, im = full[:rows], full[rows:]
            tap_re, tap_im = spectrum[lag, :rows, at], spectrum[lag, rows:, at]
            out_re = tap_re * re - tap_im * im
            out_im = tap_re * im + tap_im * re
            sum_re = out_re if sum_re is None else sum_re + out_re
            sum_im = out_im if sum_im is None else sum_im + out_im
        convolved = dot(back[:, :rows], sum_re.astype(bf16)) + dot(back[:, rows:], sum_im.astype(bf16))
        mixed = convolved * (1.0 / rows) + skip[:, at] * products[0][0, :, at].astype(f32)
        mixture[0, :, at] = mixed
        gated[0, :, at] = (mixed * gate_out[0, :, at]).astype(bf16)


def conv_forward(meta, products, spectrum, gate_out, skip, high, back):
    buckets, rows, width = gate_out.shape
    blocks = len(products)
    tile = width
    piece = pl.BlockSpec((1, rows, tile), lambda c, b: (b, 0, c))
    return pl.pallas_call(
        partial(conv_body, blocks, rows),
        grid=(width // tile, buckets),
        in_specs=[SMEM] + [piece] * blocks + [
            pl.BlockSpec((blocks + 1, 2 * rows, tile), lambda c, b: (0, 0, c)), piece,
            pl.BlockSpec((1, tile), lambda c, b: (0, c)), whole(high.shape), whole(back.shape),
        ],
        out_specs=[piece, piece],
        out_shape=[
            jax.ShapeDtypeStruct((buckets, rows, width), f32),
            jax.ShapeDtypeStruct((buckets, rows, width), bf16),
        ],
        compiler_params=params(56, 2),
        cost_estimate=cost(4 * (blocks + 1) * rows * rows * width * buckets, 16 << 20),
        name="conv_forward",
    )(meta, *products, spectrum, gate_out, skip, high, back)


def gelu_parts(u):
    cdf = 0.5 + 0.5 * lax.erf(u * (1.0 / math.sqrt(2.0)))
    pdf = jnp.exp(-0.5 * u * u) * (1.0 / math.sqrt(2.0 * math.pi))
    return u * cdf, cdf + u * pdf


def middle_body(buckets, rows, steps, meta, gated, out_w, out_b, tok, cot, gain, shift, up_w, up_b, down_w,
                gate_out, normed2, d_down, resid, active, d_up, g_up_bias, d_resid, d_mixer, d_gated, d_conv,
                g_gain, g_shift, g_out_bias, total):
    step = pl.program_id(0)

    @pl.when(step == 0)
    def _():
        for b in range(buckets):
            here = slice(b * rows, (b + 1) * rows)
            live = live_rows(meta, b, rows)
            mixer = dot(gated[here], out_w[...]) + out_b[...]
            r = tok[here].astype(f32) + live * mixer
            resid[here] = r
            hat, _ = normalized(r)
            normed2[here] = (hat * gain[...] + shift[...]).astype(bf16)
            d_down[here] = (live * cot[here].astype(f32)).astype(bf16)
            total[here] = jnp.zeros_like(total[here])

    bias_sum = None
    for b in range(buckets):
        here = slice(b * rows, (b + 1) * rows)
        u = dot(normed2[here], up_w[...]) + up_b[...]
        d_active = dot(d_down[here], down_w[...], 1, 1)
        act, slope = gelu_parts(u)
        active[here] = act.astype(bf16)
        d_u = (d_active * slope).astype(bf16)
        d_up[here] = d_u
        part = jnp.sum(d_u.astype(f32), axis=0, keepdims=True)
        bias_sum = part if bias_sum is None else bias_sum + part
        back = dot(d_u, up_w[...], 1, 1)

        total[here] += back

    g_up_bias[...] = bias_sum

    @pl.when(step == steps - 1)
    def _():
        sums = [jnp.zeros((1, gain.shape[1]), f32)] * 3
        for b in range(buckets):
            here = slice(b * rows, (b + 1) * rows)
            live = live_rows(meta, b, rows)
            hat, scale = normalized(resid[here])
            d = total[here]
            sums[0] = sums[0] + jnp.sum(d * hat, axis=0, keepdims=True)
            sums[1] = sums[1] + jnp.sum(d, axis=0, keepdims=True)
            e = d * gain[...]
            mean_e = jnp.mean(e, axis=-1, keepdims=True)
            mean_eh = jnp.mean(e * hat, axis=-1, keepdims=True)
            d_r = cot[here].astype(f32) + (e - mean_e - hat * mean_eh) * scale
            d_resid[here] = d_r
            d_m = (live * d_r).astype(bf16)
            d_mixer[here] = d_m
            sums[2] = sums[2] + jnp.sum(d_m.astype(f32), axis=0, keepdims=True)
            d_g = dot(d_m, out_w[...], 1, 1)
            d_gated[here] = d_g
            d_conv[here] = (d_g * gate_out[here]).astype(bf16)
        g_gain[...] = sums[0]
        g_shift[...] = sums[1]
        g_out_bias[...] = sums[2]


def middle(meta, gated, out_w, out_b, tok, cot, gain, shift, up_w, up_b, down_w, gate_out, buckets):
    count, width = tok.shape
    hidden = up_w.shape[1]
    tile = width
    steps = hidden // tile
    rows = count // buckets
    square = whole((count, width))
    line = whole((1, width))
    shape = jax.ShapeDtypeStruct
    return pl.pallas_call(
        partial(middle_body, buckets, rows, steps),
        grid=(steps,),
        in_specs=[
            SMEM, square, whole(out_w.shape), line, square, square, line, line,
            pl.BlockSpec((width, tile), lambda s: (0, s)),
            pl.BlockSpec((1, tile), lambda s: (0, s)),
            pl.BlockSpec((tile, width), lambda s: (s, 0)),
            square,
        ],
        out_specs=[
            square, square, square,
            pl.BlockSpec((count, tile), lambda s: (0, s)),
            pl.BlockSpec((count, tile), lambda s: (0, s)),
            pl.BlockSpec((1, tile), lambda s: (0, s)),
            square, square, square, square, line, line, line,
        ],
        out_shape=[
            shape((count, width), bf16), shape((count, width), bf16), shape((count, width), f32),
            shape((count, hidden), bf16), shape((count, hidden), bf16), shape((1, hidden), f32),
            shape((count, width), f32), shape((count, width), bf16), shape((count, width), f32),
            shape((count, width), bf16), shape((1, width), f32), shape((1, width), f32), shape((1, width), f32),
        ],
        scratch_shapes=[pltpu.VMEM((count, width), f32)],
        compiler_params=params(56),
        cost_estimate=cost(6 * count * width * hidden, 40 << 20),
        name="middle",
    )(meta, gated, out_w, out_b, tok, cot, gain, shift, up_w, up_b, down_w, gate_out)


def own_half(core, width, mine):
    half = width // 2
    return pl.ds(pl.multiple_of((core if mine else 1 - core) * half, half), half)


def weights_body(steps, meta, active, d_up, normed2, d_down, gated, d_mixer, first_kept, first_sent, g_bias, *stacks):
    del first_kept, first_sent
    kept, sent = stacks[:3], stacks[3:]
    step = pl.program_id(0)
    core = lax.rem(meta[0], 2)
    width = normed2.shape[1]
    mine, theirs = own_half(core, width, True), own_half(core, width, False)

    @pl.when(step < steps)
    def _():
        down = [dot(active[:, at], d_down[...], 0, 0).astype(bf16) for at in (mine, theirs)]
        up = [dot(normed2[:, at], d_up[...], 0, 0).astype(bf16) for at in (mine, theirs)]
        for first, stop, source, stack in ((0, 3, down, 0), (3, 4, down, 1), (0, 2, up, 1), (2, 4, up, 2)):

            @pl.when((step >= first) & (step < stop))
            def _(source=source, stack=stack):
                kept[stack][0] = source[0]
                sent[stack][0] = source[1]

    @pl.when(step == steps)
    def _():
        kept[2][0] = dot(gated[:, mine], d_mixer[...], 0, 0).astype(bf16)
        sent[2][0] = dot(gated[:, theirs], d_mixer[...], 0, 0).astype(bf16)
        g_bias[...] = jnp.sum(d_down[...].astype(f32), axis=0, keepdims=True)


def weight_grads(meta, active, d_up, normed2, d_down, gated, d_mixer, first_kept, first_sent):
    count, width = normed2.shape
    hidden = active.shape[1]
    steps = hidden // width
    assert steps == 4
    square = whole((count, width))
    shape = jax.ShapeDtypeStruct
    last = steps - 1
    columns = pl.BlockSpec((count, width), lambda s: (0, jnp.minimum(s, last)))
    half = (1, width // 2, width)
    stacks = [
        pl.BlockSpec(half, lambda s: (jnp.minimum(s, 2), 0, 0)),
        pl.BlockSpec(half, lambda s: (jnp.where(s > 2, 0, jnp.minimum(s + 1, 2)), 0, 0)),
        pl.BlockSpec(half, lambda s: (jnp.maximum(s - 2, 0), 0, 0)),
    ]
    return pl.pallas_call(
        partial(weights_body, steps),
        grid=(steps + 1,),
        in_specs=[SMEM, columns, columns, square, square, square, square] + [pl.BlockSpec(memory_space=pl.ANY)] * 2,
        out_specs=[whole((1, width)), *stacks, *stacks],
        out_shape=[shape((1, width), f32)] + [shape((n, width // 2, width), bf16) for n in (4, 3, 3)] * 2,
        input_output_aliases={7: 1, 8: 4},
        compiler_params=params(56),
        cost_estimate=cost(4 * count * width * hidden, 40 << 20),
        name="weight_grads",
    )(meta, active, d_up, normed2, d_down, gated, d_mixer, first_kept, first_sent)


def output_body(buckets, rows, steps, meta, active, down_w, down_b, resid, block_out, total):
    step = pl.program_id(0)

    @pl.when(step == 0)
    def _():
        total[...] = dot(active[...], down_w[...])

    @pl.when(step > 0)
    def _():
        total[...] += dot(active[...], down_w[...])

    @pl.when(step == steps - 1)
    def _():
        for b in range(buckets):
            here = slice(b * rows, (b + 1) * rows)
            live = live_rows(meta, b, rows)
            block_out[here] = (resid[here] + live * (total[here] + down_b[...])).astype(bf16)


def layer_output(meta, active, down_w, down_b, resid, buckets):
    count, width = resid.shape
    hidden = down_w.shape[0]
    steps = hidden // width
    return pl.pallas_call(
        partial(output_body, buckets, count // buckets, steps),
        grid=(steps,),
        in_specs=[
            SMEM, pl.BlockSpec((count, width), lambda s: (0, s)), pl.BlockSpec((width, width), lambda s: (s, 0)),
            whole((1, width)), whole((count, width)),
        ],
        out_specs=whole((count, width)),
        out_shape=jax.ShapeDtypeStruct((count, width), bf16),
        scratch_shapes=[pltpu.VMEM((count, width), f32)],
        compiler_params=params(48),
        cost_estimate=cost(2 * count * width * hidden, 14 << 20),
        name="layer_output",
    )(meta, active, down_w, down_b, resid)


def conv_back_body(blocks, rows, buckets, meta, *refs):
    grads = refs[:blocks]
    product, spectrum, skip, high, back, d_product, g_skip, g_lags, lags = refs[blocks:]
    own = meta[0]
    b = pl.program_id(1)

    @pl.when(b == 0)
    def _():
        lags[...] = jnp.zeros_like(lags)
        g_skip[...] = jnp.zeros_like(g_skip)

    full = dot(high[...], product[0])
    prod_re, prod_im = full[:rows], full[rows:]
    sum_re = sum_im = None
    for k in range(blocks):
        lag = (own ^ k) - own
        lag = jnp.where(lag < 0, blocks, lag)
        grad = dot(high[...], grads[k][0])
        re, im = grad[:rows], grad[rows:]
        tap_re, tap_im = spectrum[lag, :rows], spectrum[lag, rows:]
        out_re = tap_re * re + tap_im * im
        out_im = tap_re * im - tap_im * re
        sum_re = out_re if sum_re is None else sum_re + out_re
        sum_im = out_im if sum_im is None else sum_im + out_im
        lags[lag, :rows] += re * prod_re + im * prod_im
        lags[lag, rows:] += im * prod_re - re * prod_im
    d_own = grads[0][0].astype(f32)
    full = dot(back[:, :rows], sum_re.astype(bf16)) + dot(back[:, rows:], sum_im.astype(bf16))
    d_product[0] = full * (1.0 / rows) + skip[...] * d_own
    g_skip[...] += jnp.sum(d_own * product[0].astype(f32), axis=0, keepdims=True)

    @pl.when(b == buckets - 1)
    def _():
        g_lags[...] = lags[:blocks].astype(bf16)


def conv_backward(meta, grads, product, spectrum, skip, high, back):
    buckets, rows, width = product.shape
    blocks = len(grads)
    tile = CONV_TILE
    piece = pl.BlockSpec((1, rows, tile), lambda c, b: (b, 0, c))
    line = pl.BlockSpec((1, tile), lambda c, b: (0, c))
    shape = jax.ShapeDtypeStruct
    return pl.pallas_call(
        partial(conv_back_body, blocks, rows, buckets),
        grid=(width // tile, buckets),
        in_specs=[SMEM] + [piece] * blocks + [
            piece, pl.BlockSpec((blocks + 1, 2 * rows, tile), lambda c, b: (0, 0, c)), line, whole(high.shape),
            whole(back.shape),
        ],
        out_specs=[piece, line, pl.BlockSpec((blocks, 2 * rows, tile), lambda c, b: (0, 0, c))],
        out_shape=[shape((buckets, rows, width), f32), shape((1, width), f32), shape((blocks, 2 * rows, width), bf16)],
        scratch_shapes=[pltpu.VMEM((blocks + 1, 2 * rows, tile), f32)],
        compiler_params=params(60, 2),
        cost_estimate=cost(4 * (2 * blocks + 2) * rows * rows * width * buckets, 20 << 20),
        name="conv_backward",
    )(meta, *grads, product, spectrum, skip, high, back)


def filter_back_body(blocks, rows, tile, lags, back, hidden, filter_out, decay, shaped, table, sin_a, sin_b, cos_a, cos_b,
                     cos_c, filter_mid, filter_last, g_filter_out, g_decay, g_in, g_in_bias, g_mid, g_mid_bias,
                     g_last, g_last_bias, g_hidden):
    sign = alternating(rows)
    for c in range(decay.shape[1] // tile):
        at = slice(c * tile, (c + 1) * tile)
        sum_out = sum_decay = None
        for m in range(blocks):
            here = slice(m * rows, (m + 1) * rows)
            re, im = lags[m, :rows, at].astype(f32), lags[m, rows:, at].astype(f32)
            if m + 1 < blocks:
                re = re + sign * lags[m + 1, rows:, at].astype(f32)
                im = im - sign * lags[m + 1, :rows, at].astype(f32)
            d_taps = dot(back[:, :rows], re.astype(bf16)) + dot(back[:, rows:], im.astype(bf16))
            d_taps = d_taps * (1.0 / rows)
            ramp, fall = window_of(m * rows, rows, blocks * rows, decay[:, at])
            g_d = -jnp.sum(d_taps * shaped[here, at] * ramp * fall, axis=0, keepdims=True)
            d_shaped = (d_taps * (fall + window_floor)).astype(bf16)
            g_o = dot(hidden[here], d_shaped, 0, 0)
            sum_out = g_o if sum_out is None else sum_out + g_o
            sum_decay = g_d if sum_decay is None else sum_decay + g_d
            d_hidden = dot(d_shaped, filter_out[:, at], 1, 1)
            g_hidden[here] = d_hidden if c == 0 else g_hidden[here] + d_hidden
        g_filter_out[:, at] = sum_out
        g_decay[:, at] = sum_decay
    d_c = g_hidden[...] * cos_c[...]
    g_last_bias[...] = jnp.sum(d_c, axis=0, keepdims=True)
    d_c = d_c.astype(bf16)
    g_last[...] = dot(sin_b[...].astype(bf16), d_c, 0, 0)
    d_b = dot(d_c, filter_last[...].astype(bf16), 1, 1) * cos_b[...]
    g_mid_bias[...] = jnp.sum(d_b, axis=0, keepdims=True)
    d_b = d_b.astype(bf16)
    g_mid[...] = dot(sin_a[...].astype(bf16), d_b, 0, 0)
    d_a = dot(d_b, filter_mid[...].astype(bf16), 1, 1) * cos_a[...]
    g_in[...] = dot(table[...].astype(bf16), d_a.astype(bf16), 0, 0)
    g_in_bias[...] = jnp.sum(d_a, axis=0, keepdims=True)


def filter_backward(lags, back, hidden, filter_out, decay, shaped, table, sines, cosines, filter_mid, filter_last):
    blocks, double_rows, width = lags.shape
    total, inner = hidden.shape
    shape = jax.ShapeDtypeStruct
    outs = [shape((inner, width), f32), shape((1, width), f32),
            shape((table.shape[1], inner), f32), shape((1, inner), f32), shape((inner, inner), f32),
            shape((1, inner), f32), shape((inner, inner), f32), shape((1, inner), f32)]
    arrays = [lags, back, hidden, filter_out, decay, shaped, table, sines[0], sines[1], *cosines, filter_mid, filter_last]
    return pl.pallas_call(
        partial(filter_back_body, blocks, double_rows // 2, 256),
        grid=(1,),
        in_specs=[whole(a.shape) for a in arrays],
        out_specs=[whole(a.shape) for a in outs],
        out_shape=outs,
        scratch_shapes=[pltpu.VMEM((total, inner), f32)],
        compiler_params=params(56),
        cost_estimate=cost(10 * total * width * double_rows, 10 << 20),
        name="filter_backward",
    )(*arrays)


PACK = 128


def pack_layout(width, shapes):
    out, narrow, row = [], 0, [64, 64]
    for shape in shapes:
        r, c = (1, shape[0]) if len(shape) == 1 else shape
        if c < width:
            out.append([((slice(0, r), slice(0, c)), 0, 0, narrow)])
            narrow += 128
        elif r > 32:
            out.append([((slice(0, r), slice(0, c)), 1, 0, 0)])
        else:
            entry = []
            for j in range(c // width):
                block = 0 if row[0] + r <= PACK else 1
                entry.append(((slice(0, r), slice(j * width, (j + 1) * width)), block, row[block], 0))
                row[block] += r
            out.append(entry)
    assert max(row) <= PACK and narrow <= width
    return out


def short_back_body(buckets, rows, first, meta, *refs):
    count = 1 if first else 2
    if first:
        mixture, d_gated, *refs = refs
    else:
        d_product, *refs = refs
    mixed, refs = refs[:count], refs[count:]
    normed, cw, cb, kept, sent, g_mixed, g_conv, g_conv_bias, g_bias, taps_in, d_pad = refs
    ext = rows + HALO
    inner = meta[0] > 0
    core = lax.rem(meta[0], 2)
    tile = cb.shape[1]
    width = normed.shape[1]
    sums = [[jnp.zeros((1, tile), f32)] * 5 for _ in range(count)]
    for b in range(buckets):
        short = []
        for t in range(count):
            k = t if first else t + 1
            taps_in[t] = mixed[t][0, b].astype(f32)
            s = cb[k : k + 1]
            if not first:
                for i in range(3):
                    s = s + cw[i, k : k + 1] * taps_in[t, HALO - 2 + i : HALO - 2 + i + rows]
            short.append(s)
        if first:
            d_shorts = (d_gated[b] * mixture[b],)
        else:
            d_prod = d_product[b] * live_rows(meta, b, rows)
            d_shorts = (d_prod * short[1], d_prod * short[0])
        for t in range(count):
            k = t if first else t + 1
            d_short = d_shorts[t]
            d_pad[t, :HALO] = jnp.zeros((HALO, tile), f32)
            d_pad[t, HALO : HALO + rows] = d_short
            d_pad[t, HALO + rows :] = jnp.zeros((8, tile), f32)
            for i in range(3):
                sums[t][i] = sums[t][i] + jnp.sum(
                    d_short * taps_in[t, HALO - 2 + i : HALO - 2 + i + rows], axis=0, keepdims=True)
            sums[t][3] = sums[t][3] + jnp.sum(d_short, axis=0, keepdims=True)
            g = (cw[2, k : k + 1] * d_pad[t, :ext] + cw[1, k : k + 1] * d_pad[t, 1 : ext + 1]
                 + cw[0, k : k + 1] * d_pad[t, 2 : ext + 2])
            head = jnp.where(inner, g[:HALO], 0.0).astype(bf16)
            body = g[HALO:].astype(bf16)
            g_mixed[t, b * ext : b * ext + HALO] = head
            g_mixed[t, b * ext + HALO : (b + 1) * ext] = body
            sums[t][4] = sums[t][4] + (jnp.sum(head.astype(f32), axis=0, keepdims=True)
                                       + jnp.sum(body.astype(f32), axis=0, keepdims=True))
    for t in range(count):
        for i in range(3):
            g_conv[i, t : t + 1] = sums[t][i]
        g_conv_bias[t : t + 1] = sums[t][3]
        g_bias[t : t + 1] = sums[t][4]
        kept[t] = dot(normed[:, own_half(core, width, True)], g_mixed[t], 0, 0).astype(bf16)
        sent[t] = dot(normed[:, own_half(core, width, False)], g_mixed[t], 0, 0).astype(bf16)


def short_backward(meta, sources, mixed, normed, conv_weight, conv_bias):
    _, buckets, ext, width = mixed.shape
    rows = ext - HALO
    tile = 256
    first = len(sources) == 2
    count = 1 if first else 2
    piece = pl.BlockSpec((buckets, rows, tile), lambda c: (0, 0, c))
    columns = [pl.BlockSpec((1, buckets, ext, tile), lambda c, t=t: (t, 0, 0, c)) for t in ([0] if first else [1, 2])]
    three = pl.BlockSpec((3, tile), lambda c: (0, c))
    nine = pl.BlockSpec((3, 3, tile), lambda c: (0, 0, c))
    line = pl.BlockSpec((count, tile), lambda c: (0, c))
    half = pl.BlockSpec((count, width // 2, tile), lambda c: (3 if first else 0, 0, c))
    halves = (4 if first else 2, width // 2, width)
    shape = jax.ShapeDtypeStruct
    return pl.pallas_call(
        partial(short_back_body, buckets, rows, first),
        grid=(width // tile,),
        in_specs=[SMEM, *[piece] * len(sources), *columns, whole(normed.shape), nine, three],
        out_specs=[
            half, half, pl.BlockSpec((count, buckets * ext, tile), lambda c: (0, 0, c)),
            pl.BlockSpec((3, count, tile), lambda c: (0, 0, c)), line, line,
        ],
        out_shape=[
            shape(halves, bf16), shape(halves, bf16),
            shape((count, buckets * ext, width), bf16), shape((3, count, width), f32), shape((count, width), f32),
            shape((count, width), f32),
        ],
        scratch_shapes=[pltpu.VMEM((count, ext, tile), f32), pltpu.VMEM((count, ext + 8, tile), f32)],
        compiler_params=params(56),
        cost_estimate=cost(2 * count * buckets * ext * width * width, 10 << 20),
        name="short_backward",
    )(meta, *sources, *[mixed] * count, normed, conv_weight, conv_bias)


def token_body(buckets, rows, layout, others, meta, g_first, g_mixed, weight, tok, halo, gain, d_resid, *refs):
    parts, refs = refs[:6], refs[6:]
    smalls, (g_tokens, d_halo, kept, sent, total, pack) = refs[:others], refs[others:]
    ext = rows + HALO
    step = pl.program_id(0)
    core = lax.rem(meta[0], 2)

    @pl.when(step == 0)
    def _():
        total[...] = dot(g_first[0], weight[...], 1, 1)

    @pl.when(step > 0)
    def _():
        total[...] += dot(g_mixed[0], weight[...], 1, 1)

    @pl.when(step == 2)
    def _():
        add = [jnp.zeros((1, gain.shape[1]), f32)] * 2
        for b in range(buckets):
            for first, size, source in ((0, HALO, halo), (HALO, rows, tok)):
                d = total[b * ext + first : b * ext + first + size]
                hat, scale = normalized(source[b].astype(f32))
                add[0] = add[0] + jnp.sum(d * hat, axis=0, keepdims=True)
                add[1] = add[1] + jnp.sum(d, axis=0, keepdims=True)
                e = d * gain[...]
                mean_e = jnp.mean(e, axis=-1, keepdims=True)
                mean_eh = jnp.mean(e * hat, axis=-1, keepdims=True)
                d_v = (e - mean_e - hat * mean_eh) * scale
                if first:
                    g_tokens[b] = d_resid[b] + d_v
                else:
                    d_halo[b] = d_v
        pack[...] = jnp.zeros_like(pack)
        for source, entry in zip(add, layout[:2]):
            (_, block, row, _), = entry
            pack[block, row : row + 1] = source
        conv, conv_bias, bias = parts[0::3], parts[1::3], parts[2::3]
        for j in range(3):
            p, q = (0, 0) if j == 0 else (1, j - 1)
            _, block, row, _ = layout[2][j]
            pack[block, row : row + 1] = bias[p][q : q + 1]
            _, block, row, _ = layout[4][j]
            pack[block, row : row + 1] = conv_bias[p][q : q + 1]
            _, block, row, _ = layout[3][j]
            for i in range(3):
                pack[block, row + i : row + i + 1] = conv[p][i, q : q + 1]
        for source, entry in zip(smalls, layout[5:]):
            for (r, c), block, row, lane in entry:
                pack[block, row : row + r.stop - r.start, lane : lane + c.stop - c.start] = source[r, c]
        kept[...] = jnp.where(core == 0, pack[...], 0.0).astype(bf16)
        sent[...] = jnp.where(core == 0, 0.0, pack[...]).astype(bf16)


def token_grads(meta, g_first, g_mixed, in_weight, tok, halo, gain, d_resid, parts, smalls, layout):
    buckets, rows, width = tok.shape
    ext = rows + HALO
    shape = jax.ShapeDtypeStruct
    packed = (2, PACK, width)
    arrays = [tok, halo, gain, d_resid, *parts, *smalls]
    return pl.pallas_call(
        partial(token_body, buckets, rows, layout, len(smalls)),
        grid=(3,),
        in_specs=[
            SMEM, whole(g_first.shape), pl.BlockSpec((1, buckets * ext, width), lambda t: (jnp.maximum(t - 1, 0), 0, 0)),
            pl.BlockSpec((width, width), lambda t: (0, t)), *[whole(a.shape) for a in arrays],
        ],
        out_specs=[whole(tok.shape), whole(halo.shape), whole(packed), whole(packed)],
        out_shape=[shape(tok.shape, f32), shape(halo.shape, f32), shape(packed, bf16), shape(packed, bf16)],
        scratch_shapes=[pltpu.VMEM((buckets * ext, width), f32), pltpu.VMEM(packed, f32)],
        compiler_params=params(56),
        cost_estimate=cost(6 * buckets * ext * width * width, 30 << 20),
        name="token_grads",
    )(meta, g_first, g_mixed, in_weight, *arrays)


def index_bits(axis):
    count = lax.axis_size(axis)
    return [(axis, 1 << i) for i in range(count.bit_length() - 1)]


def bit_of(axis, bit):
    return (lax.axis_index(axis) // bit) % 2


class Part:
    def __init__(self, terms, blocks, rows):
        self.terms, self.blocks, self.rows = terms, blocks, rows

    def total(self, first, rows):
        value = None
        for array, block, row in self.terms:
            term = lax.dynamic_slice(array, (block, row + first, 0), (self.blocks, rows, array.shape[2])).astype(f32)
            value = term if value is None else value + term
        return value.astype(bf16)


def halve(parts, axis, bit):
    mine = bit_of(axis, bit)
    halves = [p.rows // 2 for p in parts]
    sent = [p.total((1 - mine) * h, h) for p, h in zip(parts, halves)]
    come = xor_permute(sent[0] if len(sent) == 1 else jnp.concatenate(sent, axis=0), axis, bit)
    out, block = [], 0
    for p, h in zip(parts, halves):
        terms = [(array, at, row + mine * h) for array, at, row in p.terms]
        out.append(Part(terms + [(come, block, 0)], p.blocks, h))
        block += p.blocks
    return out


def waiting(chains):
    return [parts[0].terms[-1][0] for parts in chains]


def arrived(chains, arrays):
    for parts, array in zip(chains, arrays):
        for p in parts:
            p.terms[-1] = (array, *p.terms[-1][1:])


def double(array, axis, bit):
    return side_of(array, xor_permute(array, axis, bit), axis, bit)


def side_of(array, other, axis, bit):
    high = bit_of(axis, bit) == 1
    return jnp.concatenate([jnp.where(high, other, array), jnp.where(high, array, other)], axis=1)


def device_of(order):
    names = [b for axis in ("seq", "batch") for b in reversed(index_bits(axis))]
    last = len(names) - 1

    def device(shard):
        return sum((shard // (1 << (last - i))) % 2 * (1 << (last - names.index(b))) for i, b in enumerate(order))

    return device


def restored(gathered, order):
    names = [b for axis in ("seq", "batch") for b in reversed(index_bits(axis))]
    _, n, rows, width = gathered.shape
    cube = gathered.reshape([2] * len(names) + [n, rows, width])
    k = len(names)
    cube = cube.transpose([k] + [names.index(b) for b in order] + [k + 1, k + 2])
    return cube.reshape(n, -1, width).astype(f32)


def spread_body(half_steps, many, meta, *refs):
    sources, (kept_p, kept_q, other_p, other_q, up, out, into) = refs[: 3 * many], refs[3 * many :]
    width = out.shape[1]
    rows = out.shape[0] // many
    for j in range(many):
        first, b, c = sources[3 * j : 3 * j + 3]
        at = slice(j * rows, (j + 1) * rows)
        for i, source in enumerate((b[0, 0], b[0, 1], c[0, 0], c[0, 1])):
            up[at, i * width : (i + 1) * width] = source.astype(f32)
        out[at] = c[0, 2].astype(f32)
        into[at, :width] = first[0, 0].astype(f32)
    own = (pl.program_id(0) // half_steps) == lax.rem(meta[0], 2)
    for i, (kept, other) in enumerate(((kept_p, other_p), (kept_q, other_q))):
        value = jnp.where(own, kept[0].astype(f32), other[0].astype(f32))
        into[:, (i + 1) * width : (i + 2) * width] = value


def spread(meta, gathered, orders, kept, other):
    devices, stacked, rows, width = gathered.shape
    if rows % 8:
        half = width // 2
        high = lax.axis_index("seq") % 2 == 1
        x, y = (jnp.concatenate(p)[:, :half].astype(f32) for p in (kept, other))
        rest = jnp.concatenate([jnp.where(high, y, x), jnp.where(high, x, y)], axis=1)
        a = restored(gathered[:, 3:4], orders[0])
        b, c = restored(gathered[:, 4:], orders[1]), restored(gathered[:, :3], orders[2])
        return (jnp.concatenate([b[0], b[1], c[0], c[1]], axis=1), c[2],
                jnp.concatenate([a[0], rest[0], rest[1]], axis=1))
    places = [device_of(order) for order in orders]
    many = 4
    steps = devices // many
    half = steps // 2
    tall = many * rows
    piece = pl.BlockSpec((1, tall, width), lambda s: (0, s % half, 0))
    shape = jax.ShapeDtypeStruct
    sources = []
    for j in range(many):
        for size, block, place in ((1, 3, places[0]), (2, 2, places[1]), (3, 0, places[2])):
            sources.append(pl.BlockSpec(
                (1, size, rows, width), lambda s, i=block, p=place, j=j: (p(s * many + j), i, 0, 0)))
    return pl.pallas_call(
        partial(spread_body, half, many),
        grid=(steps,),
        in_specs=[SMEM, *sources, piece, piece, piece, piece],
        out_specs=[
            pl.BlockSpec((tall, 4 * width), lambda s: (s, 0)),
            pl.BlockSpec((tall, width), lambda s: (s, 0)),
            pl.BlockSpec((tall, 3 * width), lambda s: (s, 0)),
        ],
        out_shape=[shape((width, 4 * width), f32), shape((width, width), f32), shape((width, 3 * width), f32)],
        compiler_params=params(60),
        cost_estimate=cost(0, 6 * devices * stacked * rows * width),
        name="spread",
    )(meta, *[gathered] * (3 * many), *kept, *other)


def spread_down_body(half_steps, meta, kept_a, kept_b, other_a, other_b, target):
    own = (pl.program_id(0) // half_steps) == lax.rem(meta[0], 2)
    for first, kept, other in ((0, kept_a, other_a), (3, kept_b, other_b)):
        for j in range(kept.shape[0]):
            target[first + j] = jnp.where(own, kept[j].astype(f32), other[j].astype(f32))


def spread_down(meta, kept, other):
    _, half_rows, width = kept[0].shape
    rows = 96
    half = half_rows // rows
    piece = lambda n: pl.BlockSpec((n, rows, width), lambda s: (0, s % half, 0))
    return pl.pallas_call(
        partial(spread_down_body, half),
        grid=(2 * half,),
        in_specs=[SMEM, piece(3), piece(1), piece(3), piece(1)],
        out_specs=pl.BlockSpec((4, rows, width), lambda s: (0, s, 0)),
        out_shape=jax.ShapeDtypeStruct((4, 2 * half_rows, width), f32),
        compiler_params=params(48),
        cost_estimate=cost(0, 24 * width * width),
        name="spread_down",
    )(meta, *kept, *other).reshape(8 * half_rows, width)


def unpack_body(layout, meta, kept_p, kept_q, other_p, other_q, *refs):
    *targets, rows = refs
    core = lax.rem(meta[0], 2)
    for i, (kept, other) in enumerate(((kept_p, other_p), (kept_q, other_q))):
        rows[i] = jnp.where(core == 0, kept[0].astype(f32), other[0].astype(f32))
    for target, entry in zip(targets, layout):
        for (r, c), block, row, lane in entry:
            size, across = r.stop - r.start, c.stop - c.start
            part = rows[block, row : row + size, lane : lane + across]
            if len(target.shape) == 1:
                target[c] = part[0]
            else:
                target[r, c] = part


def unpack(meta, kept, other, layout, shapes):
    _, rows, width = kept[0].shape
    at = (rows - PACK) // PACK
    piece = pl.BlockSpec((1, PACK, width), lambda i: (0, at, 0))
    return pl.pallas_call(
        partial(unpack_body, layout),
        grid=(1,),
        in_specs=[SMEM, piece, piece, piece, piece],
        out_specs=[whole(s) for s in shapes],
        out_shape=[jax.ShapeDtypeStruct(s, f32) for s in shapes],
        scratch_shapes=[pltpu.VMEM((2, PACK, width), f32)],
        compiler_params=params(32),
        cost_estimate=cost(0, 2 << 20),
        name="unpack",
    )(meta, *kept, *other)


def shards(
    tokens, cotangent, lengths, norm1_gain, norm1_shift, in_weight, in_bias, conv_weight, conv_bias,
    filter_in, filter_in_bias, filter_mid, filter_mid_bias, filter_last, filter_last_bias, filter_out,
    decay_rate, skip_gain, out_weight, out_bias, norm2_gain, norm2_shift, up_weight, up_bias,
    down_weight, down_bias,
):
    buckets, rows, width = tokens.shape
    hidden_width = up_weight.shape[1]
    blocks = lax.axis_size("seq")
    devices = blocks * lax.axis_size("batch")
    count = buckets * rows
    meta = jnp.concatenate([lax.axis_index("seq")[None].astype(jnp.int32), lengths.astype(jnp.int32)])
    high_np, low_np = block_tables(rows)
    high, low = jnp.asarray(high_np), jnp.asarray(low_np)
    back = jnp.asarray(np.ascontiguousarray(high_np.T))
    line = lambda a: a.reshape(1, -1)

    halo = lax.ppermute(tokens[:, rows - HALO :], "seq", [(i, i + 1) for i in range(blocks - 1)])
    conv_w = conv_weight.reshape(3, 3, width)
    conv_b = conv_bias.reshape(3, width)
    normed, mixed, product, gate_out = front(
        meta, tokens, halo, line(norm1_gain), line(norm1_shift), in_weight, in_bias.reshape(3, width), conv_w, conv_b)
    far = exchange_far(product)
    table = jnp.asarray(features(rows * blocks, filter_in.shape[0]))
    sines, cosines = filter_layers(
        table, filter_in, filter_in_bias, filter_mid, filter_mid_bias, filter_last, filter_last_bias)
    hidden = sines[2]
    shaped, spectrum = filter_spectra(hidden, filter_out, line(decay_rate), high, low, blocks)
    far, spectrum = after(far, spectrum)
    products = exchange_near(far)
    mixture, gated = conv_forward(meta, products, spectrum, gate_out, line(skip_gain), high, back)

    flat = lambda a: a.reshape(count, width)
    (normed2, d_down, resid, active, d_up, g_up_bias, d_resid, d_mixer, d_gated, d_conv,
     g_norm2_gain, g_norm2_shift, g_out_bias) = middle(
        meta, flat(gated), out_weight, line(out_bias), flat(tokens), flat(cotangent), line(norm2_gain),
        line(norm2_shift), up_weight, line(up_bias), down_weight, flat(gate_out), buckets)
    cube = lambda a: a.reshape(buckets, rows, width)
    seq_bits, batch_bits = index_bits("seq"), index_bits("batch")
    core, far_seq, near_batch, far_batch = seq_bits[0], seq_bits[1:], batch_bits[:1], batch_bits[1:]
    orders = [near_batch + far_seq + far_batch, far_seq + far_batch + near_batch, far_batch + near_batch + far_seq]
    barrier = lax.optimization_barrier

    def wave(chains, at):
        return [halve(parts, *order[at]) for parts, order in zip(chains, orders)]

    far = exchange_far(cube(d_conv))
    first_kept, first_sent, g_first, *first_parts = short_backward(
        meta, (mixture, cube(d_gated)), mixed, normed, conv_w, conv_b)
    g_down_bias, *stacks = weight_grads(
        meta, active, d_up, normed2, d_down, flat(gated), d_mixer, first_kept, first_sent)
    kept, sent = stacks[:3], stacks[3:]
    far, sent, active = after(far, sent, active)
    block_out = layer_output(meta, active, down_weight, line(down_bias), resid, buckets)
    grads = exchange_near(far)
    come = [xor_permute(a, *core) for a in sent]
    come, grads, block_out = barrier((come, grads, block_out))
    stack = lambda k, c: Part([(k, 0, 0), (c, 0, 0)], k.shape[0], k.shape[1])
    chains = [[stack(k, c)] for k, c in zip(kept, come)]
    chains = wave(chains, 0)
    d_product, g_skip, lags = conv_backward(meta, grads, product, spectrum, line(skip_gain), high, back)

    come, d_product, lags = barrier((waiting(chains), d_product, lags))
    arrived(chains, come)
    chains = wave(chains, 1)
    in_kept, in_sent, g_mixed, *other_parts = short_backward(meta, (d_product,), mixed, normed, conv_w, conv_b)
    (g_filter_out, g_decay, g_filter_in, g_filter_in_bias, g_filter_mid, g_filter_mid_bias,
     g_filter_last, g_filter_last_bias) = filter_backward(
        lags, back, hidden.astype(bf16), filter_out.astype(bf16), line(decay_rate), shaped, table, sines, cosines,
        filter_mid, filter_last)

    come, in_sent, g_filter_out, g_mixed = barrier((waiting(chains), in_sent, g_filter_out, g_mixed))
    in_come = xor_permute(in_sent, *core)
    arrived(chains, come)
    chains = wave(chains, 2)
    shapes = [
        (width,), (width,), (3 * width,), (3, 3 * width), (3 * width,), filter_in.shape, filter_in_bias.shape,
        filter_mid.shape, filter_mid_bias.shape, filter_last.shape, filter_last_bias.shape, filter_out.shape,
        (width,), (width,), (width,), (width,), (width,), (hidden_width,), (width,),
    ]
    layout = pack_layout(width, shapes)
    smalls = [
        g_filter_in, g_filter_in_bias, g_filter_mid, g_filter_mid_bias, g_filter_last, g_filter_last_bias,
        g_filter_out, g_decay, g_skip, g_out_bias, g_norm2_gain, g_norm2_shift, g_up_bias, g_down_bias,
    ]
    g_tokens, d_halo, pack_kept, pack_sent = token_grads(
        meta, g_first, g_mixed, in_weight, tokens, halo, line(norm1_gain), cube(d_resid), first_parts + other_parts,
        smalls, layout)

    come, in_come, pack_sent = barrier((waiting(chains), in_come, pack_sent))
    arrived(chains, come)
    pack_come = xor_permute(pack_sent, *core)
    for at in range(3, len(orders[0])):
        chains = wave(chains, at)
    arriving = lax.ppermute(d_halo[:, HALO - 2 :], "seq", [(i + 1, i) for i in range(blocks - 1)])
    g_tokens = g_tokens.at[:, rows - 2 :].add(arriving)
    come, pack_come = barrier((waiting(chains), pack_come))
    arrived(chains, come)
    in_kept = jnp.concatenate([in_kept, pack_kept], axis=1)
    in_come = jnp.concatenate([in_come, pack_come], axis=1)
    whole_rows = in_kept.shape[1]
    order = orders[0]
    x, y, rest = near_batch[0], far_seq[0], far_seq[1:] + far_batch

    def in_sums():
        pair = [[Part([(in_kept, i, 0), (in_come, i, 0)], 1, whole_rows)] for i in range(2)]
        for steps in ((x, y), (y, x)):
            pair = [halve(parts, *step) for parts, step in zip(pair, steps)]
            arrived(pair, (yield waiting(pair)))
        joined = pair[0] + pair[1]
        for step in rest:
            joined = halve(joined, *step)
            arrived([joined], (yield waiting([joined])))
        done = jnp.concatenate([p.total(0, p.rows) for p in joined], axis=0)
        for step in reversed(rest):
            (come,) = yield [xor_permute(done, *step)]
            done = side_of(done, come, *step)
        pair = [done[:1], done[1:]]
        for steps in ((y, x), (x, y)):
            come = yield [xor_permute(a, *step) for a, step in zip(pair, steps)]
            pair = [side_of(a, c, *step) for a, c, step in zip(pair, come, steps)]
        come = yield [xor_permute(a, *core) for a in pair]
        return pair, come

    in_steps = in_sums()
    in_wait = next(in_steps)
    sums = [p.total(0, p.rows) for parts in chains for p in parts]
    both = jnp.concatenate([sums[2], sums[0][3:], sums[1][1:]], axis=0)
    gathered = lax.all_gather(both, ("seq", "batch"), axis=0)

    down = [sums[0][:3], sums[1][:1]]
    for steps in zip(reversed(orders[0]), reversed(orders[1])):
        down = [double(a, *step) for a, step in zip(down, steps)]
    grad_down_weight = spread_down(meta, down, [xor_permute(a, *core) for a in down])

    in_result, left = None, 2 * len(order) + 1
    while in_result is None:
        left -= 1
        if left == LAST_STEPS:
            in_wait, grad_down_weight, g_tokens = barrier((in_wait, grad_down_weight, g_tokens))
        try:
            in_wait = in_steps.send(in_wait)
        except StopIteration as end:
            in_result = end.value
    in_kept, in_come = in_result
    grad_up_weight, grad_out_weight, grad_in_weight = spread(
        meta, gathered, [[core, *o] for o in orders], in_kept, in_come)
    (n1g, n1s, inb, cw, cb, fi, fib, fm, fmb, fl, flb, fo, dr, sg, ob, n2g, n2s, ub, db) = unpack(
        meta, in_kept, in_come, layout, shapes)
    return (
        cube(block_out), g_tokens, n1g, n1s, grad_in_weight, inb, cw, cb, fi, fib, fm, fmb, fl, flb, fo, dr, sg,
        grad_out_weight, ob, n2g, n2s, grad_up_weight, ub, grad_down_weight, db,
    )


def solution(mesh):
    split = P("batch", "seq", None)
    return jax.shard_map(
        shards,
        mesh=mesh,
        in_specs=(split, split, P("batch")) + (P(),) * 23,
        out_specs=(split, split) + (P(),) * 23,
        check_vma=False,
    )
```

```python
from functools import partial
import math

import jax
import jax.numpy as jnp
import numpy as np
from jax import lax
from jax.experimental import pallas as pl
from jax.experimental.pallas import tpu as pltpu
from jax.sharding import PartitionSpec as P

norm_eps = 1e-05
window_floor = 0.05
highest = lax.Precision.HIGHEST
HALO = 16
CONV_TILE = 256
LAST_STEPS = 1
bf16 = jnp.bfloat16
f32 = jnp.float32


def dot(a, b, ca=1, cb=0, precision=None):
    return lax.dot_general(
        a, b, (((ca,), (cb,)), ((), ())), precision=precision, preferred_element_type=f32
    )


def xor_permute(array, axis, bit):
    count = lax.axis_size(axis)
    return lax.ppermute(array, axis, [(i, i ^ bit) for i in range(count)])


def exchange_far(array):
    held = {0: array}
    bit = lax.axis_size("seq") // 2
    while bit > 1:
        held.update({k ^ bit: xor_permute(a, "seq", bit) for k, a in list(held.items())})
        bit //= 2
    return held


def exchange_near(held):
    held = {**held, **{k ^ 1: xor_permute(a, "seq", 1) for k, a in held.items()}}
    return [held[k] for k in range(len(held))]


def after(held, *others):
    keys = [k for k in held if k]
    flat, others = lax.optimization_barrier(([held[k] for k in keys], others))
    return {**held, **dict(zip(keys, flat))}, *others


def block_tables(rows):
    phase = (2 * np.arange(rows)[:, None] + 1) * np.arange(rows)[None, :] % (4 * rows)
    angle = phase * (2.0 * math.pi / (4 * rows))
    table = np.concatenate([np.cos(angle), -np.sin(angle)], axis=0)
    high = table.astype(jnp.bfloat16)
    low = (table - high.astype(np.float64)).astype(jnp.bfloat16)
    return high, low


def features(seq_total, emb_width):
    bands = (emb_width - 1) // 2
    steps = np.arange(seq_total)
    phases = steps[:, None] * np.arange(1, bands + 1)[None, :] % seq_total
    angles = phases * (2.0 * math.pi / seq_total)
    ramp = steps / seq_total
    return np.concatenate([ramp[:, None], np.cos(angles), np.sin(angles)], axis=1).astype(np.float32)


def filter_layers(table, filter_in, in_bias, filter_mid, mid_bias, filter_last, last_bias):
    sines, cosines, value = [], [], table
    for weight, bias in ((filter_in, in_bias), (filter_mid, mid_bias), (filter_last, last_bias)):
        phase = jnp.dot(value, weight, precision=highest) + bias
        value = jnp.sin(phase)
        sines.append(value)
        cosines.append(jnp.cos(phase))
    return sines, cosines


def normalized(values):
    center = values - jnp.mean(values, axis=-1, keepdims=True)
    scale = lax.rsqrt(jnp.mean(center * center, axis=-1, keepdims=True) + norm_eps)
    return center * scale, scale


def live_rows(meta, bucket, rows):
    place = meta[0] * rows + lax.broadcasted_iota(jnp.int32, (rows, 1), 0)
    return (place < meta[1 + bucket]).astype(f32)


LIMIT = 0


def params(mib, count=1):
    return pltpu.CompilerParams(
        dimension_semantics=("arbitrary",) * count, vmem_limit_bytes=max(mib, LIMIT) * 1024 * 1024
    )


SMEM = pl.BlockSpec(memory_space=pltpu.SMEM)


def whole(shape):
    zeros = (0,) * len(shape)
    return pl.BlockSpec(tuple(shape), lambda *_: zeros)


def cost(flops, read):
    return pl.CostEstimate(flops=flops, bytes_accessed=read, transcendentals=0)


def front_body(buckets, rows, meta, tok, halo, gain, shift, w0, w1, w2, bias, cw, cb,
               normed, mixed, product, gate_out, taps_in):
    ext = rows + HALO

    @pl.when(pl.program_id(0) == 0)
    def _():
        for b in range(buckets):
            hat, _ = normalized(halo[b].astype(f32))
            normed[b * ext : b * ext + HALO] = (hat * gain[...] + shift[...]).astype(bf16)
            hat, _ = normalized(tok[b].astype(f32))
            normed[b * ext + HALO : (b + 1) * ext] = (hat * gain[...] + shift[...]).astype(bf16)

    inner = meta[0] > 0
    for b in range(buckets):
        parts = []
        for t, w in enumerate((w0, w1, w2)):
            m = (dot(normed[b * ext : (b + 1) * ext], w[...]) + bias[t : t + 1]).astype(bf16)
            head = jnp.where(inner, m[:HALO].astype(f32), 0.0)
            mixed[t, b, :HALO] = head.astype(bf16)
            mixed[t, b, HALO:] = m[HALO:]
            taps_in[t, :HALO] = head
            taps_in[t, HALO:] = m[HALO:].astype(f32)
            s = cb[t : t + 1]
            for i in range(3):
                s = s + cw[i, t : t + 1] * taps_in[t, HALO - 2 + i : HALO - 2 + i + rows]
            parts.append(s)
        gate_out[b] = parts[0]
        product[b] = (parts[2] * parts[1] * live_rows(meta, b, rows)).astype(bf16)


def front(meta, tok, halo, gain, shift, in_weight, in_bias, conv_weight, conv_bias):
    buckets, rows, width = tok.shape
    ext = rows + HALO
    tile = 256
    steps = width // tile
    columns = [pl.BlockSpec((width, tile), lambda c, t=t: (0, t * steps + c)) for t in range(3)]
    return pl.pallas_call(
        partial(front_body, buckets, rows),
        grid=(steps,),
        in_specs=[
            SMEM, whole(tok.shape), whole(halo.shape), whole((1, width)), whole((1, width)), *columns,
            pl.BlockSpec((3, tile), lambda c: (0, c)),
            pl.BlockSpec((3, 3, tile), lambda c: (0, 0, c)),
            pl.BlockSpec((3, tile), lambda c: (0, c)),
        ],
        out_specs=[
            whole((buckets * ext, width)),
            pl.BlockSpec((3, buckets, ext, tile), lambda c: (0, 0, 0, c)),
            pl.BlockSpec((buckets, rows, tile), lambda c: (0, 0, c)),
            pl.BlockSpec((buckets, rows, tile), lambda c: (0, 0, c)),
        ],
        out_shape=[
            jax.ShapeDtypeStruct((buckets * ext, width), bf16),
            jax.ShapeDtypeStruct((3, buckets, ext, width), bf16),
            jax.ShapeDtypeStruct((buckets, rows, width), bf16),
            jax.ShapeDtypeStruct((buckets, rows, width), f32),
        ],
        scratch_shapes=[pltpu.VMEM((3, ext, tile), f32)],
        compiler_params=params(48),
        cost_estimate=cost(6 * buckets * ext * width * width, 16 << 20),
        name="front",
    )(meta, tok, halo, gain, shift, in_weight, in_weight, in_weight, in_bias, conv_weight, conv_bias)


def alternating(rows):
    parity = lax.broadcasted_iota(jnp.int32, (rows, 1), 0) % 2
    return (1 - 2 * parity).astype(f32)


def window_of(first, rows, total, decay):
    ramp = (first + lax.broadcasted_iota(jnp.int32, (rows, 1), 0)).astype(f32) * (1.0 / total)
    return ramp, jnp.exp(-ramp * decay)


def filter_body(blocks, rows, hidden, out, decay, high, low, shaped, spectrum):
    sign = alternating(rows)
    last = None
    for m in range(blocks):
        here = slice(m * rows, (m + 1) * rows)
        plain = dot(hidden[here], out[...], precision=highest)
        shaped[here] = plain
        _, fall = window_of(m * rows, rows, blocks * rows, decay[...])
        taps = plain * (fall + window_floor)
        upper = taps.astype(bf16)
        rest = (taps - upper.astype(f32)).astype(bf16)
        full = dot(high[...], upper) + (dot(high[...], rest) + dot(low[...], upper))
        re, im = full[:rows], full[rows:]
        if last is None:
            spectrum[m, :rows] = re.astype(bf16)
            spectrum[m, rows:] = im.astype(bf16)
        else:
            spectrum[m, :rows] = (re - sign * last[1]).astype(bf16)
            spectrum[m, rows:] = (im + sign * last[0]).astype(bf16)
        last = (re, im)
    spectrum[blocks] = jnp.zeros(spectrum.shape[1:], bf16)


def filter_spectra(hidden, filter_out, decay, high, low, blocks):
    total, inner = hidden.shape
    width = filter_out.shape[1]
    rows = total // blocks
    tile = 256
    return pl.pallas_call(
        partial(filter_body, blocks, rows),
        grid=(width // tile,),
        in_specs=[
            whole(hidden.shape),
            pl.BlockSpec((inner, tile), lambda c: (0, c)),
            pl.BlockSpec((1, tile), lambda c: (0, c)),
            whole(high.shape), whole(low.shape),
        ],
        out_specs=[
            pl.BlockSpec((total, tile), lambda c: (0, c)),
            pl.BlockSpec((blocks + 1, 2 * rows, tile), lambda c: (0, 0, c)),
        ],
        out_shape=[
            jax.ShapeDtypeStruct((total, width), f32),
            jax.ShapeDtypeStruct((blocks + 1, 2 * rows, width), bf16),
        ],
        compiler_params=params(48),
        cost_estimate=cost(20 * total * width * rows, 10 << 20),
        name="filter_spectra",
    )(hidden, filter_out, decay, high, low)


def conv_body(blocks, rows, meta, *refs):
    products = refs[:blocks]
    spectrum, gate_out, skip, high, back, mixture, gated = refs[blocks:]
    own = meta[0]
    for c in range(products[0].shape[2] // CONV_TILE):
        at = slice(c * CONV_TILE, (c + 1) * CONV_TILE)
        sum_re = sum_im = None
        for k in range(blocks):
            lag = own - (own ^ k)
            lag = jnp.where(lag < 0, blocks, lag)
            full = dot(high[...], products[k][0, :, at])
            re, im = full[:rows], full[rows:]
            tap_re, tap_im = spectrum[lag, :rows, at].astype(f32), spectrum[lag, rows:, at].astype(f32)
            out_re = tap_re * re - tap_im * im
            out_im = tap_re * im + tap_im * re
            sum_re = out_re if sum_re is None else sum_re + out_re
            sum_im = out_im if sum_im is None else sum_im + out_im
        convolved = dot(back[:, :rows], sum_re.astype(bf16)) + dot(back[:, rows:], sum_im.astype(bf16))
        mixed = convolved * (1.0 / rows) + skip[:, at] * products[0][0, :, at].astype(f32)
        mixture[0, :, at] = mixed
        gated[0, :, at] = (mixed * gate_out[0, :, at]).astype(bf16)


def conv_forward(meta, products, spectrum, gate_out, skip, high, back):
    buckets, rows, width = gate_out.shape
    blocks = len(products)
    tile = width
    piece = pl.BlockSpec((1, rows, tile), lambda c, b: (b, 0, c))
    return pl.pallas_call(
        partial(conv_body, blocks, rows),
        grid=(width // tile, buckets),
        in_specs=[SMEM] + [piece] * blocks + [
            pl.BlockSpec((blocks + 1, 2 * rows, tile), lambda c, b: (0, 0, c)), piece,
            pl.BlockSpec((1, tile), lambda c, b: (0, c)), whole(high.shape), whole(back.shape),
        ],
        out_specs=[piece, piece],
        out_shape=[
            jax.ShapeDtypeStruct((buckets, rows, width), f32),
            jax.ShapeDtypeStruct((buckets, rows, width), bf16),
        ],
        compiler_params=params(56, 2),
        cost_estimate=cost(4 * (blocks + 1) * rows * rows * width * buckets, 16 << 20),
        name="conv_forward",
    )(meta, *products, spectrum, gate_out, skip, high, back)


def gelu_parts(u):
    cdf = 0.5 + 0.5 * lax.erf(u * (1.0 / math.sqrt(2.0)))
    pdf = jnp.exp(-0.5 * u * u) * (1.0 / math.sqrt(2.0 * math.pi))
    return u * cdf, cdf + u * pdf


def middle_body(buckets, rows, steps, meta, gated, out_w, out_b, tok, cot, gain, shift, up_w, up_b, down_w,
                gate_out, normed2, d_down, resid, active, d_up, g_up_bias, d_resid, d_mixer, d_gated, d_conv,
                g_gain, g_shift, g_out_bias, total):
    step = pl.program_id(0)

    @pl.when(step == 0)
    def _():
        for b in range(buckets):
            here = slice(b * rows, (b + 1) * rows)
            live = live_rows(meta, b, rows)
            mixer = dot(gated[here], out_w[...]) + out_b[...]
            r = tok[here].astype(f32) + live * mixer
            resid[here] = r
            hat, _ = normalized(r)
            normed2[here] = (hat * gain[...] + shift[...]).astype(bf16)
            d_down[here] = (live * cot[here].astype(f32)).astype(bf16)
            total[here] = jnp.zeros_like(total[here])

    bias_sum = None
    for b in range(buckets):
        here = slice(b * rows, (b + 1) * rows)
        u = dot(normed2[here], up_w[...]) + up_b[...]
        d_active = dot(d_down[here], down_w[...], 1, 1)
        act, slope = gelu_parts(u)
        active[here] = act.astype(bf16)
        d_u = (d_active * slope).astype(bf16)
        d_up[here] = d_u
        part = jnp.sum(d_u.astype(f32), axis=0, keepdims=True)
        bias_sum = part if bias_sum is None else bias_sum + part
        back = dot(d_u, up_w[...], 1, 1)

        total[here] += back

    g_up_bias[...] = bias_sum

    @pl.when(step == steps - 1)
    def _():
        sums = [jnp.zeros((1, gain.shape[1]), f32)] * 3
        for b in range(buckets):
            here = slice(b * rows, (b + 1) * rows)
            live = live_rows(meta, b, rows)
            hat, scale = normalized(resid[here])
            d = total[here]
            sums[0] = sums[0] + jnp.sum(d * hat, axis=0, keepdims=True)
            sums[1] = sums[1] + jnp.sum(d, axis=0, keepdims=True)
            e = d * gain[...]
            mean_e = jnp.mean(e, axis=-1, keepdims=True)
            mean_eh = jnp.mean(e * hat, axis=-1, keepdims=True)
            d_r = cot[here].astype(f32) + (e - mean_e - hat * mean_eh) * scale
            d_resid[here] = d_r
            d_m = (live * d_r).astype(bf16)
            d_mixer[here] = d_m
            sums[2] = sums[2] + jnp.sum(d_m.astype(f32), axis=0, keepdims=True)
            d_g = dot(d_m, out_w[...], 1, 1)
            d_gated[here] = d_g
            d_conv[here] = (d_g * gate_out[here]).astype(bf16)
        g_gain[...] = sums[0]
        g_shift[...] = sums[1]
        g_out_bias[...] = sums[2]


def middle(meta, gated, out_w, out_b, tok, cot, gain, shift, up_w, up_b, down_w, gate_out, buckets):
    count, width = tok.shape
    hidden = up_w.shape[1]
    tile = width
    steps = hidden // tile
    rows = count // buckets
    square = whole((count, width))
    line = whole((1, width))
    shape = jax.ShapeDtypeStruct
    return pl.pallas_call(
        partial(middle_body, buckets, rows, steps),
        grid=(steps,),
        in_specs=[
            SMEM, square, whole(out_w.shape), line, square, square, line, line,
            pl.BlockSpec((width, tile), lambda s: (0, s)),
            pl.BlockSpec((1, tile), lambda s: (0, s)),
            pl.BlockSpec((tile, width), lambda s: (s, 0)),
            square,
        ],
        out_specs=[
            square, square, square,
            pl.BlockSpec((count, tile), lambda s: (0, s)),
            pl.BlockSpec((count, tile), lambda s: (0, s)),
            pl.BlockSpec((1, tile), lambda s: (0, s)),
            square, square, square, square, line, line, line,
        ],
        out_shape=[
            shape((count, width), bf16), shape((count, width), bf16), shape((count, width), f32),
            shape((count, hidden), bf16), shape((count, hidden), bf16), shape((1, hidden), f32),
            shape((count, width), f32), shape((count, width), bf16), shape((count, width), f32),
            shape((count, width), bf16), shape((1, width), f32), shape((1, width), f32), shape((1, width), f32),
        ],
        scratch_shapes=[pltpu.VMEM((count, width), f32)],
        compiler_params=params(56),
        cost_estimate=cost(6 * count * width * hidden, 40 << 20),
        name="middle",
    )(meta, gated, out_w, out_b, tok, cot, gain, shift, up_w, up_b, down_w, gate_out)


def own_half(core, width, mine):
    half = width // 2
    return pl.ds(pl.multiple_of((core if mine else 1 - core) * half, half), half)


def weights_body(steps, meta, active, d_up, normed2, d_down, gated, d_mixer, first_kept, first_sent, g_bias, *stacks):
    del first_kept, first_sent
    kept, sent = stacks[:3], stacks[3:]
    step = pl.program_id(0)
    core = lax.rem(meta[0], 2)
    width = normed2.shape[1]
    mine, theirs = own_half(core, width, True), own_half(core, width, False)

    @pl.when(step < steps)
    def _():
        down = [dot(active[:, at], d_down[...], 0, 0).astype(bf16) for at in (mine, theirs)]
        up = [dot(normed2[:, at], d_up[...], 0, 0).astype(bf16) for at in (mine, theirs)]
        for first, stop, source, stack in ((0, 3, down, 0), (3, 4, down, 1), (0, 2, up, 1), (2, 4, up, 2)):

            @pl.when((step >= first) & (step < stop))
            def _(source=source, stack=stack):
                kept[stack][0] = source[0]
                sent[stack][0] = source[1]

    @pl.when(step == steps)
    def _():
        kept[2][0] = dot(gated[:, mine], d_mixer[...], 0, 0).astype(bf16)
        sent[2][0] = dot(gated[:, theirs], d_mixer[...], 0, 0).astype(bf16)
        g_bias[...] = jnp.sum(d_down[...].astype(f32), axis=0, keepdims=True)


def weight_grads(meta, active, d_up, normed2, d_down, gated, d_mixer, first_kept, first_sent):
    count, width = normed2.shape
    hidden = active.shape[1]
    steps = hidden // width
    assert steps == 4
    square = whole((count, width))
    shape = jax.ShapeDtypeStruct
    last = steps - 1
    columns = pl.BlockSpec((count, width), lambda s: (0, jnp.minimum(s, last)))
    half = (1, width // 2, width)
    stacks = [
        pl.BlockSpec(half, lambda s: (jnp.minimum(s, 2), 0, 0)),
        pl.BlockSpec(half, lambda s: (jnp.where(s > 2, 0, jnp.minimum(s + 1, 2)), 0, 0)),
        pl.BlockSpec(half, lambda s: (jnp.maximum(s - 2, 0), 0, 0)),
    ]
    return pl.pallas_call(
        partial(weights_body, steps),
        grid=(steps + 1,),
        in_specs=[SMEM, columns, columns, square, square, square, square] + [pl.BlockSpec(memory_space=pl.ANY)] * 2,
        out_specs=[whole((1, width)), *stacks, *stacks],
        out_shape=[shape((1, width), f32)] + [shape((n, width // 2, width), bf16) for n in (4, 3, 3)] * 2,
        input_output_aliases={7: 1, 8: 4},
        compiler_params=params(56),
        cost_estimate=cost(4 * count * width * hidden, 40 << 20),
        name="weight_grads",
    )(meta, active, d_up, normed2, d_down, gated, d_mixer, first_kept, first_sent)


def output_body(buckets, rows, steps, meta, active, down_w, down_b, resid, block_out, total):
    step = pl.program_id(0)

    @pl.when(step == 0)
    def _():
        total[...] = dot(active[...], down_w[...])

    @pl.when(step > 0)
    def _():
        total[...] += dot(active[...], down_w[...])

    @pl.when(step == steps - 1)
    def _():
        for b in range(buckets):
            here = slice(b * rows, (b + 1) * rows)
            live = live_rows(meta, b, rows)
            block_out[here] = (resid[here] + live * (total[here] + down_b[...])).astype(bf16)


def layer_output(meta, active, down_w, down_b, resid, buckets):
    count, width = resid.shape
    hidden = down_w.shape[0]
    steps = hidden // width
    return pl.pallas_call(
        partial(output_body, buckets, count // buckets, steps),
        grid=(steps,),
        in_specs=[
            SMEM, pl.BlockSpec((count, width), lambda s: (0, s)), pl.BlockSpec((width, width), lambda s: (s, 0)),
            whole((1, width)), whole((count, width)),
        ],
        out_specs=whole((count, width)),
        out_shape=jax.ShapeDtypeStruct((count, width), bf16),
        scratch_shapes=[pltpu.VMEM((count, width), f32)],
        compiler_params=params(48),
        cost_estimate=cost(2 * count * width * hidden, 14 << 20),
        name="layer_output",
    )(meta, active, down_w, down_b, resid)


def conv_back_body(blocks, rows, buckets, meta, *refs):
    grads = refs[:blocks]
    product, spectrum, skip, high, back, d_product, g_skip, g_lags, lags = refs[blocks:]
    own = meta[0]
    b = pl.program_id(1)

    @pl.when(b == 0)
    def _():
        lags[...] = jnp.zeros_like(lags)
        g_skip[...] = jnp.zeros_like(g_skip)

    full = dot(high[...], product[0])
    prod_re, prod_im = full[:rows], full[rows:]
    sum_re = sum_im = None
    for k in range(blocks):
        lag = (own ^ k) - own
        lag = jnp.where(lag < 0, blocks, lag)
        grad = dot(high[...], grads[k][0])
        re, im = grad[:rows], grad[rows:]
        tap_re, tap_im = spectrum[lag, :rows].astype(f32), spectrum[lag, rows:].astype(f32)
        out_re = tap_re * re + tap_im * im
        out_im = tap_re * im - tap_im * re
        sum_re = out_re if sum_re is None else sum_re + out_re
        sum_im = out_im if sum_im is None else sum_im + out_im
        lags[lag, :rows] += re * prod_re + im * prod_im
        lags[lag, rows:] += im * prod_re - re * prod_im
    d_own = grads[0][0].astype(f32)
    full = dot(back[:, :rows], sum_re.astype(bf16)) + dot(back[:, rows:], sum_im.astype(bf16))
    d_product[0] = full * (1.0 / rows) + skip[...] * d_own
    g_skip[...] += jnp.sum(d_own * product[0].astype(f32), axis=0, keepdims=True)

    @pl.when(b == buckets - 1)
    def _():
        g_lags[...] = lags[:blocks].astype(bf16)


def conv_backward(meta, grads, product, spectrum, skip, high, back):
    buckets, rows, width = product.shape
    blocks = len(grads)
    tile = CONV_TILE
    piece = pl.BlockSpec((1, rows, tile), lambda c, b: (b, 0, c))
    line = pl.BlockSpec((1, tile), lambda c, b: (0, c))
    shape = jax.ShapeDtypeStruct
    return pl.pallas_call(
        partial(conv_back_body, blocks, rows, buckets),
        grid=(width // tile, buckets),
        in_specs=[SMEM] + [piece] * blocks + [
            piece, pl.BlockSpec((blocks + 1, 2 * rows, tile), lambda c, b: (0, 0, c)), line, whole(high.shape),
            whole(back.shape),
        ],
        out_specs=[piece, line, pl.BlockSpec((blocks, 2 * rows, tile), lambda c, b: (0, 0, c))],
        out_shape=[shape((buckets, rows, width), f32), shape((1, width), f32), shape((blocks, 2 * rows, width), bf16)],
        scratch_shapes=[pltpu.VMEM((blocks + 1, 2 * rows, tile), f32)],
        compiler_params=params(60, 2),
        cost_estimate=cost(4 * (2 * blocks + 2) * rows * rows * width * buckets, 20 << 20),
        name="conv_backward",
    )(meta, *grads, product, spectrum, skip, high, back)


def filter_back_body(blocks, rows, tile, lags, back, hidden, filter_out, decay, shaped, table, sin_a, sin_b, cos_a, cos_b,
                     cos_c, filter_mid, filter_last, g_filter_out, g_decay, g_in, g_in_bias, g_mid, g_mid_bias,
                     g_last, g_last_bias, g_hidden):
    sign = alternating(rows)
    for c in range(decay.shape[1] // tile):
        at = slice(c * tile, (c + 1) * tile)
        sum_out = sum_decay = None
        for m in range(blocks):
            here = slice(m * rows, (m + 1) * rows)
            re, im = lags[m, :rows, at].astype(f32), lags[m, rows:, at].astype(f32)
            if m + 1 < blocks:
                re = re + sign * lags[m + 1, rows:, at].astype(f32)
                im = im - sign * lags[m + 1, :rows, at].astype(f32)
            d_taps = dot(back[:, :rows], re.astype(bf16)) + dot(back[:, rows:], im.astype(bf16))
            d_taps = d_taps * (1.0 / rows)
            ramp, fall = window_of(m * rows, rows, blocks * rows, decay[:, at])
            g_d = -jnp.sum(d_taps * shaped[here, at] * ramp * fall, axis=0, keepdims=True)
            d_shaped = (d_taps * (fall + window_floor)).astype(bf16)
            g_o = dot(hidden[here], d_shaped, 0, 0)
            sum_out = g_o if sum_out is None else sum_out + g_o
            sum_decay = g_d if sum_decay is None else sum_decay + g_d
            d_hidden = dot(d_shaped, filter_out[:, at], 1, 1)
            g_hidden[here] = d_hidden if c == 0 else g_hidden[here] + d_hidden
        g_filter_out[:, at] = sum_out
        g_decay[:, at] = sum_decay
    d_c = g_hidden[...] * cos_c[...]
    g_last_bias[...] = jnp.sum(d_c, axis=0, keepdims=True)
    d_c = d_c.astype(bf16)
    g_last[...] = dot(sin_b[...].astype(bf16), d_c, 0, 0)
    d_b = dot(d_c, filter_last[...].astype(bf16), 1, 1) * cos_b[...]
    g_mid_bias[...] = jnp.sum(d_b, axis=0, keepdims=True)
    d_b = d_b.astype(bf16)
    g_mid[...] = dot(sin_a[...].astype(bf16), d_b, 0, 0)
    d_a = dot(d_b, filter_mid[...].astype(bf16), 1, 1) * cos_a[...]
    g_in[...] = dot(table[...].astype(bf16), d_a.astype(bf16), 0, 0)
    g_in_bias[...] = jnp.sum(d_a, axis=0, keepdims=True)


def filter_backward(lags, back, hidden, filter_out, decay, shaped, table, sines, cosines, filter_mid, filter_last):
    blocks, double_rows, width = lags.shape
    total, inner = hidden.shape
    shape = jax.ShapeDtypeStruct
    outs = [shape((inner, width), f32), shape((1, width), f32),
            shape((table.shape[1], inner), f32), shape((1, inner), f32), shape((inner, inner), f32),
            shape((1, inner), f32), shape((inner, inner), f32), shape((1, inner), f32)]
    arrays = [lags, back, hidden, filter_out, decay, shaped, table, sines[0], sines[1], *cosines, filter_mid, filter_last]
    return pl.pallas_call(
        partial(filter_back_body, blocks, double_rows // 2, 256),
        grid=(1,),
        in_specs=[whole(a.shape) for a in arrays],
        out_specs=[whole(a.shape) for a in outs],
        out_shape=outs,
        scratch_shapes=[pltpu.VMEM((total, inner), f32)],
        compiler_params=params(56),
        cost_estimate=cost(10 * total * width * double_rows, 10 << 20),
        name="filter_backward",
    )(*arrays)


PACK = 128


def pack_layout(width, shapes):
    out, narrow, row = [], 0, [64, 64]
    for shape in shapes:
        r, c = (1, shape[0]) if len(shape) == 1 else shape
        if c < width:
            out.append([((slice(0, r), slice(0, c)), 0, 0, narrow)])
            narrow += 128
        elif r > 32:
            out.append([((slice(0, r), slice(0, c)), 1, 0, 0)])
        else:
            entry = []
            for j in range(c // width):
                block = 0 if row[0] + r <= PACK else 1
                entry.append(((slice(0, r), slice(j * width, (j + 1) * width)), block, row[block], 0))
                row[block] += r
            out.append(entry)
    assert max(row) <= PACK and narrow <= width
    return out


def short_back_body(buckets, rows, first, meta, *refs):
    count = 1 if first else 2
    if first:
        mixture, d_gated, *refs = refs
    else:
        d_product, *refs = refs
    mixed, refs = refs[:count], refs[count:]
    normed, cw, cb, kept, sent, g_mixed, g_conv, g_conv_bias, g_bias, taps_in, d_pad = refs
    ext = rows + HALO
    inner = meta[0] > 0
    core = lax.rem(meta[0], 2)
    tile = cb.shape[1]
    width = normed.shape[1]
    sums = [[jnp.zeros((1, tile), f32)] * 5 for _ in range(count)]
    for b in range(buckets):
        short = []
        for t in range(count):
            k = t if first else t + 1
            taps_in[t] = mixed[t][0, b].astype(f32)
            s = cb[k : k + 1]
            if not first:
                for i in range(3):
                    s = s + cw[i, k : k + 1] * taps_in[t, HALO - 2 + i : HALO - 2 + i + rows]
            short.append(s)
        if first:
            d_shorts = (d_gated[b] * mixture[b],)
        else:
            d_prod = d_product[b] * live_rows(meta, b, rows)
            d_shorts = (d_prod * short[1], d_prod * short[0])
        for t in range(count):
            k = t if first else t + 1
            d_short = d_shorts[t]
            d_pad[t, :HALO] = jnp.zeros((HALO, tile), f32)
            d_pad[t, HALO : HALO + rows] = d_short
            d_pad[t, HALO + rows :] = jnp.zeros((8, tile), f32)
            for i in range(3):
                sums[t][i] = sums[t][i] + jnp.sum(
                    d_short * taps_in[t, HALO - 2 + i : HALO - 2 + i + rows], axis=0, keepdims=True)
            sums[t][3] = sums[t][3] + jnp.sum(d_short, axis=0, keepdims=True)
            g = (cw[2, k : k + 1] * d_pad[t, :ext] + cw[1, k : k + 1] * d_pad[t, 1 : ext + 1]
                 + cw[0, k : k + 1] * d_pad[t, 2 : ext + 2])
            head = jnp.where(inner, g[:HALO], 0.0).astype(bf16)
            body = g[HALO:].astype(bf16)
            g_mixed[t, b * ext : b * ext + HALO] = head
            g_mixed[t, b * ext + HALO : (b + 1) * ext] = body
            sums[t][4] = sums[t][4] + (jnp.sum(head.astype(f32), axis=0, keepdims=True)
                                       + jnp.sum(body.astype(f32), axis=0, keepdims=True))
    for t in range(count):
        for i in range(3):
            g_conv[i, t : t + 1] = sums[t][i]
        g_conv_bias[t : t + 1] = sums[t][3]
        g_bias[t : t + 1] = sums[t][4]
        kept[t] = dot(normed[:, own_half(core, width, True)], g_mixed[t], 0, 0).astype(bf16)
        sent[t] = dot(normed[:, own_half(core, width, False)], g_mixed[t], 0, 0).astype(bf16)


def short_backward(meta, sources, mixed, normed, conv_weight, conv_bias):
    _, buckets, ext, width = mixed.shape
    rows = ext - HALO
    tile = 256
    first = len(sources) == 2
    count = 1 if first else 2
    piece = pl.BlockSpec((buckets, rows, tile), lambda c: (0, 0, c))
    columns = [pl.BlockSpec((1, buckets, ext, tile), lambda c, t=t: (t, 0, 0, c)) for t in ([0] if first else [1, 2])]
    three = pl.BlockSpec((3, tile), lambda c: (0, c))
    nine = pl.BlockSpec((3, 3, tile), lambda c: (0, 0, c))
    line = pl.BlockSpec((count, tile), lambda c: (0, c))
    half = pl.BlockSpec((count, width // 2, tile), lambda c: (3 if first else 0, 0, c))
    halves = (4 if first else 2, width // 2, width)
    shape = jax.ShapeDtypeStruct
    return pl.pallas_call(
        partial(short_back_body, buckets, rows, first),
        grid=(width // tile,),
        in_specs=[SMEM, *[piece] * len(sources), *columns, whole(normed.shape), nine, three],
        out_specs=[
            half, half, pl.BlockSpec((count, buckets * ext, tile), lambda c: (0, 0, c)),
            pl.BlockSpec((3, count, tile), lambda c: (0, 0, c)), line, line,
        ],
        out_shape=[
            shape(halves, bf16), shape(halves, bf16),
            shape((count, buckets * ext, width), bf16), shape((3, count, width), f32), shape((count, width), f32),
            shape((count, width), f32),
        ],
        scratch_shapes=[pltpu.VMEM((count, ext, tile), f32), pltpu.VMEM((count, ext + 8, tile), f32)],
        compiler_params=params(56),
        cost_estimate=cost(2 * count * buckets * ext * width * width, 10 << 20),
        name="short_backward",
    )(meta, *sources, *[mixed] * count, normed, conv_weight, conv_bias)


def token_body(buckets, rows, layout, others, meta, g_first, g_mixed, weight, tok, halo, gain, d_resid, *refs):
    parts, refs = refs[:6], refs[6:]
    smalls, (g_tokens, d_halo, kept, sent, total, pack) = refs[:others], refs[others:]
    ext = rows + HALO
    step = pl.program_id(0)
    core = lax.rem(meta[0], 2)

    @pl.when(step == 0)
    def _():
        total[...] = dot(g_first[0], weight[...], 1, 1)

    @pl.when(step > 0)
    def _():
        total[...] += dot(g_mixed[0], weight[...], 1, 1)

    @pl.when(step == 2)
    def _():
        add = [jnp.zeros((1, gain.shape[1]), f32)] * 2
        for b in range(buckets):
            for first, size, source in ((0, HALO, halo), (HALO, rows, tok)):
                d = total[b * ext + first : b * ext + first + size]
                hat, scale = normalized(source[b].astype(f32))
                add[0] = add[0] + jnp.sum(d * hat, axis=0, keepdims=True)
                add[1] = add[1] + jnp.sum(d, axis=0, keepdims=True)
                e = d * gain[...]
                mean_e = jnp.mean(e, axis=-1, keepdims=True)
                mean_eh = jnp.mean(e * hat, axis=-1, keepdims=True)
                d_v = (e - mean_e - hat * mean_eh) * scale
                if first:
                    g_tokens[b] = d_resid[b] + d_v
                else:
                    d_halo[b] = d_v
        pack[...] = jnp.zeros_like(pack)
        for source, entry in zip(add, layout[:2]):
            (_, block, row, _), = entry
            pack[block, row : row + 1] = source
        conv, conv_bias, bias = parts[0::3], parts[1::3], parts[2::3]
        for j in range(3):
            p, q = (0, 0) if j == 0 else (1, j - 1)
            _, block, row, _ = layout[2][j]
            pack[block, row : row + 1] = bias[p][q : q + 1]
            _, block, row, _ = layout[4][j]
            pack[block, row : row + 1] = conv_bias[p][q : q + 1]
            _, block, row, _ = layout[3][j]
            for i in range(3):
                pack[block, row + i : row + i + 1] = conv[p][i, q : q + 1]
        for source, entry in zip(smalls, layout[5:]):
            for (r, c), block, row, lane in entry:
                pack[block, row : row + r.stop - r.start, lane : lane + c.stop - c.start] = source[r, c]
        kept[...] = jnp.where(core == 0, pack[...], 0.0).astype(bf16)
        sent[...] = jnp.where(core == 0, 0.0, pack[...]).astype(bf16)


def token_grads(meta, g_first, g_mixed, in_weight, tok, halo, gain, d_resid, parts, smalls, layout):
    buckets, rows, width = tok.shape
    ext = rows + HALO
    shape = jax.ShapeDtypeStruct
    packed = (2, PACK, width)
    arrays = [tok, halo, gain, d_resid, *parts, *smalls]
    return pl.pallas_call(
        partial(token_body, buckets, rows, layout, len(smalls)),
        grid=(3,),
        in_specs=[
            SMEM, whole(g_first.shape), pl.BlockSpec((1, buckets * ext, width), lambda t: (jnp.maximum(t - 1, 0), 0, 0)),
            pl.BlockSpec((width, width), lambda t: (0, t)), *[whole(a.shape) for a in arrays],
        ],
        out_specs=[whole(tok.shape), whole(halo.shape), whole(packed), whole(packed)],
        out_shape=[shape(tok.shape, f32), shape(halo.shape, f32), shape(packed, bf16), shape(packed, bf16)],
        scratch_shapes=[pltpu.VMEM((buckets * ext, width), f32), pltpu.VMEM(packed, f32)],
        compiler_params=params(56),
        cost_estimate=cost(6 * buckets * ext * width * width, 30 << 20),
        name="token_grads",
    )(meta, g_first, g_mixed, in_weight, *arrays)


def index_bits(axis):
    count = lax.axis_size(axis)
    return [(axis, 1 << i) for i in range(count.bit_length() - 1)]


def bit_of(axis, bit):
    return (lax.axis_index(axis) // bit) % 2


class Part:
    def __init__(self, terms, blocks, rows):
        self.terms, self.blocks, self.rows = terms, blocks, rows

    def total(self, first, rows):
        value = None
        for array, block, row in self.terms:
            term = lax.dynamic_slice(array, (block, row + first, 0), (self.blocks, rows, array.shape[2])).astype(f32)
            value = term if value is None else value + term
        return value.astype(bf16)


def halve(parts, axis, bit):
    mine = bit_of(axis, bit)
    halves = [p.rows // 2 for p in parts]
    sent = [p.total((1 - mine) * h, h) for p, h in zip(parts, halves)]
    come = xor_permute(sent[0] if len(sent) == 1 else jnp.concatenate(sent, axis=0), axis, bit)
    out, block = [], 0
    for p, h in zip(parts, halves):
        terms = [(array, at, row + mine * h) for array, at, row in p.terms]
        out.append(Part(terms + [(come, block, 0)], p.blocks, h))
        block += p.blocks
    return out


def waiting(chains):
    return [parts[0].terms[-1][0] for parts in chains]


def arrived(chains, arrays):
    for parts, array in zip(chains, arrays):
        for p in parts:
            p.terms[-1] = (array, *p.terms[-1][1:])


def double(array, axis, bit):
    return side_of(array, xor_permute(array, axis, bit), axis, bit)


def side_of(array, other, axis, bit):
    high = bit_of(axis, bit) == 1
    return jnp.concatenate([jnp.where(high, other, array), jnp.where(high, array, other)], axis=1)


def device_of(order):
    names = [b for axis in ("seq", "batch") for b in reversed(index_bits(axis))]
    last = len(names) - 1

    def device(shard):
        return sum((shard // (1 << (last - i))) % 2 * (1 << (last - names.index(b))) for i, b in enumerate(order))

    return device


def restored(gathered, order):
    names = [b for axis in ("seq", "batch") for b in reversed(index_bits(axis))]
    _, n, rows, width = gathered.shape
    cube = gathered.reshape([2] * len(names) + [n, rows, width])
    k = len(names)
    cube = cube.transpose([k] + [names.index(b) for b in order] + [k + 1, k + 2])
    return cube.reshape(n, -1, width).astype(f32)


def spread_body(half_steps, many, meta, *refs):
    sources, (kept_p, kept_q, other_p, other_q, up, out, into) = refs[: 3 * many], refs[3 * many :]
    width = out.shape[1]
    rows = out.shape[0] // many
    for j in range(many):
        first, b, c = sources[3 * j : 3 * j + 3]
        at = slice(j * rows, (j + 1) * rows)
        for i, source in enumerate((b[0, 0], b[0, 1], c[0, 0], c[0, 1])):
            up[at, i * width : (i + 1) * width] = source.astype(f32)
        out[at] = c[0, 2].astype(f32)
        into[at, :width] = first[0, 0].astype(f32)
    own = (pl.program_id(0) // half_steps) == lax.rem(meta[0], 2)
    for i, (kept, other) in enumerate(((kept_p, other_p), (kept_q, other_q))):
        value = jnp.where(own, kept[0].astype(f32), other[0].astype(f32))
        into[:, (i + 1) * width : (i + 2) * width] = value


def spread(meta, gathered, orders, kept, other):
    devices, stacked, rows, width = gathered.shape
    if rows % 8:
        half = width // 2
        high = lax.axis_index("seq") % 2 == 1
        x, y = (jnp.concatenate(p)[:, :half].astype(f32) for p in (kept, other))
        rest = jnp.concatenate([jnp.where(high, y, x), jnp.where(high, x, y)], axis=1)
        a = restored(gathered[:, 3:4], orders[0])
        b, c = restored(gathered[:, 4:], orders[1]), restored(gathered[:, :3], orders[2])
        return (jnp.concatenate([b[0], b[1], c[0], c[1]], axis=1), c[2],
                jnp.concatenate([a[0], rest[0], rest[1]], axis=1))
    places = [device_of(order) for order in orders]
    many = 4
    steps = devices // many
    half = steps // 2
    tall = many * rows
    piece = pl.BlockSpec((1, tall, width), lambda s: (0, s % half, 0))
    shape = jax.ShapeDtypeStruct
    sources = []
    for j in range(many):
        for size, block, place in ((1, 3, places[0]), (2, 2, places[1]), (3, 0, places[2])):
            sources.append(pl.BlockSpec(
                (1, size, rows, width), lambda s, i=block, p=place, j=j: (p(s * many + j), i, 0, 0)))
    return pl.pallas_call(
        partial(spread_body, half, many),
        grid=(steps,),
        in_specs=[SMEM, *sources, piece, piece, piece, piece],
        out_specs=[
            pl.BlockSpec((tall, 4 * width), lambda s: (s, 0)),
            pl.BlockSpec((tall, width), lambda s: (s, 0)),
            pl.BlockSpec((tall, 3 * width), lambda s: (s, 0)),
        ],
        out_shape=[shape((width, 4 * width), f32), shape((width, width), f32), shape((width, 3 * width), f32)],
        compiler_params=params(60),
        cost_estimate=cost(0, 6 * devices * stacked * rows * width),
        name="spread",
    )(meta, *[gathered] * (3 * many), *kept, *other)


def spread_down_body(half_steps, meta, kept_a, kept_b, other_a, other_b, target):
    own = (pl.program_id(0) // half_steps) == lax.rem(meta[0], 2)
    for first, kept, other in ((0, kept_a, other_a), (3, kept_b, other_b)):
        for j in range(kept.shape[0]):
            target[first + j] = jnp.where(own, kept[j].astype(f32), other[j].astype(f32))


def spread_down(meta, kept, other):
    _, half_rows, width = kept[0].shape
    rows = 96
    half = half_rows // rows
    piece = lambda n: pl.BlockSpec((n, rows, width), lambda s: (0, s % half, 0))
    return pl.pallas_call(
        partial(spread_down_body, half),
        grid=(2 * half,),
        in_specs=[SMEM, piece(3), piece(1), piece(3), piece(1)],
        out_specs=pl.BlockSpec((4, rows, width), lambda s: (0, s, 0)),
        out_shape=jax.ShapeDtypeStruct((4, 2 * half_rows, width), f32),
        compiler_params=params(48),
        cost_estimate=cost(0, 24 * width * width),
        name="spread_down",
    )(meta, *kept, *other).reshape(8 * half_rows, width)


def unpack_body(layout, meta, kept_p, kept_q, other_p, other_q, *refs):
    *targets, rows = refs
    core = lax.rem(meta[0], 2)
    for i, (kept, other) in enumerate(((kept_p, other_p), (kept_q, other_q))):
        rows[i] = jnp.where(core == 0, kept[0].astype(f32), other[0].astype(f32))
    for target, entry in zip(targets, layout):
        for (r, c), block, row, lane in entry:
            size, across = r.stop - r.start, c.stop - c.start
            part = rows[block, row : row + size, lane : lane + across]
            if len(target.shape) == 1:
                target[c] = part[0]
            else:
                target[r, c] = part


def unpack(meta, kept, other, layout, shapes):
    _, rows, width = kept[0].shape
    at = (rows - PACK) // PACK
    piece = pl.BlockSpec((1, PACK, width), lambda i: (0, at, 0))
    return pl.pallas_call(
        partial(unpack_body, layout),
        grid=(1,),
        in_specs=[SMEM, piece, piece, piece, piece],
        out_specs=[whole(s) for s in shapes],
        out_shape=[jax.ShapeDtypeStruct(s, f32) for s in shapes],
        scratch_shapes=[pltpu.VMEM((2, PACK, width), f32)],
        compiler_params=params(32),
        cost_estimate=cost(0, 2 << 20),
        name="unpack",
    )(meta, *kept, *other)


def shards(
    tokens, cotangent, lengths, norm1_gain, norm1_shift, in_weight, in_bias, conv_weight, conv_bias,
    filter_in, filter_in_bias, filter_mid, filter_mid_bias, filter_last, filter_last_bias, filter_out,
    decay_rate, skip_gain, out_weight, out_bias, norm2_gain, norm2_shift, up_weight, up_bias,
    down_weight, down_bias,
):
    buckets, rows, width = tokens.shape
    hidden_width = up_weight.shape[1]
    blocks = lax.axis_size("seq")
    devices = blocks * lax.axis_size("batch")
    count = buckets * rows
    meta = jnp.concatenate([lax.axis_index("seq")[None].astype(jnp.int32), lengths.astype(jnp.int32)])
    high_np, low_np = block_tables(rows)
    high, low = jnp.asarray(high_np), jnp.asarray(low_np)
    back = jnp.asarray(np.ascontiguousarray(high_np.T))
    line = lambda a: a.reshape(1, -1)

    halo = lax.ppermute(tokens[:, rows - HALO :], "seq", [(i, i + 1) for i in range(blocks - 1)])
    conv_w = conv_weight.reshape(3, 3, width)
    conv_b = conv_bias.reshape(3, width)
    normed, mixed, product, gate_out = front(
        meta, tokens, halo, line(norm1_gain), line(norm1_shift), in_weight, in_bias.reshape(3, width), conv_w, conv_b)
    far = exchange_far(product)
    table = jnp.asarray(features(rows * blocks, filter_in.shape[0]))
    sines, cosines = filter_layers(
        table, filter_in, filter_in_bias, filter_mid, filter_mid_bias, filter_last, filter_last_bias)
    hidden = sines[2]
    shaped, spectrum = filter_spectra(hidden, filter_out, line(decay_rate), high, low, blocks)
    far, spectrum = after(far, spectrum)
    products = exchange_near(far)
    mixture, gated = conv_forward(meta, products, spectrum, gate_out, line(skip_gain), high, back)

    flat = lambda a: a.reshape(count, width)
    (normed2, d_down, resid, active, d_up, g_up_bias, d_resid, d_mixer, d_gated, d_conv,
     g_norm2_gain, g_norm2_shift, g_out_bias) = middle(
        meta, flat(gated), out_weight, line(out_bias), flat(tokens), flat(cotangent), line(norm2_gain),
        line(norm2_shift), up_weight, line(up_bias), down_weight, flat(gate_out), buckets)
    cube = lambda a: a.reshape(buckets, rows, width)
    seq_bits, batch_bits = index_bits("seq"), index_bits("batch")
    core, far_seq, near_batch, far_batch = seq_bits[0], seq_bits[1:], batch_bits[:1], batch_bits[1:]
    orders = [near_batch + far_seq + far_batch, far_seq + far_batch + near_batch, far_batch + near_batch + far_seq]
    barrier = lax.optimization_barrier

    def wave(chains, at):
        return [halve(parts, *order[at]) for parts, order in zip(chains, orders)]

    far = exchange_far(cube(d_conv))
    first_kept, first_sent, g_first, *first_parts = short_backward(
        meta, (mixture, cube(d_gated)), mixed, normed, conv_w, conv_b)
    g_down_bias, *stacks = weight_grads(
        meta, active, d_up, normed2, d_down, flat(gated), d_mixer, first_kept, first_sent)
    kept, sent = stacks[:3], stacks[3:]
    far, sent, active = after(far, sent, active)
    block_out = layer_output(meta, active, down_weight, line(down_bias), resid, buckets)
    grads = exchange_near(far)
    come = [xor_permute(a, *core) for a in sent]
    come, grads, block_out = barrier((come, grads, block_out))
    stack = lambda k, c: Part([(k, 0, 0), (c, 0, 0)], k.shape[0], k.shape[1])
    chains = [[stack(k, c)] for k, c in zip(kept, come)]
    chains = wave(chains, 0)
    d_product, g_skip, lags = conv_backward(meta, grads, product, spectrum, line(skip_gain), high, back)

    come, d_product, lags = barrier((waiting(chains), d_product, lags))
    arrived(chains, come)
    chains = wave(chains, 1)
    in_kept, in_sent, g_mixed, *other_parts = short_backward(meta, (d_product,), mixed, normed, conv_w, conv_b)
    (g_filter_out, g_decay, g_filter_in, g_filter_in_bias, g_filter_mid, g_filter_mid_bias,
     g_filter_last, g_filter_last_bias) = filter_backward(
        lags, back, hidden.astype(bf16), filter_out.astype(bf16), line(decay_rate), shaped, table, sines, cosines,
        filter_mid, filter_last)

    come, in_sent, g_filter_out, g_mixed = barrier((waiting(chains), in_sent, g_filter_out, g_mixed))
    in_come = xor_permute(in_sent, *core)
    arrived(chains, come)
    chains = wave(chains, 2)
    shapes = [
        (width,), (width,), (3 * width,), (3, 3 * width), (3 * width,), filter_in.shape, filter_in_bias.shape,
        filter_mid.shape, filter_mid_bias.shape, filter_last.shape, filter_last_bias.shape, filter_out.shape,
        (width,), (width,), (width,), (width,), (width,), (hidden_width,), (width,),
    ]
    layout = pack_layout(width, shapes)
    smalls = [
        g_filter_in, g_filter_in_bias, g_filter_mid, g_filter_mid_bias, g_filter_last, g_filter_last_bias,
        g_filter_out, g_decay, g_skip, g_out_bias, g_norm2_gain, g_norm2_shift, g_up_bias, g_down_bias,
    ]
    g_tokens, d_halo, pack_kept, pack_sent = token_grads(
        meta, g_first, g_mixed, in_weight, tokens, halo, line(norm1_gain), cube(d_resid), first_parts + other_parts,
        smalls, layout)

    come, in_come, pack_sent = barrier((waiting(chains), in_come, pack_sent))
    arrived(chains, come)
    pack_come = xor_permute(pack_sent, *core)
    for at in range(3, len(orders[0])):
        chains = wave(chains, at)
    arriving = lax.ppermute(d_halo[:, HALO - 2 :], "seq", [(i + 1, i) for i in range(blocks - 1)])
    g_tokens = g_tokens.at[:, rows - 2 :].add(arriving)
    come, pack_come = barrier((waiting(chains), pack_come))
    arrived(chains, come)
    in_kept = jnp.concatenate([in_kept, pack_kept], axis=1)
    in_come = jnp.concatenate([in_come, pack_come], axis=1)
    whole_rows = in_kept.shape[1]
    order = orders[0]
    x, y, rest = near_batch[0], far_seq[0], far_seq[1:] + far_batch

    def in_sums():
        pair = [[Part([(in_kept, i, 0), (in_come, i, 0)], 1, whole_rows)] for i in range(2)]
        for steps in ((x, y), (y, x)):
            pair = [halve(parts, *step) for parts, step in zip(pair, steps)]
            arrived(pair, (yield waiting(pair)))
        joined = pair[0] + pair[1]
        for step in rest:
            joined = halve(joined, *step)
            arrived([joined], (yield waiting([joined])))
        done = jnp.concatenate([p.total(0, p.rows) for p in joined], axis=0)
        for step in reversed(rest):
            (come,) = yield [xor_permute(done, *step)]
            done = side_of(done, come, *step)
        pair = [done[:1], done[1:]]
        for steps in ((y, x), (x, y)):
            come = yield [xor_permute(a, *step) for a, step in zip(pair, steps)]
            pair = [side_of(a, c, *step) for a, c, step in zip(pair, come, steps)]
        come = yield [xor_permute(a, *core) for a in pair]
        return pair, come

    in_steps = in_sums()
    in_wait = next(in_steps)
    sums = [p.total(0, p.rows) for parts in chains for p in parts]
    both = jnp.concatenate([sums[2], sums[0][3:], sums[1][1:]], axis=0)
    gathered = lax.all_gather(both, ("seq", "batch"), axis=0)

    down = [sums[0][:3], sums[1][:1]]
    for steps in zip(reversed(orders[0]), reversed(orders[1])):
        down = [double(a, *step) for a, step in zip(down, steps)]
    grad_down_weight = spread_down(meta, down, [xor_permute(a, *core) for a in down])

    in_wait, g_tokens = barrier((in_wait, g_tokens))
    in_result, left = None, 2 * len(order) + 1
    while in_result is None:
        left -= 1
        if left == LAST_STEPS:
            in_wait, grad_down_weight = barrier((in_wait, grad_down_weight))
        try:
            in_wait = in_steps.send(in_wait)
        except StopIteration as end:
            in_result = end.value
    in_kept, in_come = in_result
    grad_up_weight, grad_out_weight, grad_in_weight = spread(
        meta, gathered, [[core, *o] for o in orders], in_kept, in_come)
    (n1g, n1s, inb, cw, cb, fi, fib, fm, fmb, fl, flb, fo, dr, sg, ob, n2g, n2s, ub, db) = unpack(
        meta, in_kept, in_come, layout, shapes)
    return (
        cube(block_out), g_tokens, n1g, n1s, grad_in_weight, inb, cw, cb, fi, fib, fm, fmb, fl, flb, fo, dr, sg,
        grad_out_weight, ob, n2g, n2s, grad_up_weight, ub, grad_down_weight, db,
    )


def solution(mesh):
    split = P("batch", "seq", None)
    return jax.shard_map(
        shards,
        mesh=mesh,
        in_specs=(split, split, P("batch")) + (P(),) * 23,
        out_specs=(split, split) + (P(),) * 23,
        check_vma=False,
    )
```

```python
from functools import partial
import math

import jax
import jax.numpy as jnp
import numpy as np
from jax import lax
from jax.experimental import pallas as pl
from jax.experimental.pallas import tpu as pltpu
from jax.sharding import PartitionSpec as P

norm_eps = 1e-05
window_floor = 0.05
highest = lax.Precision.HIGHEST
HALO = 16
CONV_TILE = 256
LAST_STEPS = 1
bf16 = jnp.bfloat16
f32 = jnp.float32


def dot(a, b, ca=1, cb=0, precision=None):
    return lax.dot_general(
        a, b, (((ca,), (cb,)), ((), ())), precision=precision, preferred_element_type=f32
    )


def xor_permute(array, axis, bit):
    count = lax.axis_size(axis)
    return lax.ppermute(array, axis, [(i, i ^ bit) for i in range(count)])


def exchange_far(array):
    held = {0: array}
    bit = lax.axis_size("seq") // 2
    while bit > 1:
        held.update({k ^ bit: xor_permute(a, "seq", bit) for k, a in list(held.items())})
        bit //= 2
    return held


def exchange_near(held):
    held = {**held, **{k ^ 1: xor_permute(a, "seq", 1) for k, a in held.items()}}
    return [held[k] for k in range(len(held))]


def after(held, *others):
    keys = [k for k in held if k]
    flat, others = lax.optimization_barrier(([held[k] for k in keys], others))
    return {**held, **dict(zip(keys, flat))}, *others


def block_tables(rows):
    phase = (2 * np.arange(rows)[:, None] + 1) * np.arange(rows)[None, :] % (4 * rows)
    angle = phase * (2.0 * math.pi / (4 * rows))
    table = np.concatenate([np.cos(angle), -np.sin(angle)], axis=0)
    high = table.astype(jnp.bfloat16)
    low = (table - high.astype(np.float64)).astype(jnp.bfloat16)
    return high, low


def features(seq_total, emb_width):
    bands = (emb_width - 1) // 2
    steps = np.arange(seq_total)
    phases = steps[:, None] * np.arange(1, bands + 1)[None, :] % seq_total
    angles = phases * (2.0 * math.pi / seq_total)
    ramp = steps / seq_total
    return np.concatenate([ramp[:, None], np.cos(angles), np.sin(angles)], axis=1).astype(np.float32)


def filter_layers(table, filter_in, in_bias, filter_mid, mid_bias, filter_last, last_bias):
    sines, cosines, value = [], [], table
    for weight, bias in ((filter_in, in_bias), (filter_mid, mid_bias), (filter_last, last_bias)):
        phase = jnp.dot(value, weight, precision=highest) + bias
        value = jnp.sin(phase)
        sines.append(value)
        cosines.append(jnp.cos(phase))
    return sines, cosines


def normalized(values):
    center = values - jnp.mean(values, axis=-1, keepdims=True)
    scale = lax.rsqrt(jnp.mean(center * center, axis=-1, keepdims=True) + norm_eps)
    return center * scale, scale


def live_rows(meta, bucket, rows):
    place = meta[0] * rows + lax.broadcasted_iota(jnp.int32, (rows, 1), 0)
    return (place < meta[1 + bucket]).astype(f32)


LIMIT = 0


def params(mib, count=1):
    return pltpu.CompilerParams(
        dimension_semantics=("arbitrary",) * count, vmem_limit_bytes=max(mib, LIMIT) * 1024 * 1024
    )


SMEM = pl.BlockSpec(memory_space=pltpu.SMEM)


def whole(shape):
    zeros = (0,) * len(shape)
    return pl.BlockSpec(tuple(shape), lambda *_: zeros)


def cost(flops, read):
    return pl.CostEstimate(flops=flops, bytes_accessed=read, transcendentals=0)


def front_body(buckets, rows, meta, tok, halo, gain, shift, w0, w1, w2, bias, cw, cb,
               normed, mixed, product, gate_out, taps_in):
    ext = rows + HALO

    @pl.when(pl.program_id(0) == 0)
    def _():
        for b in range(buckets):
            hat, _ = normalized(halo[b].astype(f32))
            normed[b * ext : b * ext + HALO] = (hat * gain[...] + shift[...]).astype(bf16)
            hat, _ = normalized(tok[b].astype(f32))
            normed[b * ext + HALO : (b + 1) * ext] = (hat * gain[...] + shift[...]).astype(bf16)

    inner = meta[0] > 0
    for b in range(buckets):
        parts = []
        for t, w in enumerate((w0, w1, w2)):
            m = (dot(normed[b * ext : (b + 1) * ext], w[...]) + bias[t : t + 1]).astype(bf16)
            head = jnp.where(inner, m[:HALO].astype(f32), 0.0)
            mixed[t, b, :HALO] = head.astype(bf16)
            mixed[t, b, HALO:] = m[HALO:]
            taps_in[t, :HALO] = head
            taps_in[t, HALO:] = m[HALO:].astype(f32)
            s = cb[t : t + 1]
            for i in range(3):
                s = s + cw[i, t : t + 1] * taps_in[t, HALO - 2 + i : HALO - 2 + i + rows]
            parts.append(s)
        gate_out[b] = parts[0]
        product[b] = (parts[2] * parts[1] * live_rows(meta, b, rows)).astype(bf16)


def front(meta, tok, halo, gain, shift, in_weight, in_bias, conv_weight, conv_bias):
    buckets, rows, width = tok.shape
    ext = rows + HALO
    tile = 256
    steps = width // tile
    columns = [pl.BlockSpec((width, tile), lambda c, t=t: (0, t * steps + c)) for t in range(3)]
    return pl.pallas_call(
        partial(front_body, buckets, rows),
        grid=(steps,),
        in_specs=[
            SMEM, whole(tok.shape), whole(halo.shape), whole((1, width)), whole((1, width)), *columns,
            pl.BlockSpec((3, tile), lambda c: (0, c)),
            pl.BlockSpec((3, 3, tile), lambda c: (0, 0, c)),
            pl.BlockSpec((3, tile), lambda c: (0, c)),
        ],
        out_specs=[
            whole((buckets * ext, width)),
            pl.BlockSpec((3, buckets, ext, tile), lambda c: (0, 0, 0, c)),
            pl.BlockSpec((buckets, rows, tile), lambda c: (0, 0, c)),
            pl.BlockSpec((buckets, rows, tile), lambda c: (0, 0, c)),
        ],
        out_shape=[
            jax.ShapeDtypeStruct((buckets * ext, width), bf16),
            jax.ShapeDtypeStruct((3, buckets, ext, width), bf16),
            jax.ShapeDtypeStruct((buckets, rows, width), bf16),
            jax.ShapeDtypeStruct((buckets, rows, width), f32),
        ],
        scratch_shapes=[pltpu.VMEM((3, ext, tile), f32)],
        compiler_params=params(48),
        cost_estimate=cost(6 * buckets * ext * width * width, 16 << 20),
        name="front",
    )(meta, tok, halo, gain, shift, in_weight, in_weight, in_weight, in_bias, conv_weight, conv_bias)


def alternating(rows):
    parity = lax.broadcasted_iota(jnp.int32, (rows, 1), 0) % 2
    return (1 - 2 * parity).astype(f32)


def window_of(first, rows, total, decay):
    ramp = (first + lax.broadcasted_iota(jnp.int32, (rows, 1), 0)).astype(f32) * (1.0 / total)
    return ramp, jnp.exp(-ramp * decay)


def filter_body(blocks, rows, hidden, out, decay, high, low, shaped, spectrum):
    sign = alternating(rows)
    last = None
    for m in range(blocks):
        here = slice(m * rows, (m + 1) * rows)
        plain = dot(hidden[here], out[...], precision=highest)
        shaped[here] = plain
        _, fall = window_of(m * rows, rows, blocks * rows, decay[...])
        taps = plain * (fall + window_floor)
        upper = taps.astype(bf16)
        rest = (taps - upper.astype(f32)).astype(bf16)
        full = dot(high[...], upper) + (dot(high[...], rest) + dot(low[...], upper))
        re, im = full[:rows], full[rows:]
        if last is None:
            spectrum[m, :rows] = re
            spectrum[m, rows:] = im
        else:
            spectrum[m, :rows] = re - sign * last[1]
            spectrum[m, rows:] = im + sign * last[0]
        last = (re, im)
    spectrum[blocks] = jnp.zeros(spectrum.shape[1:], f32)


def filter_spectra(hidden, filter_out, decay, high, low, blocks):
    total, inner = hidden.shape
    width = filter_out.shape[1]
    rows = total // blocks
    tile = 256
    return pl.pallas_call(
        partial(filter_body, blocks, rows),
        grid=(width // tile,),
        in_specs=[
            whole(hidden.shape),
            pl.BlockSpec((inner, tile), lambda c: (0, c)),
            pl.BlockSpec((1, tile), lambda c: (0, c)),
            whole(high.shape), whole(low.shape),
        ],
        out_specs=[
            pl.BlockSpec((total, tile), lambda c: (0, c)),
            pl.BlockSpec((blocks + 1, 2 * rows, tile), lambda c: (0, 0, c)),
        ],
        out_shape=[
            jax.ShapeDtypeStruct((total, width), f32),
            jax.ShapeDtypeStruct((blocks + 1, 2 * rows, width), f32),
        ],
        compiler_params=params(48),
        cost_estimate=cost(20 * total * width * rows, 10 << 20),
        name="filter_spectra",
    )(hidden, filter_out, decay, high, low)


def conv_body(blocks, rows, meta, *refs):
    products = refs[:blocks]
    spectrum, gate_out, skip, high, back, mixture, gated = refs[blocks:]
    own = meta[0]
    for c in range(products[0].shape[2] // CONV_TILE):
        at = slice(c * CONV_TILE, (c + 1) * CONV_TILE)
        sum_re = sum_im = None
        for k in range(blocks):
            lag = own - (own ^ k)
            lag = jnp.where(lag < 0, blocks, lag)
            full = dot(high[...], products[k][0, :, at])
            re, im = full[:rows], full[rows:]
            tap_re, tap_im = spectrum[lag, :rows, at], spectrum[lag, rows:, at]
            out_re = tap_re * re - tap_im * im
            out_im = tap_re * im + tap_im * re
            sum_re = out_re if sum_re is None else sum_re + out_re
            sum_im = out_im if sum_im is None else sum_im + out_im
        convolved = dot(back[:, :rows], sum_re.astype(bf16)) + dot(back[:, rows:], sum_im.astype(bf16))
        mixed = convolved * (1.0 / rows) + skip[:, at] * products[0][0, :, at].astype(f32)
        mixture[0, :, at] = mixed
        gated[0, :, at] = (mixed * gate_out[0, :, at]).astype(bf16)


def conv_forward(meta, products, spectrum, gate_out, skip, high, back):
    buckets, rows, width = gate_out.shape
    blocks = len(products)
    tile = width
    piece = pl.BlockSpec((1, rows, tile), lambda c, b: (b, 0, c))
    return pl.pallas_call(
        partial(conv_body, blocks, rows),
        grid=(width // tile, buckets),
        in_specs=[SMEM] + [piece] * blocks + [
            pl.BlockSpec((blocks + 1, 2 * rows, tile), lambda c, b: (0, 0, c)), piece,
            pl.BlockSpec((1, tile), lambda c, b: (0, c)), whole(high.shape), whole(back.shape),
        ],
        out_specs=[piece, piece],
        out_shape=[
            jax.ShapeDtypeStruct((buckets, rows, width), f32),
            jax.ShapeDtypeStruct((buckets, rows, width), bf16),
        ],
        compiler_params=params(56, 2),
        cost_estimate=cost(4 * (blocks + 1) * rows * rows * width * buckets, 16 << 20),
        name="conv_forward",
    )(meta, *products, spectrum, gate_out, skip, high, back)


def gelu_parts(u):
    cdf = 0.5 + 0.5 * lax.erf(u * (1.0 / math.sqrt(2.0)))
    pdf = jnp.exp(-0.5 * u * u) * (1.0 / math.sqrt(2.0 * math.pi))
    return u * cdf, cdf + u * pdf


def middle_body(buckets, rows, steps, meta, gated, out_w, out_b, tok, cot, gain, shift, up_w, up_b, down_w,
                gate_out, normed2, d_down, resid, active, d_up, g_up_bias, d_resid, d_mixer, d_gated, d_conv,
                g_gain, g_shift, g_out_bias, total):
    step = pl.program_id(0)

    @pl.when(step == 0)
    def _():
        for b in range(buckets):
            here = slice(b * rows, (b + 1) * rows)
            live = live_rows(meta, b, rows)
            mixer = dot(gated[here], out_w[...]) + out_b[...]
            r = tok[here].astype(f32) + live * mixer
            resid[here] = r
            hat, _ = normalized(r)
            normed2[here] = (hat * gain[...] + shift[...]).astype(bf16)
            d_down[here] = (live * cot[here].astype(f32)).astype(bf16)
            total[here] = jnp.zeros_like(total[here])

    bias_sum = None
    for b in range(buckets):
        here = slice(b * rows, (b + 1) * rows)
        u = dot(normed2[here], up_w[...]) + up_b[...]
        d_active = dot(d_down[here], down_w[...], 1, 1)
        act, slope = gelu_parts(u)
        active[here] = act.astype(bf16)
        d_u = (d_active * slope).astype(bf16)
        d_up[here] = d_u
        part = jnp.sum(d_u.astype(f32), axis=0, keepdims=True)
        bias_sum = part if bias_sum is None else bias_sum + part
        back = dot(d_u, up_w[...], 1, 1)

        total[here] += back

    g_up_bias[...] = bias_sum

    @pl.when(step == steps - 1)
    def _():
        sums = [jnp.zeros((1, gain.shape[1]), f32)] * 3
        for b in range(buckets):
            here = slice(b * rows, (b + 1) * rows)
            live = live_rows(meta, b, rows)
            hat, scale = normalized(resid[here])
            d = total[here]
            sums[0] = sums[0] + jnp.sum(d * hat, axis=0, keepdims=True)
            sums[1] = sums[1] + jnp.sum(d, axis=0, keepdims=True)
            e = d * gain[...]
            mean_e = jnp.mean(e, axis=-1, keepdims=True)
            mean_eh = jnp.mean(e * hat, axis=-1, keepdims=True)
            d_r = cot[here].astype(f32) + (e - mean_e - hat * mean_eh) * scale
            d_resid[here] = d_r
            d_m = (live * d_r).astype(bf16)
            d_mixer[here] = d_m
            sums[2] = sums[2] + jnp.sum(d_m.astype(f32), axis=0, keepdims=True)
            d_g = dot(d_m, out_w[...], 1, 1)
            d_gated[here] = d_g
            d_conv[here] = (d_g * gate_out[here]).astype(bf16)
        g_gain[...] = sums[0]
        g_shift[...] = sums[1]
        g_out_bias[...] = sums[2]


def middle(meta, gated, out_w, out_b, tok, cot, gain, shift, up_w, up_b, down_w, gate_out, buckets):
    count, width = tok.shape
    hidden = up_w.shape[1]
    tile = width
    steps = hidden // tile
    rows = count // buckets
    square = whole((count, width))
    line = whole((1, width))
    shape = jax.ShapeDtypeStruct
    return pl.pallas_call(
        partial(middle_body, buckets, rows, steps),
        grid=(steps,),
        in_specs=[
            SMEM, square, whole(out_w.shape), line, square, square, line, line,
            pl.BlockSpec((width, tile), lambda s: (0, s)),
            pl.BlockSpec((1, tile), lambda s: (0, s)),
            pl.BlockSpec((tile, width), lambda s: (s, 0)),
            square,
        ],
        out_specs=[
            square, square, square,
            pl.BlockSpec((count, tile), lambda s: (0, s)),
            pl.BlockSpec((count, tile), lambda s: (0, s)),
            pl.BlockSpec((1, tile), lambda s: (0, s)),
            square, square, square, square, line, line, line,
        ],
        out_shape=[
            shape((count, width), bf16), shape((count, width), bf16), shape((count, width), f32),
            shape((count, hidden), bf16), shape((count, hidden), bf16), shape((1, hidden), f32),
            shape((count, width), f32), shape((count, width), bf16), shape((count, width), f32),
            shape((count, width), bf16), shape((1, width), f32), shape((1, width), f32), shape((1, width), f32),
        ],
        scratch_shapes=[pltpu.VMEM((count, width), f32)],
        compiler_params=params(56),
        cost_estimate=cost(6 * count * width * hidden, 40 << 20),
        name="middle",
    )(meta, gated, out_w, out_b, tok, cot, gain, shift, up_w, up_b, down_w, gate_out)


def own_half(core, width, mine):
    half = width // 2
    return pl.ds(pl.multiple_of((core if mine else 1 - core) * half, half), half)


def weights_body(steps, meta, active, d_up, normed2, d_down, gated, d_mixer, first_kept, first_sent, g_bias, *stacks):
    del first_kept, first_sent
    kept, sent = stacks[:3], stacks[3:]
    step = pl.program_id(0)
    core = lax.rem(meta[0], 2)
    width = normed2.shape[1]
    mine, theirs = own_half(core, width, True), own_half(core, width, False)

    @pl.when(step < steps)
    def _():
        down = [dot(active[:, at], d_down[...], 0, 0).astype(bf16) for at in (mine, theirs)]
        up = [dot(normed2[:, at], d_up[...], 0, 0).astype(bf16) for at in (mine, theirs)]
        for first, stop, source, stack in ((0, 3, down, 0), (3, 4, down, 1), (0, 2, up, 1), (2, 4, up, 2)):

            @pl.when((step >= first) & (step < stop))
            def _(source=source, stack=stack):
                kept[stack][0] = source[0]
                sent[stack][0] = source[1]

    @pl.when(step == steps)
    def _():
        kept[2][0] = dot(gated[:, mine], d_mixer[...], 0, 0).astype(bf16)
        sent[2][0] = dot(gated[:, theirs], d_mixer[...], 0, 0).astype(bf16)
        g_bias[...] = jnp.sum(d_down[...].astype(f32), axis=0, keepdims=True)


def weight_grads(meta, active, d_up, normed2, d_down, gated, d_mixer, first_kept, first_sent):
    count, width = normed2.shape
    hidden = active.shape[1]
    steps = hidden // width
    assert steps == 4
    square = whole((count, width))
    shape = jax.ShapeDtypeStruct
    last = steps - 1
    columns = pl.BlockSpec((count, width), lambda s: (0, jnp.minimum(s, last)))
    half = (1, width // 2, width)
    stacks = [
        pl.BlockSpec(half, lambda s: (jnp.minimum(s, 2), 0, 0)),
        pl.BlockSpec(half, lambda s: (jnp.where(s > 2, 0, jnp.minimum(s + 1, 2)), 0, 0)),
        pl.BlockSpec(half, lambda s: (jnp.maximum(s - 2, 0), 0, 0)),
    ]
    return pl.pallas_call(
        partial(weights_body, steps),
        grid=(steps + 1,),
        in_specs=[SMEM, columns, columns, square, square, square, square] + [pl.BlockSpec(memory_space=pl.ANY)] * 2,
        out_specs=[whole((1, width)), *stacks, *stacks],
        out_shape=[shape((1, width), f32)] + [shape((n, width // 2, width), bf16) for n in (4, 3, 3)] * 2,
        input_output_aliases={7: 1, 8: 4},
        compiler_params=params(56),
        cost_estimate=cost(4 * count * width * hidden, 40 << 20),
        name="weight_grads",
    )(meta, active, d_up, normed2, d_down, gated, d_mixer, first_kept, first_sent)


def output_body(buckets, rows, steps, meta, active, down_w, down_b, resid, block_out, total):
    step = pl.program_id(0)

    @pl.when(step == 0)
    def _():
        total[...] = dot(active[...], down_w[...])

    @pl.when(step > 0)
    def _():
        total[...] += dot(active[...], down_w[...])

    @pl.when(step == steps - 1)
    def _():
        for b in range(buckets):
            here = slice(b * rows, (b + 1) * rows)
            live = live_rows(meta, b, rows)
            block_out[here] = (resid[here] + live * (total[here] + down_b[...])).astype(bf16)


def layer_output(meta, active, down_w, down_b, resid, buckets):
    count, width = resid.shape
    hidden = down_w.shape[0]
    steps = hidden // width
    return pl.pallas_call(
        partial(output_body, buckets, count // buckets, steps),
        grid=(steps,),
        in_specs=[
            SMEM, pl.BlockSpec((count, width), lambda s: (0, s)), pl.BlockSpec((width, width), lambda s: (s, 0)),
            whole((1, width)), whole((count, width)),
        ],
        out_specs=whole((count, width)),
        out_shape=jax.ShapeDtypeStruct((count, width), bf16),
        scratch_shapes=[pltpu.VMEM((count, width), f32)],
        compiler_params=params(48),
        cost_estimate=cost(2 * count * width * hidden, 14 << 20),
        name="layer_output",
    )(meta, active, down_w, down_b, resid)


def conv_back_body(blocks, rows, buckets, meta, *refs):
    grads = refs[:blocks]
    product, spectrum, skip, high, back, d_product, g_skip, g_lags, lags = refs[blocks:]
    own = meta[0]
    b = pl.program_id(1)

    @pl.when(b == 0)
    def _():
        lags[...] = jnp.zeros_like(lags)
        g_skip[...] = jnp.zeros_like(g_skip)

    full = dot(high[...], product[0])
    prod_re, prod_im = full[:rows], full[rows:]
    sum_re = sum_im = None
    for k in range(blocks):
        lag = (own ^ k) - own
        lag = jnp.where(lag < 0, blocks, lag)
        grad = dot(high[...], grads[k][0])
        re, im = grad[:rows], grad[rows:]
        tap_re, tap_im = spectrum[lag, :rows], spectrum[lag, rows:]
        out_re = tap_re * re + tap_im * im
        out_im = tap_re * im - tap_im * re
        sum_re = out_re if sum_re is None else sum_re + out_re
        sum_im = out_im if sum_im is None else sum_im + out_im
        lags[lag, :rows] += re * prod_re + im * prod_im
        lags[lag, rows:] += im * prod_re - re * prod_im
    d_own = grads[0][0].astype(f32)
    full = dot(back[:, :rows], sum_re.astype(bf16)) + dot(back[:, rows:], sum_im.astype(bf16))
    d_product[0] = full * (1.0 / rows) + skip[...] * d_own
    g_skip[...] += jnp.sum(d_own * product[0].astype(f32), axis=0, keepdims=True)

    @pl.when(b == buckets - 1)
    def _():
        g_lags[...] = lags[:blocks].astype(bf16)


def conv_backward(meta, grads, product, spectrum, skip, high, back):
    buckets, rows, width = product.shape
    blocks = len(grads)
    tile = CONV_TILE
    piece = pl.BlockSpec((1, rows, tile), lambda c, b: (b, 0, c))
    line = pl.BlockSpec((1, tile), lambda c, b: (0, c))
    shape = jax.ShapeDtypeStruct
    return pl.pallas_call(
        partial(conv_back_body, blocks, rows, buckets),
        grid=(width // tile, buckets),
        in_specs=[SMEM] + [piece] * blocks + [
            piece, pl.BlockSpec((blocks + 1, 2 * rows, tile), lambda c, b: (0, 0, c)), line, whole(high.shape),
            whole(back.shape),
        ],
        out_specs=[piece, line, pl.BlockSpec((blocks, 2 * rows, tile), lambda c, b: (0, 0, c))],
        out_shape=[shape((buckets, rows, width), f32), shape((1, width), f32), shape((blocks, 2 * rows, width), bf16)],
        scratch_shapes=[pltpu.VMEM((blocks + 1, 2 * rows, tile), f32)],
        compiler_params=params(60, 2),
        cost_estimate=cost(4 * (2 * blocks + 2) * rows * rows * width * buckets, 20 << 20),
        name="conv_backward",
    )(meta, *grads, product, spectrum, skip, high, back)


def filter_back_body(blocks, rows, tile, lags, back, hidden, filter_out, decay, shaped, table, sin_a, sin_b, cos_a, cos_b,
                     cos_c, filter_mid, filter_last, g_filter_out, g_decay, g_in, g_in_bias, g_mid, g_mid_bias,
                     g_last, g_last_bias, g_hidden):
    sign = alternating(rows)
    for c in range(decay.shape[1] // tile):
        at = slice(c * tile, (c + 1) * tile)
        sum_out = sum_decay = None
        for m in range(blocks):
            here = slice(m * rows, (m + 1) * rows)
            re, im = lags[m, :rows, at].astype(f32), lags[m, rows:, at].astype(f32)
            if m + 1 < blocks:
                re = re + sign * lags[m + 1, rows:, at].astype(f32)
                im = im - sign * lags[m + 1, :rows, at].astype(f32)
            d_taps = dot(back[:, :rows], re.astype(bf16)) + dot(back[:, rows:], im.astype(bf16))
            d_taps = d_taps * (1.0 / rows)
            ramp, fall = window_of(m * rows, rows, blocks * rows, decay[:, at])
            g_d = -jnp.sum(d_taps * shaped[here, at] * ramp * fall, axis=0, keepdims=True)
            d_shaped = (d_taps * (fall + window_floor)).astype(bf16)
            g_o = dot(hidden[here], d_shaped, 0, 0)
            sum_out = g_o if sum_out is None else sum_out + g_o
            sum_decay = g_d if sum_decay is None else sum_decay + g_d
            d_hidden = dot(d_shaped, filter_out[:, at], 1, 1)
            g_hidden[here] = d_hidden if c == 0 else g_hidden[here] + d_hidden
        g_filter_out[:, at] = sum_out
        g_decay[:, at] = sum_decay
    d_c = g_hidden[...] * cos_c[...]
    g_last_bias[...] = jnp.sum(d_c, axis=0, keepdims=True)
    d_c = d_c.astype(bf16)
    g_last[...] = dot(sin_b[...].astype(bf16), d_c, 0, 0)
    d_b = dot(d_c, filter_last[...].astype(bf16), 1, 1) * cos_b[...]
    g_mid_bias[...] = jnp.sum(d_b, axis=0, keepdims=True)
    d_b = d_b.astype(bf16)
    g_mid[...] = dot(sin_a[...].astype(bf16), d_b, 0, 0)
    d_a = dot(d_b, filter_mid[...].astype(bf16), 1, 1) * cos_a[...]
    g_in[...] = dot(table[...].astype(bf16), d_a.astype(bf16), 0, 0)
    g_in_bias[...] = jnp.sum(d_a, axis=0, keepdims=True)


def filter_backward(lags, back, hidden, filter_out, decay, shaped, table, sines, cosines, filter_mid, filter_last):
    blocks, double_rows, width = lags.shape
    total, inner = hidden.shape
    shape = jax.ShapeDtypeStruct
    outs = [shape((inner, width), f32), shape((1, width), f32),
            shape((table.shape[1], inner), f32), shape((1, inner), f32), shape((inner, inner), f32),
            shape((1, inner), f32), shape((inner, inner), f32), shape((1, inner), f32)]
    arrays = [lags, back, hidden, filter_out, decay, shaped, table, sines[0], sines[1], *cosines, filter_mid, filter_last]
    return pl.pallas_call(
        partial(filter_back_body, blocks, double_rows // 2, 256),
        grid=(1,),
        in_specs=[whole(a.shape) for a in arrays],
        out_specs=[whole(a.shape) for a in outs],
        out_shape=outs,
        scratch_shapes=[pltpu.VMEM((total, inner), f32)],
        compiler_params=params(56),
        cost_estimate=cost(10 * total * width * double_rows, 10 << 20),
        name="filter_backward",
    )(*arrays)


PACK = 128


def pack_layout(width, shapes):
    out, narrow, row = [], 0, [64, 64]
    for shape in shapes:
        r, c = (1, shape[0]) if len(shape) == 1 else shape
        if c < width:
            out.append([((slice(0, r), slice(0, c)), 0, 0, narrow)])
            narrow += 128
        elif r > 32:
            out.append([((slice(0, r), slice(0, c)), 1, 0, 0)])
        else:
            entry = []
            for j in range(c // width):
                block = 0 if row[0] + r <= PACK else 1
                entry.append(((slice(0, r), slice(j * width, (j + 1) * width)), block, row[block], 0))
                row[block] += r
            out.append(entry)
    assert max(row) <= PACK and narrow <= width
    return out


def short_back_body(buckets, rows, first, meta, *refs):
    count = 1 if first else 2
    if first:
        mixture, d_gated, *refs = refs
    else:
        d_product, *refs = refs
    mixed, refs = refs[:count], refs[count:]
    normed, cw, cb, kept, sent, g_mixed, g_conv, g_conv_bias, g_bias, taps_in, d_pad = refs
    ext = rows + HALO
    inner = meta[0] > 0
    core = lax.rem(meta[0], 2)
    tile = cb.shape[1]
    width = normed.shape[1]
    sums = [[jnp.zeros((1, tile), f32)] * 5 for _ in range(count)]
    for b in range(buckets):
        short = []
        for t in range(count):
            k = t if first else t + 1
            taps_in[t] = mixed[t][0, b].astype(f32)
            s = cb[k : k + 1]
            if not first:
                for i in range(3):
                    s = s + cw[i, k : k + 1] * taps_in[t, HALO - 2 + i : HALO - 2 + i + rows]
            short.append(s)
        if first:
            d_shorts = (d_gated[b] * mixture[b],)
        else:
            d_prod = d_product[b] * live_rows(meta, b, rows)
            d_shorts = (d_prod * short[1], d_prod * short[0])
        for t in range(count):
            k = t if first else t + 1
            d_short = d_shorts[t]
            d_pad[t, :HALO] = jnp.zeros((HALO, tile), f32)
            d_pad[t, HALO : HALO + rows] = d_short
            d_pad[t, HALO + rows :] = jnp.zeros((8, tile), f32)
            for i in range(3):
                sums[t][i] = sums[t][i] + jnp.sum(
                    d_short * taps_in[t, HALO - 2 + i : HALO - 2 + i + rows], axis=0, keepdims=True)
            sums[t][3] = sums[t][3] + jnp.sum(d_short, axis=0, keepdims=True)
            g = (cw[2, k : k + 1] * d_pad[t, :ext] + cw[1, k : k + 1] * d_pad[t, 1 : ext + 1]
                 + cw[0, k : k + 1] * d_pad[t, 2 : ext + 2])
            head = jnp.where(inner, g[:HALO], 0.0).astype(bf16)
            body = g[HALO:].astype(bf16)
            g_mixed[t, b * ext : b * ext + HALO] = head
            g_mixed[t, b * ext + HALO : (b + 1) * ext] = body
            sums[t][4] = sums[t][4] + (jnp.sum(head.astype(f32), axis=0, keepdims=True)
                                       + jnp.sum(body.astype(f32), axis=0, keepdims=True))
    for t in range(count):
        for i in range(3):
            g_conv[i, t : t + 1] = sums[t][i]
        g_conv_bias[t : t + 1] = sums[t][3]
        g_bias[t : t + 1] = sums[t][4]
        kept[t] = dot(normed[:, own_half(core, width, True)], g_mixed[t], 0, 0).astype(bf16)
        sent[t] = dot(normed[:, own_half(core, width, False)], g_mixed[t], 0, 0).astype(bf16)


def short_backward(meta, sources, mixed, normed, conv_weight, conv_bias):
    _, buckets, ext, width = mixed.shape
    rows = ext - HALO
    tile = 256
    first = len(sources) == 2
    count = 1 if first else 2
    piece = pl.BlockSpec((buckets, rows, tile), lambda c: (0, 0, c))
    columns = [pl.BlockSpec((1, buckets, ext, tile), lambda c, t=t: (t, 0, 0, c)) for t in ([0] if first else [1, 2])]
    three = pl.BlockSpec((3, tile), lambda c: (0, c))
    nine = pl.BlockSpec((3, 3, tile), lambda c: (0, 0, c))
    line = pl.BlockSpec((count, tile), lambda c: (0, c))
    half = pl.BlockSpec((count, width // 2, tile), lambda c: (3 if first else 0, 0, c))
    halves = (4, width // 2, width) if first else (2, width // 2 + PACK, width)
    shape = jax.ShapeDtypeStruct
    return pl.pallas_call(
        partial(short_back_body, buckets, rows, first),
        grid=(width // tile,),
        in_specs=[SMEM, *[piece] * len(sources), *columns, whole(normed.shape), nine, three],
        out_specs=[
            half, half, pl.BlockSpec((count, buckets * ext, tile), lambda c: (0, 0, c)),
            pl.BlockSpec((3, count, tile), lambda c: (0, 0, c)), line, line,
        ],
        out_shape=[
            shape(halves, bf16), shape(halves, bf16),
            shape((count, buckets * ext, width), bf16), shape((3, count, width), f32), shape((count, width), f32),
            shape((count, width), f32),
        ],
        scratch_shapes=[pltpu.VMEM((count, ext, tile), f32), pltpu.VMEM((count, ext + 8, tile), f32)],
        compiler_params=params(56),
        cost_estimate=cost(2 * count * buckets * ext * width * width, 10 << 20),
        name="short_backward",
    )(meta, *sources, *[mixed] * count, normed, conv_weight, conv_bias)


def token_body(buckets, rows, layout, others, meta, g_first, g_mixed, weight, tok, halo, gain, d_resid, *refs):
    parts, refs = refs[:6], refs[6:]
    smalls, (_, _, g_tokens, d_halo, kept, sent, total, pack) = refs[:others], refs[others:]
    ext = rows + HALO
    step = pl.program_id(0)
    core = lax.rem(meta[0], 2)

    @pl.when(step == 0)
    def _():
        total[...] = dot(g_first[0], weight[...], 1, 1)

    @pl.when(step > 0)
    def _():
        total[...] += dot(g_mixed[0], weight[...], 1, 1)

    @pl.when(step == 2)
    def _():
        add = [jnp.zeros((1, gain.shape[1]), f32)] * 2
        for b in range(buckets):
            for first, size, source in ((0, HALO, halo), (HALO, rows, tok)):
                d = total[b * ext + first : b * ext + first + size]
                hat, scale = normalized(source[b].astype(f32))
                add[0] = add[0] + jnp.sum(d * hat, axis=0, keepdims=True)
                add[1] = add[1] + jnp.sum(d, axis=0, keepdims=True)
                e = d * gain[...]
                mean_e = jnp.mean(e, axis=-1, keepdims=True)
                mean_eh = jnp.mean(e * hat, axis=-1, keepdims=True)
                d_v = (e - mean_e - hat * mean_eh) * scale
                if first:
                    g_tokens[b] = d_resid[b] + d_v
                else:
                    d_halo[b] = d_v
        pack[...] = jnp.zeros_like(pack)
        for source, entry in zip(add, layout[:2]):
            (_, block, row, _), = entry
            pack[block, row : row + 1] = source
        conv, conv_bias, bias = parts[0::3], parts[1::3], parts[2::3]
        for j in range(3):
            p, q = (0, 0) if j == 0 else (1, j - 1)
            _, block, row, _ = layout[2][j]
            pack[block, row : row + 1] = bias[p][q : q + 1]
            _, block, row, _ = layout[4][j]
            pack[block, row : row + 1] = conv_bias[p][q : q + 1]
            _, block, row, _ = layout[3][j]
            for i in range(3):
                pack[block, row + i : row + i + 1] = conv[p][i, q : q + 1]
        for source, entry in zip(smalls, layout[5:]):
            for (r, c), block, row, lane in entry:
                pack[block, row : row + r.stop - r.start, lane : lane + c.stop - c.start] = source[r, c]
        kept[...] = jnp.where(core == 0, pack[...], 0.0).astype(bf16)
        sent[...] = jnp.where(core == 0, 0.0, pack[...]).astype(bf16)


def token_grads(meta, g_first, g_mixed, in_weight, tok, halo, gain, d_resid, parts, smalls, layout, in_kept, in_sent):
    buckets, rows, width = tok.shape
    ext = rows + HALO
    shape = jax.ShapeDtypeStruct
    packed = (2, PACK, width)
    arrays = [tok, halo, gain, d_resid, *parts, *smalls]
    last = pl.BlockSpec(packed, lambda t: (0, (width // 2) // PACK, 0))
    return pl.pallas_call(
        partial(token_body, buckets, rows, layout, len(smalls)),
        grid=(3,),
        in_specs=[
            SMEM, whole(g_first.shape), pl.BlockSpec((1, buckets * ext, width), lambda t: (jnp.maximum(t - 1, 0), 0, 0)),
            pl.BlockSpec((width, width), lambda t: (0, t)), *[whole(a.shape) for a in arrays],
            *[pl.BlockSpec(memory_space=pl.ANY)] * 2,
        ],
        out_specs=[whole(tok.shape), whole(halo.shape), last, last],
        out_shape=[shape(tok.shape, f32), shape(halo.shape, f32), shape(in_kept.shape, bf16), shape(in_sent.shape, bf16)],
        input_output_aliases={4 + len(arrays): 2, 5 + len(arrays): 3},
        scratch_shapes=[pltpu.VMEM((buckets * ext, width), f32), pltpu.VMEM(packed, f32)],
        compiler_params=params(56),
        cost_estimate=cost(6 * buckets * ext * width * width, 30 << 20),
        name="token_grads",
    )(meta, g_first, g_mixed, in_weight, *arrays, in_kept, in_sent)


def index_bits(axis):
    count = lax.axis_size(axis)
    return [(axis, 1 << i) for i in range(count.bit_length() - 1)]


def bit_of(axis, bit):
    return (lax.axis_index(axis) // bit) % 2


class Part:
    def __init__(self, terms, blocks, rows):
        self.terms, self.blocks, self.rows = terms, blocks, rows

    def total(self, first, rows):
        value = None
        for array, block, row in self.terms:
            term = lax.dynamic_slice(array, (block, row + first, 0), (self.blocks, rows, array.shape[2])).astype(f32)
            value = term if value is None else value + term
        return value.astype(bf16)


def halve(parts, axis, bit):
    mine = bit_of(axis, bit)
    halves = [p.rows // 2 for p in parts]
    sent = [p.total((1 - mine) * h, h) for p, h in zip(parts, halves)]
    come = xor_permute(sent[0] if len(sent) == 1 else jnp.concatenate(sent, axis=0), axis, bit)
    out, block = [], 0
    for p, h in zip(parts, halves):
        terms = [(array, at, row + mine * h) for array, at, row in p.terms]
        out.append(Part(terms + [(come, block, 0)], p.blocks, h))
        block += p.blocks
    return out


def waiting(chains):
    return [parts[0].terms[-1][0] for parts in chains]


def arrived(chains, arrays):
    for parts, array in zip(chains, arrays):
        for p in parts:
            p.terms[-1] = (array, *p.terms[-1][1:])


def double(array, axis, bit):
    return side_of(array, xor_permute(array, axis, bit), axis, bit)


def side_of(array, other, axis, bit):
    high = bit_of(axis, bit) == 1
    return jnp.concatenate([jnp.where(high, other, array), jnp.where(high, array, other)], axis=1)


def device_of(order):
    names = [b for axis in ("seq", "batch") for b in reversed(index_bits(axis))]
    last = len(names) - 1

    def device(shard):
        return sum((shard // (1 << (last - i))) % 2 * (1 << (last - names.index(b))) for i, b in enumerate(order))

    return device


def restored(gathered, order):
    names = [b for axis in ("seq", "batch") for b in reversed(index_bits(axis))]
    _, n, rows, width = gathered.shape
    cube = gathered.reshape([2] * len(names) + [n, rows, width])
    k = len(names)
    cube = cube.transpose([k] + [names.index(b) for b in order] + [k + 1, k + 2])
    return cube.reshape(n, -1, width).astype(f32)


def spread_body(half_steps, many, meta, *refs):
    sources, (kept_p, kept_q, other_p, other_q, up, out, into) = refs[: 3 * many], refs[3 * many :]
    width = out.shape[1]
    rows = out.shape[0] // many
    for j in range(many):
        first, b, c = sources[3 * j : 3 * j + 3]
        at = slice(j * rows, (j + 1) * rows)
        for i, source in enumerate((b[0, 0], b[0, 1], c[0, 0], c[0, 1])):
            up[at, i * width : (i + 1) * width] = source.astype(f32)
        out[at] = c[0, 2].astype(f32)
        into[at, :width] = first[0, 0].astype(f32)
    own = (pl.program_id(0) // half_steps) == lax.rem(meta[0], 2)
    for i, (kept, other) in enumerate(((kept_p, other_p), (kept_q, other_q))):
        value = jnp.where(own, kept[0].astype(f32), other[0].astype(f32))
        into[:, (i + 1) * width : (i + 2) * width] = value


def spread(meta, gathered, orders, kept, other):
    devices, stacked, rows, width = gathered.shape
    if rows % 8:
        half = width // 2
        high = lax.axis_index("seq") % 2 == 1
        x, y = (jnp.concatenate(p)[:, :half].astype(f32) for p in (kept, other))
        rest = jnp.concatenate([jnp.where(high, y, x), jnp.where(high, x, y)], axis=1)
        a = restored(gathered[:, 3:4], orders[0])
        b, c = restored(gathered[:, 4:], orders[1]), restored(gathered[:, :3], orders[2])
        return (jnp.concatenate([b[0], b[1], c[0], c[1]], axis=1), c[2],
                jnp.concatenate([a[0], rest[0], rest[1]], axis=1))
    places = [device_of(order) for order in orders]
    many = 4
    steps = devices // many
    half = steps // 2
    tall = many * rows
    piece = pl.BlockSpec((1, tall, width), lambda s: (0, s % half, 0))
    shape = jax.ShapeDtypeStruct
    sources = []
    for j in range(many):
        for size, block, place in ((1, 3, places[0]), (2, 2, places[1]), (3, 0, places[2])):
            sources.append(pl.BlockSpec(
                (1, size, rows, width), lambda s, i=block, p=place, j=j: (p(s * many + j), i, 0, 0)))
    return pl.pallas_call(
        partial(spread_body, half, many),
        grid=(steps,),
        in_specs=[SMEM, *sources, piece, piece, piece, piece],
        out_specs=[
            pl.BlockSpec((tall, 4 * width), lambda s: (s, 0)),
            pl.BlockSpec((tall, width), lambda s: (s, 0)),
            pl.BlockSpec((tall, 3 * width), lambda s: (s, 0)),
        ],
        out_shape=[shape((width, 4 * width), f32), shape((width, width), f32), shape((width, 3 * width), f32)],
        compiler_params=params(60),
        cost_estimate=cost(0, 6 * devices * stacked * rows * width),
        name="spread",
    )(meta, *[gathered] * (3 * many), *kept, *other)


def spread_down_body(half_steps, meta, kept_a, kept_b, other_a, other_b, target):
    own = (pl.program_id(0) // half_steps) == lax.rem(meta[0], 2)
    for first, kept, other in ((0, kept_a, other_a), (3, kept_b, other_b)):
        for j in range(kept.shape[0]):
            target[first + j] = jnp.where(own, kept[j].astype(f32), other[j].astype(f32))


def spread_down(meta, kept, other):
    _, half_rows, width = kept[0].shape
    rows = 96
    half = half_rows // rows
    piece = lambda n: pl.BlockSpec((n, rows, width), lambda s: (0, s % half, 0))
    return pl.pallas_call(
        partial(spread_down_body, half),
        grid=(2 * half,),
        in_specs=[SMEM, piece(3), piece(1), piece(3), piece(1)],
        out_specs=pl.BlockSpec((4, rows, width), lambda s: (0, s, 0)),
        out_shape=jax.ShapeDtypeStruct((4, 2 * half_rows, width), f32),
        compiler_params=params(48),
        cost_estimate=cost(0, 24 * width * width),
        name="spread_down",
    )(meta, *kept, *other).reshape(8 * half_rows, width)


def unpack_body(layout, meta, kept_p, kept_q, other_p, other_q, *refs):
    *targets, rows = refs
    core = lax.rem(meta[0], 2)
    for i, (kept, other) in enumerate(((kept_p, other_p), (kept_q, other_q))):
        rows[i] = jnp.where(core == 0, kept[0].astype(f32), other[0].astype(f32))
    for target, entry in zip(targets, layout):
        for (r, c), block, row, lane in entry:
            size, across = r.stop - r.start, c.stop - c.start
            part = rows[block, row : row + size, lane : lane + across]
            if len(target.shape) == 1:
                target[c] = part[0]
            else:
                target[r, c] = part


def unpack(meta, kept, other, layout, shapes):
    _, rows, width = kept[0].shape
    at = (rows - PACK) // PACK
    piece = pl.BlockSpec((1, PACK, width), lambda i: (0, at, 0))
    return pl.pallas_call(
        partial(unpack_body, layout),
        grid=(1,),
        in_specs=[SMEM, piece, piece, piece, piece],
        out_specs=[whole(s) for s in shapes],
        out_shape=[jax.ShapeDtypeStruct(s, f32) for s in shapes],
        scratch_shapes=[pltpu.VMEM((2, PACK, width), f32)],
        compiler_params=params(32),
        cost_estimate=cost(0, 2 << 20),
        name="unpack",
    )(meta, *kept, *other)


def shards(
    tokens, cotangent, lengths, norm1_gain, norm1_shift, in_weight, in_bias, conv_weight, conv_bias,
    filter_in, filter_in_bias, filter_mid, filter_mid_bias, filter_last, filter_last_bias, filter_out,
    decay_rate, skip_gain, out_weight, out_bias, norm2_gain, norm2_shift, up_weight, up_bias,
    down_weight, down_bias,
):
    buckets, rows, width = tokens.shape
    hidden_width = up_weight.shape[1]
    blocks = lax.axis_size("seq")
    devices = blocks * lax.axis_size("batch")
    count = buckets * rows
    meta = jnp.concatenate([lax.axis_index("seq")[None].astype(jnp.int32), lengths.astype(jnp.int32)])
    high_np, low_np = block_tables(rows)
    high, low = jnp.asarray(high_np), jnp.asarray(low_np)
    back = jnp.asarray(np.ascontiguousarray(high_np.T))
    line = lambda a: a.reshape(1, -1)

    halo = lax.ppermute(tokens[:, rows - HALO :], "seq", [(i, i + 1) for i in range(blocks - 1)])
    conv_w = conv_weight.reshape(3, 3, width)
    conv_b = conv_bias.reshape(3, width)
    normed, mixed, product, gate_out = front(
        meta, tokens, halo, line(norm1_gain), line(norm1_shift), in_weight, in_bias.reshape(3, width), conv_w, conv_b)
    far = exchange_far(product)
    table = jnp.asarray(features(rows * blocks, filter_in.shape[0]))
    sines, cosines = filter_layers(
        table, filter_in, filter_in_bias, filter_mid, filter_mid_bias, filter_last, filter_last_bias)
    hidden = sines[2]
    shaped, spectrum = filter_spectra(hidden, filter_out, line(decay_rate), high, low, blocks)
    far, spectrum = after(far, spectrum)
    products = exchange_near(far)
    mixture, gated = conv_forward(meta, products, spectrum, gate_out, line(skip_gain), high, back)

    flat = lambda a: a.reshape(count, width)
    (normed2, d_down, resid, active, d_up, g_up_bias, d_resid, d_mixer, d_gated, d_conv,
     g_norm2_gain, g_norm2_shift, g_out_bias) = middle(
        meta, flat(gated), out_weight, line(out_bias), flat(tokens), flat(cotangent), line(norm2_gain),
        line(norm2_shift), up_weight, line(up_bias), down_weight, flat(gate_out), buckets)
    cube = lambda a: a.reshape(buckets, rows, width)
    seq_bits, batch_bits = index_bits("seq"), index_bits("batch")
    core, far_seq, near_batch, far_batch = seq_bits[0], seq_bits[1:], batch_bits[:1], batch_bits[1:]
    orders = [near_batch + far_seq + far_batch, far_seq + far_batch + near_batch, far_batch + near_batch + far_seq]
    barrier = lax.optimization_barrier

    def wave(chains, at):
        return [halve(parts, *order[at]) for parts, order in zip(chains, orders)]

    far = exchange_far(cube(d_conv))
    first_kept, first_sent, g_first, *first_parts = short_backward(
        meta, (mixture, cube(d_gated)), mixed, normed, conv_w, conv_b)
    g_down_bias, *stacks = weight_grads(
        meta, active, d_up, normed2, d_down, flat(gated), d_mixer, first_kept, first_sent)
    kept, sent = stacks[:3], stacks[3:]
    far, sent, active = after(far, sent, active)
    block_out = layer_output(meta, active, down_weight, line(down_bias), resid, buckets)
    grads = exchange_near(far)
    come = [xor_permute(a, *core) for a in sent]
    come, grads, block_out = barrier((come, grads, block_out))
    stack = lambda k, c: Part([(k, 0, 0), (c, 0, 0)], k.shape[0], k.shape[1])
    chains = [[stack(k, c)] for k, c in zip(kept, come)]
    chains = wave(chains, 0)
    d_product, g_skip, lags = conv_backward(meta, grads, product, spectrum, line(skip_gain), high, back)

    come, d_product, lags = barrier((waiting(chains), d_product, lags))
    arrived(chains, come)
    chains = wave(chains, 1)
    in_kept, in_sent, g_mixed, *other_parts = short_backward(meta, (d_product,), mixed, normed, conv_w, conv_b)
    (g_filter_out, g_decay, g_filter_in, g_filter_in_bias, g_filter_mid, g_filter_mid_bias,
     g_filter_last, g_filter_last_bias) = filter_backward(
        lags, back, hidden.astype(bf16), filter_out.astype(bf16), line(decay_rate), shaped, table, sines, cosines,
        filter_mid, filter_last)

    come, in_sent, g_filter_out, g_mixed = barrier((waiting(chains), in_sent, g_filter_out, g_mixed))
    arrived(chains, come)
    chains = wave(chains, 2)
    shapes = [
        (width,), (width,), (3 * width,), (3, 3 * width), (3 * width,), filter_in.shape, filter_in_bias.shape,
        filter_mid.shape, filter_mid_bias.shape, filter_last.shape, filter_last_bias.shape, filter_out.shape,
        (width,), (width,), (width,), (width,), (width,), (hidden_width,), (width,),
    ]
    layout = pack_layout(width, shapes)
    smalls = [
        g_filter_in, g_filter_in_bias, g_filter_mid, g_filter_mid_bias, g_filter_last, g_filter_last_bias,
        g_filter_out, g_decay, g_skip, g_out_bias, g_norm2_gain, g_norm2_shift, g_up_bias, g_down_bias,
    ]
    g_tokens, d_halo, in_kept, in_sent = token_grads(
        meta, g_first, g_mixed, in_weight, tokens, halo, line(norm1_gain), cube(d_resid), first_parts + other_parts,
        smalls, layout, in_kept, in_sent)

    come, in_kept, in_sent = barrier((waiting(chains), in_kept, in_sent))
    arrived(chains, come)
    in_come = xor_permute(in_sent, *core)
    for at in range(3, len(orders[0])):
        chains = wave(chains, at)
    arriving = lax.ppermute(d_halo[:, HALO - 2 :], "seq", [(i + 1, i) for i in range(blocks - 1)])
    g_tokens = g_tokens.at[:, rows - 2 :].add(arriving)
    whole_rows = in_kept.shape[1]
    order = orders[0]
    x, y, rest = near_batch[0], far_seq[0], far_seq[1:] + far_batch

    def in_sums():
        pair = [[Part([(in_kept, i, 0), (in_come, i, 0)], 1, whole_rows)] for i in range(2)]
        for steps in ((x, y), (y, x)):
            pair = [halve(parts, *step) for parts, step in zip(pair, steps)]
            arrived(pair, (yield waiting(pair)))
        joined = pair[0] + pair[1]
        for step in rest:
            joined = halve(joined, *step)
            arrived([joined], (yield waiting([joined])))
        done = jnp.concatenate([p.total(0, p.rows) for p in joined], axis=0)
        for step in reversed(rest):
            (come,) = yield [xor_permute(done, *step)]
            done = side_of(done, come, *step)
        pair = [done[:1], done[1:]]
        for steps in ((y, x), (x, y)):
            come = yield [xor_permute(a, *step) for a, step in zip(pair, steps)]
            pair = [side_of(a, c, *step) for a, c, step in zip(pair, come, steps)]
        come = yield [xor_permute(a, *core) for a in pair]
        return pair, come

    in_steps = in_sums()
    in_wait = next(in_steps)
    come, in_wait = barrier((waiting(chains), in_wait))
    arrived(chains, come)
    sums = [p.total(0, p.rows) for parts in chains for p in parts]
    both = jnp.concatenate([sums[2], sums[0][3:], sums[1][1:]], axis=0)
    gathered = lax.all_gather(both, ("seq", "batch"), axis=0)

    down = [sums[0][:3], sums[1][:1]]
    for steps in zip(reversed(orders[0]), reversed(orders[1])):
        down = [double(a, *step) for a, step in zip(down, steps)]
    grad_down_weight = spread_down(meta, down, [xor_permute(a, *core) for a in down])

    in_result, left = None, 2 * len(order) + 1
    while in_result is None:
        left -= 1
        if left == LAST_STEPS:
            in_wait, grad_down_weight, g_tokens = barrier((in_wait, grad_down_weight, g_tokens))
        try:
            in_wait = in_steps.send(in_wait)
        except StopIteration as end:
            in_result = end.value
    in_kept, in_come = in_result
    grad_up_weight, grad_out_weight, grad_in_weight = spread(
        meta, gathered, [[core, *o] for o in orders], in_kept, in_come)
    (n1g, n1s, inb, cw, cb, fi, fib, fm, fmb, fl, flb, fo, dr, sg, ob, n2g, n2s, ub, db) = unpack(
        meta, in_kept, in_come, layout, shapes)
    return (
        cube(block_out), g_tokens, n1g, n1s, grad_in_weight, inb, cw, cb, fi, fib, fm, fmb, fl, flb, fo, dr, sg,
        grad_out_weight, ob, n2g, n2s, grad_up_weight, ub, grad_down_weight, db,
    )


def solution(mesh):
    split = P("batch", "seq", None)
    return jax.shard_map(
        shards,
        mesh=mesh,
        in_specs=(split, split, P("batch")) + (P(),) * 23,
        out_specs=(split, split) + (P(),) * 23,
        check_vma=False,
    )
```

```python
from functools import partial
import math

import jax
import jax.numpy as jnp
import numpy as np
from jax import lax
from jax.experimental import pallas as pl
from jax.experimental.pallas import tpu as pltpu
from jax.sharding import PartitionSpec as P

norm_eps = 1e-05
window_floor = 0.05
highest = lax.Precision.HIGHEST
HALO = 16
CONV_TILE = 256
LAST_STEPS = 1
bf16 = jnp.bfloat16
f32 = jnp.float32


def dot(a, b, ca=1, cb=0, precision=None):
    return lax.dot_general(
        a, b, (((ca,), (cb,)), ((), ())), precision=precision, preferred_element_type=f32
    )


def xor_permute(array, axis, bit):
    count = lax.axis_size(axis)
    return lax.ppermute(array, axis, [(i, i ^ bit) for i in range(count)])


def exchange_far(array):
    held = {0: array}
    bit = lax.axis_size("seq") // 2
    while bit > 1:
        held.update({k ^ bit: xor_permute(a, "seq", bit) for k, a in list(held.items())})
        bit //= 2
    return held


def exchange_near(held):
    held = {**held, **{k ^ 1: xor_permute(a, "seq", 1) for k, a in held.items()}}
    return [held[k] for k in range(len(held))]


def after(held, *others):
    keys = [k for k in held if k]
    flat, others = lax.optimization_barrier(([held[k] for k in keys], others))
    return {**held, **dict(zip(keys, flat))}, *others


def block_tables(rows):
    phase = (2 * np.arange(rows)[:, None] + 1) * np.arange(rows)[None, :] % (4 * rows)
    angle = phase * (2.0 * math.pi / (4 * rows))
    table = np.concatenate([np.cos(angle), -np.sin(angle)], axis=0)
    high = table.astype(jnp.bfloat16)
    low = (table - high.astype(np.float64)).astype(jnp.bfloat16)
    return high, low


def features(seq_total, emb_width):
    bands = (emb_width - 1) // 2
    steps = np.arange(seq_total)
    phases = steps[:, None] * np.arange(1, bands + 1)[None, :] % seq_total
    angles = phases * (2.0 * math.pi / seq_total)
    ramp = steps / seq_total
    return np.concatenate([ramp[:, None], np.cos(angles), np.sin(angles)], axis=1).astype(np.float32)


def filter_layers(table, filter_in, in_bias, filter_mid, mid_bias, filter_last, last_bias):
    sines, cosines, value = [], [], table
    for weight, bias in ((filter_in, in_bias), (filter_mid, mid_bias), (filter_last, last_bias)):
        phase = jnp.dot(value, weight, precision=highest) + bias
        value = jnp.sin(phase)
        sines.append(value)
        cosines.append(jnp.cos(phase))
    return sines, cosines


def normalized(values):
    center = values - jnp.mean(values, axis=-1, keepdims=True)
    scale = lax.rsqrt(jnp.mean(center * center, axis=-1, keepdims=True) + norm_eps)
    return center * scale, scale


def live_rows(meta, bucket, rows):
    place = meta[0] * rows + lax.broadcasted_iota(jnp.int32, (rows, 1), 0)
    return (place < meta[1 + bucket]).astype(f32)


LIMIT = 0


def params(mib, count=1):
    return pltpu.CompilerParams(
        dimension_semantics=("arbitrary",) * count, vmem_limit_bytes=max(mib, LIMIT) * 1024 * 1024
    )


SMEM = pl.BlockSpec(memory_space=pltpu.SMEM)


def whole(shape):
    zeros = (0,) * len(shape)
    return pl.BlockSpec(tuple(shape), lambda *_: zeros)


def cost(flops, read):
    return pl.CostEstimate(flops=flops, bytes_accessed=read, transcendentals=0)


def front_body(buckets, rows, meta, tok, halo, gain, shift, w0, w1, w2, bias, cw, cb,
               normed, mixed, product, gate_out, taps_in):
    ext = rows + HALO

    @pl.when(pl.program_id(0) == 0)
    def _():
        for b in range(buckets):
            hat, _ = normalized(halo[b].astype(f32))
            normed[b * ext : b * ext + HALO] = (hat * gain[...] + shift[...]).astype(bf16)
            hat, _ = normalized(tok[b].astype(f32))
            normed[b * ext + HALO : (b + 1) * ext] = (hat * gain[...] + shift[...]).astype(bf16)

    inner = meta[0] > 0
    for b in range(buckets):
        parts = []
        for t, w in enumerate((w0, w1, w2)):
            m = (dot(normed[b * ext : (b + 1) * ext], w[...]) + bias[t : t + 1]).astype(bf16)
            head = jnp.where(inner, m[:HALO].astype(f32), 0.0)
            mixed[t, b, :HALO] = head.astype(bf16)
            mixed[t, b, HALO:] = m[HALO:]
            taps_in[t, :HALO] = head
            taps_in[t, HALO:] = m[HALO:].astype(f32)
            s = cb[t : t + 1]
            for i in range(3):
                s = s + cw[i, t : t + 1] * taps_in[t, HALO - 2 + i : HALO - 2 + i + rows]
            parts.append(s)
        gate_out[b] = parts[0]
        product[b] = (parts[2] * parts[1] * live_rows(meta, b, rows)).astype(bf16)


def front(meta, tok, halo, gain, shift, in_weight, in_bias, conv_weight, conv_bias):
    buckets, rows, width = tok.shape
    ext = rows + HALO
    tile = 256
    steps = width // tile
    columns = [pl.BlockSpec((width, tile), lambda c, t=t: (0, t * steps + c)) for t in range(3)]
    return pl.pallas_call(
        partial(front_body, buckets, rows),
        grid=(steps,),
        in_specs=[
            SMEM, whole(tok.shape), whole(halo.shape), whole((1, width)), whole((1, width)), *columns,
            pl.BlockSpec((3, tile), lambda c: (0, c)),
            pl.BlockSpec((3, 3, tile), lambda c: (0, 0, c)),
            pl.BlockSpec((3, tile), lambda c: (0, c)),
        ],
        out_specs=[
            whole((buckets * ext, width)),
            pl.BlockSpec((3, buckets, ext, tile), lambda c: (0, 0, 0, c)),
            pl.BlockSpec((buckets, rows, tile), lambda c: (0, 0, c)),
            pl.BlockSpec((buckets, rows, tile), lambda c: (0, 0, c)),
        ],
        out_shape=[
            jax.ShapeDtypeStruct((buckets * ext, width), bf16),
            jax.ShapeDtypeStruct((3, buckets, ext, width), bf16),
            jax.ShapeDtypeStruct((buckets, rows, width), bf16),
            jax.ShapeDtypeStruct((buckets, rows, width), f32),
        ],
        scratch_shapes=[pltpu.VMEM((3, ext, tile), f32)],
        compiler_params=params(48),
        cost_estimate=cost(6 * buckets * ext * width * width, 16 << 20),
        name="front",
    )(meta, tok, halo, gain, shift, in_weight, in_weight, in_weight, in_bias, conv_weight, conv_bias)


def alternating(rows):
    parity = lax.broadcasted_iota(jnp.int32, (rows, 1), 0) % 2
    return (1 - 2 * parity).astype(f32)


def window_of(first, rows, total, decay):
    ramp = (first + lax.broadcasted_iota(jnp.int32, (rows, 1), 0)).astype(f32) * (1.0 / total)
    return ramp, jnp.exp(-ramp * decay)


def filter_body(blocks, rows, hidden, out, decay, high, low, shaped, spectrum):
    sign = alternating(rows)
    last = None
    for m in range(blocks):
        here = slice(m * rows, (m + 1) * rows)
        plain = dot(hidden[here], out[...], precision=highest)
        shaped[here] = plain
        _, fall = window_of(m * rows, rows, blocks * rows, decay[...])
        taps = plain * (fall + window_floor)
        upper = taps.astype(bf16)
        rest = (taps - upper.astype(f32)).astype(bf16)
        full = dot(high[...], upper) + (dot(high[...], rest) + dot(low[...], upper))
        re, im = full[:rows], full[rows:]
        if last is None:
            spectrum[m, :rows] = re
            spectrum[m, rows:] = im
        else:
            spectrum[m, :rows] = re - sign * last[1]
            spectrum[m, rows:] = im + sign * last[0]
        last = (re, im)
    spectrum[blocks] = jnp.zeros(spectrum.shape[1:], f32)


def filter_spectra(hidden, filter_out, decay, high, low, blocks):
    total, inner = hidden.shape
    width = filter_out.shape[1]
    rows = total // blocks
    tile = 256
    return pl.pallas_call(
        partial(filter_body, blocks, rows),
        grid=(width // tile,),
        in_specs=[
            whole(hidden.shape),
            pl.BlockSpec((inner, tile), lambda c: (0, c)),
            pl.BlockSpec((1, tile), lambda c: (0, c)),
            whole(high.shape), whole(low.shape),
        ],
        out_specs=[
            pl.BlockSpec((total, tile), lambda c: (0, c)),
            pl.BlockSpec((blocks + 1, 2 * rows, tile), lambda c: (0, 0, c)),
        ],
        out_shape=[
            jax.ShapeDtypeStruct((total, width), f32),
            jax.ShapeDtypeStruct((blocks + 1, 2 * rows, width), f32),
        ],
        compiler_params=params(48),
        cost_estimate=cost(20 * total * width * rows, 10 << 20),
        name="filter_spectra",
    )(hidden, filter_out, decay, high, low)


def conv_body(blocks, rows, meta, *refs):
    products = refs[:blocks]
    spectrum, gate_out, skip, high, back, mixture, gated = refs[blocks:]
    own = meta[0]
    for c in range(products[0].shape[2] // CONV_TILE):
        at = slice(c * CONV_TILE, (c + 1) * CONV_TILE)
        sum_re = sum_im = None
        for k in range(blocks):
            lag = own - (own ^ k)
            lag = jnp.where(lag < 0, blocks, lag)
            full = dot(high[...], products[k][0, :, at])
            re, im = full[:rows], full[rows:]
            tap_re, tap_im = spectrum[lag, :rows, at], spectrum[lag, rows:, at]
            out_re = tap_re * re - tap_im * im
            out_im = tap_re * im + tap_im * re
            sum_re = out_re if sum_re is None else sum_re + out_re
            sum_im = out_im if sum_im is None else sum_im + out_im
        convolved = dot(back[:, :rows], sum_re.astype(bf16)) + dot(back[:, rows:], sum_im.astype(bf16))
        mixed = convolved * (1.0 / rows) + skip[:, at] * products[0][0, :, at].astype(f32)
        mixture[0, :, at] = mixed
        gated[0, :, at] = (mixed * gate_out[0, :, at]).astype(bf16)


def conv_forward(meta, products, spectrum, gate_out, skip, high, back):
    buckets, rows, width = gate_out.shape
    blocks = len(products)
    tile = width
    piece = pl.BlockSpec((1, rows, tile), lambda c, b: (b, 0, c))
    return pl.pallas_call(
        partial(conv_body, blocks, rows),
        grid=(width // tile, buckets),
        in_specs=[SMEM] + [piece] * blocks + [
            pl.BlockSpec((blocks + 1, 2 * rows, tile), lambda c, b: (0, 0, c)), piece,
            pl.BlockSpec((1, tile), lambda c, b: (0, c)), whole(high.shape), whole(back.shape),
        ],
        out_specs=[piece, piece],
        out_shape=[
            jax.ShapeDtypeStruct((buckets, rows, width), f32),
            jax.ShapeDtypeStruct((buckets, rows, width), bf16),
        ],
        compiler_params=params(56, 2),
        cost_estimate=cost(4 * (blocks + 1) * rows * rows * width * buckets, 16 << 20),
        name="conv_forward",
    )(meta, *products, spectrum, gate_out, skip, high, back)


def gelu_parts(u):
    cdf = 0.5 + 0.5 * lax.erf(u * (1.0 / math.sqrt(2.0)))
    pdf = jnp.exp(-0.5 * u * u) * (1.0 / math.sqrt(2.0 * math.pi))
    return u * cdf, cdf + u * pdf


def middle_body(buckets, rows, steps, meta, gated, out_w, out_b, tok, cot, gain, shift, up_w, up_b, down_w,
                gate_out, normed2, d_down, resid, active, d_up, g_up_bias, d_resid, d_mixer, d_gated, d_conv,
                g_gain, g_shift, g_out_bias, total):
    step = pl.program_id(0)

    @pl.when(step == 0)
    def _():
        for b in range(buckets):
            here = slice(b * rows, (b + 1) * rows)
            live = live_rows(meta, b, rows)
            mixer = dot(gated[here], out_w[...]) + out_b[...]
            r = tok[here].astype(f32) + live * mixer
            resid[here] = r
            hat, _ = normalized(r)
            normed2[here] = (hat * gain[...] + shift[...]).astype(bf16)
            d_down[here] = (live * cot[here].astype(f32)).astype(bf16)
            total[here] = jnp.zeros_like(total[here])

    bias_sum = None
    for b in range(buckets):
        here = slice(b * rows, (b + 1) * rows)
        u = dot(normed2[here], up_w[...]) + up_b[...]
        d_active = dot(d_down[here], down_w[...], 1, 1)
        act, slope = gelu_parts(u)
        active[here] = act.astype(bf16)
        d_u = (d_active * slope).astype(bf16)
        d_up[here] = d_u
        part = jnp.sum(d_u.astype(f32), axis=0, keepdims=True)
        bias_sum = part if bias_sum is None else bias_sum + part
        back = dot(d_u, up_w[...], 1, 1)

        total[here] += back

    g_up_bias[...] = bias_sum

    @pl.when(step == steps - 1)
    def _():
        sums = [jnp.zeros((1, gain.shape[1]), f32)] * 3
        for b in range(buckets):
            here = slice(b * rows, (b + 1) * rows)
            live = live_rows(meta, b, rows)
            hat, scale = normalized(resid[here])
            d = total[here]
            sums[0] = sums[0] + jnp.sum(d * hat, axis=0, keepdims=True)
            sums[1] = sums[1] + jnp.sum(d, axis=0, keepdims=True)
            e = d * gain[...]
            mean_e = jnp.mean(e, axis=-1, keepdims=True)
            mean_eh = jnp.mean(e * hat, axis=-1, keepdims=True)
            d_r = cot[here].astype(f32) + (e - mean_e - hat * mean_eh) * scale
            d_resid[here] = d_r
            d_m = (live * d_r).astype(bf16)
            d_mixer[here] = d_m
            sums[2] = sums[2] + jnp.sum(d_m.astype(f32), axis=0, keepdims=True)
            d_g = dot(d_m, out_w[...], 1, 1)
            d_gated[here] = d_g
            d_conv[here] = (d_g * gate_out[here]).astype(bf16)
        g_gain[...] = sums[0]
        g_shift[...] = sums[1]
        g_out_bias[...] = sums[2]


def middle(meta, gated, out_w, out_b, tok, cot, gain, shift, up_w, up_b, down_w, gate_out, buckets):
    count, width = tok.shape
    hidden = up_w.shape[1]
    tile = width
    steps = hidden // tile
    rows = count // buckets
    square = whole((count, width))
    line = whole((1, width))
    shape = jax.ShapeDtypeStruct
    return pl.pallas_call(
        partial(middle_body, buckets, rows, steps),
        grid=(steps,),
        in_specs=[
            SMEM, square, whole(out_w.shape), line, square, square, line, line,
            pl.BlockSpec((width, tile), lambda s: (0, s)),
            pl.BlockSpec((1, tile), lambda s: (0, s)),
            pl.BlockSpec((tile, width), lambda s: (s, 0)),
            square,
        ],
        out_specs=[
            square, square, square,
            pl.BlockSpec((count, tile), lambda s: (0, s)),
            pl.BlockSpec((count, tile), lambda s: (0, s)),
            pl.BlockSpec((1, tile), lambda s: (0, s)),
            square, square, square, square, line, line, line,
        ],
        out_shape=[
            shape((count, width), bf16), shape((count, width), bf16), shape((count, width), f32),
            shape((count, hidden), bf16), shape((count, hidden), bf16), shape((1, hidden), f32),
            shape((count, width), f32), shape((count, width), bf16), shape((count, width), f32),
            shape((count, width), bf16), shape((1, width), f32), shape((1, width), f32), shape((1, width), f32),
        ],
        scratch_shapes=[pltpu.VMEM((count, width), f32)],
        compiler_params=params(56),
        cost_estimate=cost(6 * count * width * hidden, 40 << 20),
        name="middle",
    )(meta, gated, out_w, out_b, tok, cot, gain, shift, up_w, up_b, down_w, gate_out)


def own_half(core, width, mine):
    half = width // 2
    return pl.ds(pl.multiple_of((core if mine else 1 - core) * half, half), half)


def weights_body(steps, meta, active, d_up, normed2, d_down, gated, d_mixer, first_kept, first_sent, g_bias, *stacks):
    del first_kept, first_sent
    kept, sent = stacks[:3], stacks[3:]
    step = pl.program_id(0)
    core = lax.rem(meta[0], 2)
    width = normed2.shape[1]
    mine, theirs = own_half(core, width, True), own_half(core, width, False)

    @pl.when(step < steps)
    def _():
        down = [dot(active[:, at], d_down[...], 0, 0).astype(bf16) for at in (mine, theirs)]
        up = [dot(normed2[:, at], d_up[...], 0, 0).astype(bf16) for at in (mine, theirs)]
        for first, stop, source, stack in ((0, 3, down, 0), (3, 4, down, 1), (0, 2, up, 1), (2, 4, up, 2)):

            @pl.when((step >= first) & (step < stop))
            def _(source=source, stack=stack):
                kept[stack][0] = source[0]
                sent[stack][0] = source[1]

    @pl.when(step == steps)
    def _():
        kept[2][0] = dot(gated[:, mine], d_mixer[...], 0, 0).astype(bf16)
        sent[2][0] = dot(gated[:, theirs], d_mixer[...], 0, 0).astype(bf16)
        g_bias[...] = jnp.sum(d_down[...].astype(f32), axis=0, keepdims=True)


def weight_grads(meta, active, d_up, normed2, d_down, gated, d_mixer, first_kept, first_sent):
    count, width = normed2.shape
    hidden = active.shape[1]
    steps = hidden // width
    assert steps == 4
    square = whole((count, width))
    shape = jax.ShapeDtypeStruct
    last = steps - 1
    columns = pl.BlockSpec((count, width), lambda s: (0, jnp.minimum(s, last)))
    half = (1, width // 2, width)
    stacks = [
        pl.BlockSpec(half, lambda s: (jnp.minimum(s, 2), 0, 0)),
        pl.BlockSpec(half, lambda s: (jnp.where(s > 2, 0, jnp.minimum(s + 1, 2)), 0, 0)),
        pl.BlockSpec(half, lambda s: (jnp.maximum(s - 2, 0), 0, 0)),
    ]
    return pl.pallas_call(
        partial(weights_body, steps),
        grid=(steps + 1,),
        in_specs=[SMEM, columns, columns, square, square, square, square] + [pl.BlockSpec(memory_space=pl.ANY)] * 2,
        out_specs=[whole((1, width)), *stacks, *stacks],
        out_shape=[shape((1, width), f32)] + [shape((n, width // 2, width), bf16) for n in (4, 3, 3)] * 2,
        input_output_aliases={7: 1, 8: 4},
        compiler_params=params(56),
        cost_estimate=cost(4 * count * width * hidden, 40 << 20),
        name="weight_grads",
    )(meta, active, d_up, normed2, d_down, gated, d_mixer, first_kept, first_sent)


def output_body(buckets, rows, steps, meta, active, down_w, down_b, resid, block_out, total):
    step = pl.program_id(0)

    @pl.when(step == 0)
    def _():
        total[...] = dot(active[...], down_w[...])

    @pl.when(step > 0)
    def _():
        total[...] += dot(active[...], down_w[...])

    @pl.when(step == steps - 1)
    def _():
        for b in range(buckets):
            here = slice(b * rows, (b + 1) * rows)
            live = live_rows(meta, b, rows)
            block_out[here] = (resid[here] + live * (total[here] + down_b[...])).astype(bf16)


def layer_output(meta, active, down_w, down_b, resid, buckets):
    count, width = resid.shape
    hidden = down_w.shape[0]
    steps = hidden // width
    return pl.pallas_call(
        partial(output_body, buckets, count // buckets, steps),
        grid=(steps,),
        in_specs=[
            SMEM, pl.BlockSpec((count, width), lambda s: (0, s)), pl.BlockSpec((width, width), lambda s: (s, 0)),
            whole((1, width)), whole((count, width)),
        ],
        out_specs=whole((count, width)),
        out_shape=jax.ShapeDtypeStruct((count, width), bf16),
        scratch_shapes=[pltpu.VMEM((count, width), f32)],
        compiler_params=params(48),
        cost_estimate=cost(2 * count * width * hidden, 14 << 20),
        name="layer_output",
    )(meta, active, down_w, down_b, resid)


def conv_back_body(blocks, rows, buckets, meta, *refs):
    grads = refs[:blocks]
    product, spectrum, skip, high, back, d_product, g_skip, g_lags, lags = refs[blocks:]
    own = meta[0]
    b = pl.program_id(1)

    @pl.when(b == 0)
    def _():
        lags[...] = jnp.zeros_like(lags)
        g_skip[...] = jnp.zeros_like(g_skip)

    full = dot(high[...], product[0])
    prod_re, prod_im = full[:rows], full[rows:]
    sum_re = sum_im = None
    for k in range(blocks):
        lag = (own ^ k) - own
        lag = jnp.where(lag < 0, blocks, lag)
        grad = dot(high[...], grads[k][0])
        re, im = grad[:rows], grad[rows:]
        tap_re, tap_im = spectrum[lag, :rows], spectrum[lag, rows:]
        out_re = tap_re * re + tap_im * im
        out_im = tap_re * im - tap_im * re
        sum_re = out_re if sum_re is None else sum_re + out_re
        sum_im = out_im if sum_im is None else sum_im + out_im
        lags[lag, :rows] += re * prod_re + im * prod_im
        lags[lag, rows:] += im * prod_re - re * prod_im
    d_own = grads[0][0].astype(f32)
    full = dot(back[:, :rows], sum_re.astype(bf16)) + dot(back[:, rows:], sum_im.astype(bf16))
    d_product[0] = full * (1.0 / rows) + skip[...] * d_own
    g_skip[...] += jnp.sum(d_own * product[0].astype(f32), axis=0, keepdims=True)

    @pl.when(b == buckets - 1)
    def _():
        g_lags[...] = lags[:blocks].astype(bf16)


def conv_backward(meta, grads, product, spectrum, skip, high, back):
    buckets, rows, width = product.shape
    blocks = len(grads)
    tile = CONV_TILE
    piece = pl.BlockSpec((1, rows, tile), lambda c, b: (b, 0, c))
    line = pl.BlockSpec((1, tile), lambda c, b: (0, c))
    shape = jax.ShapeDtypeStruct
    return pl.pallas_call(
        partial(conv_back_body, blocks, rows, buckets),
        grid=(width // tile, buckets),
        in_specs=[SMEM] + [piece] * blocks + [
            piece, pl.BlockSpec((blocks + 1, 2 * rows, tile), lambda c, b: (0, 0, c)), line, whole(high.shape),
            whole(back.shape),
        ],
        out_specs=[piece, line, pl.BlockSpec((blocks, 2 * rows, tile), lambda c, b: (0, 0, c))],
        out_shape=[shape((buckets, rows, width), f32), shape((1, width), f32), shape((blocks, 2 * rows, width), bf16)],
        scratch_shapes=[pltpu.VMEM((blocks + 1, 2 * rows, tile), f32)],
        compiler_params=params(60, 2),
        cost_estimate=cost(4 * (2 * blocks + 2) * rows * rows * width * buckets, 20 << 20),
        name="conv_backward",
    )(meta, *grads, product, spectrum, skip, high, back)


def filter_back_body(blocks, rows, tile, lags, back, hidden, filter_out, decay, shaped, table, sin_a, sin_b, cos_a, cos_b,
                     cos_c, filter_mid, filter_last, g_filter_out, g_decay, g_in, g_in_bias, g_mid, g_mid_bias,
                     g_last, g_last_bias, g_hidden):
    sign = alternating(rows)
    for c in range(decay.shape[1] // tile):
        at = slice(c * tile, (c + 1) * tile)
        sum_out = sum_decay = None
        for m in range(blocks):
            here = slice(m * rows, (m + 1) * rows)
            re, im = lags[m, :rows, at].astype(f32), lags[m, rows:, at].astype(f32)
            if m + 1 < blocks:
                re = re + sign * lags[m + 1, rows:, at].astype(f32)
                im = im - sign * lags[m + 1, :rows, at].astype(f32)
            d_taps = dot(back[:, :rows], re.astype(bf16)) + dot(back[:, rows:], im.astype(bf16))
            d_taps = d_taps * (1.0 / rows)
            ramp, fall = window_of(m * rows, rows, blocks * rows, decay[:, at])
            g_d = -jnp.sum(d_taps * shaped[here, at] * ramp * fall, axis=0, keepdims=True)
            d_shaped = (d_taps * (fall + window_floor)).astype(bf16)
            g_o = dot(hidden[here], d_shaped, 0, 0)
            sum_out = g_o if sum_out is None else sum_out + g_o
            sum_decay = g_d if sum_decay is None else sum_decay + g_d
            d_hidden = dot(d_shaped, filter_out[:, at], 1, 1)
            g_hidden[here] = d_hidden if c == 0 else g_hidden[here] + d_hidden
        g_filter_out[:, at] = sum_out
        g_decay[:, at] = sum_decay
    d_c = g_hidden[...] * cos_c[...]
    g_last_bias[...] = jnp.sum(d_c, axis=0, keepdims=True)
    d_c = d_c.astype(bf16)
    g_last[...] = dot(sin_b[...].astype(bf16), d_c, 0, 0)
    d_b = dot(d_c, filter_last[...].astype(bf16), 1, 1) * cos_b[...]
    g_mid_bias[...] = jnp.sum(d_b, axis=0, keepdims=True)
    d_b = d_b.astype(bf16)
    g_mid[...] = dot(sin_a[...].astype(bf16), d_b, 0, 0)
    d_a = dot(d_b, filter_mid[...].astype(bf16), 1, 1) * cos_a[...]
    g_in[...] = dot(table[...].astype(bf16), d_a.astype(bf16), 0, 0)
    g_in_bias[...] = jnp.sum(d_a, axis=0, keepdims=True)


def filter_backward(lags, back, hidden, filter_out, decay, shaped, table, sines, cosines, filter_mid, filter_last):
    blocks, double_rows, width = lags.shape
    total, inner = hidden.shape
    shape = jax.ShapeDtypeStruct
    outs = [shape((inner, width), f32), shape((1, width), f32),
            shape((table.shape[1], inner), f32), shape((1, inner), f32), shape((inner, inner), f32),
            shape((1, inner), f32), shape((inner, inner), f32), shape((1, inner), f32)]
    arrays = [lags, back, hidden, filter_out, decay, shaped, table, sines[0], sines[1], *cosines, filter_mid, filter_last]
    return pl.pallas_call(
        partial(filter_back_body, blocks, double_rows // 2, 256),
        grid=(1,),
        in_specs=[whole(a.shape) for a in arrays],
        out_specs=[whole(a.shape) for a in outs],
        out_shape=outs,
        scratch_shapes=[pltpu.VMEM((total, inner), f32)],
        compiler_params=params(56),
        cost_estimate=cost(10 * total * width * double_rows, 10 << 20),
        name="filter_backward",
    )(*arrays)


PACK = 128


def pack_layout(width, shapes):
    out, narrow, row = [], 0, [64, 64]
    for shape in shapes:
        r, c = (1, shape[0]) if len(shape) == 1 else shape
        if c < width:
            out.append([((slice(0, r), slice(0, c)), 0, 0, narrow)])
            narrow += 128
        elif r > 32:
            out.append([((slice(0, r), slice(0, c)), 1, 0, 0)])
        else:
            entry = []
            for j in range(c // width):
                block = 0 if row[0] + r <= PACK else 1
                entry.append(((slice(0, r), slice(j * width, (j + 1) * width)), block, row[block], 0))
                row[block] += r
            out.append(entry)
    assert max(row) <= PACK and narrow <= width
    return out


def short_back_body(buckets, rows, first, meta, *refs):
    count = 1 if first else 2
    if first:
        mixture, d_gated, *refs = refs
    else:
        d_product, *refs = refs
    mixed, refs = refs[:count], refs[count:]
    normed, cw, cb, kept, sent, g_mixed, g_conv, g_conv_bias, g_bias, taps_in, d_pad = refs
    ext = rows + HALO
    inner = meta[0] > 0
    core = lax.rem(meta[0], 2)
    tile = cb.shape[1]
    width = normed.shape[1]
    sums = [[jnp.zeros((1, tile), f32)] * 5 for _ in range(count)]
    for b in range(buckets):
        short = []
        for t in range(count):
            k = t if first else t + 1
            taps_in[t] = mixed[t][0, b].astype(f32)
            s = cb[k : k + 1]
            if not first:
                for i in range(3):
                    s = s + cw[i, k : k + 1] * taps_in[t, HALO - 2 + i : HALO - 2 + i + rows]
            short.append(s)
        if first:
            d_shorts = (d_gated[b] * mixture[b],)
        else:
            d_prod = d_product[b] * live_rows(meta, b, rows)
            d_shorts = (d_prod * short[1], d_prod * short[0])
        for t in range(count):
            k = t if first else t + 1
            d_short = d_shorts[t]
            d_pad[t, :HALO] = jnp.zeros((HALO, tile), f32)
            d_pad[t, HALO : HALO + rows] = d_short
            d_pad[t, HALO + rows :] = jnp.zeros((8, tile), f32)
            for i in range(3):
                sums[t][i] = sums[t][i] + jnp.sum(
                    d_short * taps_in[t, HALO - 2 + i : HALO - 2 + i + rows], axis=0, keepdims=True)
            sums[t][3] = sums[t][3] + jnp.sum(d_short, axis=0, keepdims=True)
            g = (cw[2, k : k + 1] * d_pad[t, :ext] + cw[1, k : k + 1] * d_pad[t, 1 : ext + 1]
                 + cw[0, k : k + 1] * d_pad[t, 2 : ext + 2])
            head = jnp.where(inner, g[:HALO], 0.0).astype(bf16)
            body = g[HALO:].astype(bf16)
            g_mixed[t, b * ext : b * ext + HALO] = head
            g_mixed[t, b * ext + HALO : (b + 1) * ext] = body
            sums[t][4] = sums[t][4] + (jnp.sum(head.astype(f32), axis=0, keepdims=True)
                                       + jnp.sum(body.astype(f32), axis=0, keepdims=True))
    for t in range(count):
        for i in range(3):
            g_conv[i, t : t + 1] = sums[t][i]
        g_conv_bias[t : t + 1] = sums[t][3]
        g_bias[t : t + 1] = sums[t][4]
        kept[t] = dot(normed[:, own_half(core, width, True)], g_mixed[t], 0, 0).astype(bf16)
        sent[t] = dot(normed[:, own_half(core, width, False)], g_mixed[t], 0, 0).astype(bf16)


def short_backward(meta, sources, mixed, normed, conv_weight, conv_bias):
    _, buckets, ext, width = mixed.shape
    rows = ext - HALO
    tile = 256
    first = len(sources) == 2
    count = 1 if first else 2
    piece = pl.BlockSpec((buckets, rows, tile), lambda c: (0, 0, c))
    columns = [pl.BlockSpec((1, buckets, ext, tile), lambda c, t=t: (t, 0, 0, c)) for t in ([0] if first else [1, 2])]
    three = pl.BlockSpec((3, tile), lambda c: (0, c))
    nine = pl.BlockSpec((3, 3, tile), lambda c: (0, 0, c))
    line = pl.BlockSpec((count, tile), lambda c: (0, c))
    half = pl.BlockSpec((count, width // 2, tile), lambda c: (3 if first else 0, 0, c))
    halves = (4, width // 2, width) if first else (2, width // 2 + PACK, width)
    shape = jax.ShapeDtypeStruct
    return pl.pallas_call(
        partial(short_back_body, buckets, rows, first),
        grid=(width // tile,),
        in_specs=[SMEM, *[piece] * len(sources), *columns, whole(normed.shape), nine, three],
        out_specs=[
            half, half, pl.BlockSpec((count, buckets * ext, tile), lambda c: (0, 0, c)),
            pl.BlockSpec((3, count, tile), lambda c: (0, 0, c)), line, line,
        ],
        out_shape=[
            shape(halves, bf16), shape(halves, bf16),
            shape((count, buckets * ext, width), bf16), shape((3, count, width), f32), shape((count, width), f32),
            shape((count, width), f32),
        ],
        scratch_shapes=[pltpu.VMEM((count, ext, tile), f32), pltpu.VMEM((count, ext + 8, tile), f32)],
        compiler_params=params(56),
        cost_estimate=cost(2 * count * buckets * ext * width * width, 10 << 20),
        name="short_backward",
    )(meta, *sources, *[mixed] * count, normed, conv_weight, conv_bias)


def token_body(buckets, rows, layout, others, meta, g_first, g_mixed, weight, tok, halo, gain, d_resid, *refs):
    parts, refs = refs[:6], refs[6:]
    smalls, (_, _, g_tokens, d_halo, kept, sent, total, pack) = refs[:others], refs[others:]
    ext = rows + HALO
    step = pl.program_id(0)
    core = lax.rem(meta[0], 2)

    @pl.when(step == 0)
    def _():
        total[...] = dot(g_first[0], weight[...], 1, 1)

    @pl.when(step > 0)
    def _():
        total[...] += dot(g_mixed[0], weight[...], 1, 1)

    @pl.when(step == 2)
    def _():
        add = [jnp.zeros((1, gain.shape[1]), f32)] * 2
        for b in range(buckets):
            for first, size, source in ((0, HALO, halo), (HALO, rows, tok)):
                d = total[b * ext + first : b * ext + first + size]
                hat, scale = normalized(source[b].astype(f32))
                add[0] = add[0] + jnp.sum(d * hat, axis=0, keepdims=True)
                add[1] = add[1] + jnp.sum(d, axis=0, keepdims=True)
                e = d * gain[...]
                mean_e = jnp.mean(e, axis=-1, keepdims=True)
                mean_eh = jnp.mean(e * hat, axis=-1, keepdims=True)
                d_v = (e - mean_e - hat * mean_eh) * scale
                if first:
                    g_tokens[b] = d_resid[b] + d_v
                else:
                    d_halo[b] = d_v
        pack[...] = jnp.zeros_like(pack)
        for source, entry in zip(add, layout[:2]):
            (_, block, row, _), = entry
            pack[block, row : row + 1] = source
        conv, conv_bias, bias = parts[0::3], parts[1::3], parts[2::3]
        for j in range(3):
            p, q = (0, 0) if j == 0 else (1, j - 1)
            _, block, row, _ = layout[2][j]
            pack[block, row : row + 1] = bias[p][q : q + 1]
            _, block, row, _ = layout[4][j]
            pack[block, row : row + 1] = conv_bias[p][q : q + 1]
            _, block, row, _ = layout[3][j]
            for i in range(3):
                pack[block, row + i : row + i + 1] = conv[p][i, q : q + 1]
        for source, entry in zip(smalls, layout[5:]):
            for (r, c), block, row, lane in entry:
                pack[block, row : row + r.stop - r.start, lane : lane + c.stop - c.start] = source[r, c]
        kept[...] = jnp.where(core == 0, pack[...], 0.0).astype(bf16)
        sent[...] = jnp.where(core == 0, 0.0, pack[...]).astype(bf16)


def token_grads(meta, g_first, g_mixed, in_weight, tok, halo, gain, d_resid, parts, smalls, layout, in_kept, in_sent):
    buckets, rows, width = tok.shape
    ext = rows + HALO
    shape = jax.ShapeDtypeStruct
    packed = (2, PACK, width)
    arrays = [tok, halo, gain, d_resid, *parts, *smalls]
    last = pl.BlockSpec(packed, lambda t: (0, (width // 2) // PACK, 0))
    return pl.pallas_call(
        partial(token_body, buckets, rows, layout, len(smalls)),
        grid=(3,),
        in_specs=[
            SMEM, whole(g_first.shape), pl.BlockSpec((1, buckets * ext, width), lambda t: (jnp.maximum(t - 1, 0), 0, 0)),
            pl.BlockSpec((width, width), lambda t: (0, t)), *[whole(a.shape) for a in arrays],
            *[pl.BlockSpec(memory_space=pl.ANY)] * 2,
        ],
        out_specs=[whole(tok.shape), whole(halo.shape), last, last],
        out_shape=[shape(tok.shape, f32), shape(halo.shape, f32), shape(in_kept.shape, bf16), shape(in_sent.shape, bf16)],
        input_output_aliases={4 + len(arrays): 2, 5 + len(arrays): 3},
        scratch_shapes=[pltpu.VMEM((buckets * ext, width), f32), pltpu.VMEM(packed, f32)],
        compiler_params=params(56),
        cost_estimate=cost(6 * buckets * ext * width * width, 30 << 20),
        name="token_grads",
    )(meta, g_first, g_mixed, in_weight, *arrays, in_kept, in_sent)


def index_bits(axis):
    count = lax.axis_size(axis)
    return [(axis, 1 << i) for i in range(count.bit_length() - 1)]


def bit_of(axis, bit):
    return (lax.axis_index(axis) // bit) % 2


class Part:
    def __init__(self, terms, blocks, rows):
        self.terms, self.blocks, self.rows = terms, blocks, rows

    def total(self, first, rows):
        value = None
        for array, block, row in self.terms:
            term = lax.dynamic_slice(array, (block, row + first, 0), (self.blocks, rows, array.shape[2])).astype(f32)
            value = term if value is None else value + term
        return value.astype(bf16)


def halve(parts, axis, bit):
    mine = bit_of(axis, bit)
    halves = [p.rows // 2 for p in parts]
    sent = [p.total((1 - mine) * h, h) for p, h in zip(parts, halves)]
    come = xor_permute(sent[0] if len(sent) == 1 else jnp.concatenate(sent, axis=0), axis, bit)
    out, block = [], 0
    for p, h in zip(parts, halves):
        terms = [(array, at, row + mine * h) for array, at, row in p.terms]
        out.append(Part(terms + [(come, block, 0)], p.blocks, h))
        block += p.blocks
    return out


def waiting(chains):
    return [parts[0].terms[-1][0] for parts in chains]


def arrived(chains, arrays):
    for parts, array in zip(chains, arrays):
        for p in parts:
            p.terms[-1] = (array, *p.terms[-1][1:])


def double(array, axis, bit):
    return side_of(array, xor_permute(array, axis, bit), axis, bit)


def side_of(array, other, axis, bit):
    high = bit_of(axis, bit) == 1
    return jnp.concatenate([jnp.where(high, other, array), jnp.where(high, array, other)], axis=1)


def device_of(order):
    names = [b for axis in ("seq", "batch") for b in reversed(index_bits(axis))]
    last = len(names) - 1

    def device(shard):
        return sum((shard // (1 << (last - i))) % 2 * (1 << (last - names.index(b))) for i, b in enumerate(order))

    return device


def restored(gathered, order):
    names = [b for axis in ("seq", "batch") for b in reversed(index_bits(axis))]
    _, n, rows, width = gathered.shape
    cube = gathered.reshape([2] * len(names) + [n, rows, width])
    k = len(names)
    cube = cube.transpose([k] + [names.index(b) for b in order] + [k + 1, k + 2])
    return cube.reshape(n, -1, width).astype(f32)


def spread_body(half_steps, many, meta, *refs):
    sources, (kept_p, kept_q, other_p, other_q, up, out, into) = refs[: 3 * many], refs[3 * many :]
    width = out.shape[1]
    rows = out.shape[0] // many
    for j in range(many):
        first, b, c = sources[3 * j : 3 * j + 3]
        at = slice(j * rows, (j + 1) * rows)
        for i, source in enumerate((b[0, 0], b[0, 1], c[0, 0], c[0, 1])):
            up[at, i * width : (i + 1) * width] = source.astype(f32)
        out[at] = c[0, 2].astype(f32)
        into[at, :width] = first[0, 0].astype(f32)
    own = (pl.program_id(0) // half_steps) == lax.rem(meta[0], 2)
    for i, (kept, other) in enumerate(((kept_p, other_p), (kept_q, other_q))):
        value = jnp.where(own, kept[0].astype(f32), other[0].astype(f32))
        into[:, (i + 1) * width : (i + 2) * width] = value


def spread(meta, gathered, orders, kept, other):
    devices, stacked, rows, width = gathered.shape
    if rows % 8:
        half = width // 2
        high = lax.axis_index("seq") % 2 == 1
        x, y = (jnp.concatenate(p)[:, :half].astype(f32) for p in (kept, other))
        rest = jnp.concatenate([jnp.where(high, y, x), jnp.where(high, x, y)], axis=1)
        a = restored(gathered[:, 3:4], orders[0])
        b, c = restored(gathered[:, 4:], orders[1]), restored(gathered[:, :3], orders[2])
        return (jnp.concatenate([b[0], b[1], c[0], c[1]], axis=1), c[2],
                jnp.concatenate([a[0], rest[0], rest[1]], axis=1))
    places = [device_of(order) for order in orders]
    many = 4
    steps = devices // many
    half = steps // 2
    tall = many * rows
    piece = pl.BlockSpec((1, tall, width), lambda s: (0, s % half, 0))
    shape = jax.ShapeDtypeStruct
    sources = []
    for j in range(many):
        for size, block, place in ((1, 3, places[0]), (2, 2, places[1]), (3, 0, places[2])):
            sources.append(pl.BlockSpec(
                (1, size, rows, width), lambda s, i=block, p=place, j=j: (p(s * many + j), i, 0, 0)))
    return pl.pallas_call(
        partial(spread_body, half, many),
        grid=(steps,),
        in_specs=[SMEM, *sources, piece, piece, piece, piece],
        out_specs=[
            pl.BlockSpec((tall, 4 * width), lambda s: (s, 0)),
            pl.BlockSpec((tall, width), lambda s: (s, 0)),
            pl.BlockSpec((tall, 3 * width), lambda s: (s, 0)),
        ],
        out_shape=[shape((width, 4 * width), f32), shape((width, width), f32), shape((width, 3 * width), f32)],
        compiler_params=params(60),
        cost_estimate=cost(0, 6 * devices * stacked * rows * width),
        name="spread",
    )(meta, *[gathered] * (3 * many), *kept, *other)


def spread_down_body(half_steps, meta, kept_a, kept_b, other_a, other_b, target):
    own = (pl.program_id(0) // half_steps) == lax.rem(meta[0], 2)
    for first, kept, other in ((0, kept_a, other_a), (3, kept_b, other_b)):
        for j in range(kept.shape[0]):
            target[first + j] = jnp.where(own, kept[j].astype(f32), other[j].astype(f32))


def spread_down(meta, kept, other):
    _, half_rows, width = kept[0].shape
    rows = 96
    half = half_rows // rows
    piece = lambda n: pl.BlockSpec((n, rows, width), lambda s: (0, s % half, 0))
    return pl.pallas_call(
        partial(spread_down_body, half),
        grid=(2 * half,),
        in_specs=[SMEM, piece(3), piece(1), piece(3), piece(1)],
        out_specs=pl.BlockSpec((4, rows, width), lambda s: (0, s, 0)),
        out_shape=jax.ShapeDtypeStruct((4, 2 * half_rows, width), f32),
        compiler_params=params(48),
        cost_estimate=cost(0, 24 * width * width),
        name="spread_down",
    )(meta, *kept, *other).reshape(8 * half_rows, width)


def unpack_body(layout, meta, kept_p, kept_q, other_p, other_q, *refs):
    *targets, rows = refs
    core = lax.rem(meta[0], 2)
    for i, (kept, other) in enumerate(((kept_p, other_p), (kept_q, other_q))):
        rows[i] = jnp.where(core == 0, kept[0].astype(f32), other[0].astype(f32))
    for target, entry in zip(targets, layout):
        for (r, c), block, row, lane in entry:
            size, across = r.stop - r.start, c.stop - c.start
            part = rows[block, row : row + size, lane : lane + across]
            if len(target.shape) == 1:
                target[c] = part[0]
            else:
                target[r, c] = part


def unpack(meta, kept, other, layout, shapes):
    _, rows, width = kept[0].shape
    at = (rows - PACK) // PACK
    piece = pl.BlockSpec((1, PACK, width), lambda i: (0, at, 0))
    return pl.pallas_call(
        partial(unpack_body, layout),
        grid=(1,),
        in_specs=[SMEM, piece, piece, piece, piece],
        out_specs=[whole(s) for s in shapes],
        out_shape=[jax.ShapeDtypeStruct(s, f32) for s in shapes],
        scratch_shapes=[pltpu.VMEM((2, PACK, width), f32)],
        compiler_params=params(32),
        cost_estimate=cost(0, 2 << 20),
        name="unpack",
    )(meta, *kept, *other)


def shards(
    tokens, cotangent, lengths, norm1_gain, norm1_shift, in_weight, in_bias, conv_weight, conv_bias,
    filter_in, filter_in_bias, filter_mid, filter_mid_bias, filter_last, filter_last_bias, filter_out,
    decay_rate, skip_gain, out_weight, out_bias, norm2_gain, norm2_shift, up_weight, up_bias,
    down_weight, down_bias,
):
    buckets, rows, width = tokens.shape
    hidden_width = up_weight.shape[1]
    blocks = lax.axis_size("seq")
    devices = blocks * lax.axis_size("batch")
    count = buckets * rows
    meta = jnp.concatenate([lax.axis_index("seq")[None].astype(jnp.int32), lengths.astype(jnp.int32)])
    high_np, low_np = block_tables(rows)
    high, low = jnp.asarray(high_np), jnp.asarray(low_np)
    back = jnp.asarray(np.ascontiguousarray(high_np.T))
    line = lambda a: a.reshape(1, -1)

    halo = lax.ppermute(tokens[:, rows - HALO :], "seq", [(i, i + 1) for i in range(blocks - 1)])
    conv_w = conv_weight.reshape(3, 3, width)
    conv_b = conv_bias.reshape(3, width)
    normed, mixed, product, gate_out = front(
        meta, tokens, halo, line(norm1_gain), line(norm1_shift), in_weight, in_bias.reshape(3, width), conv_w, conv_b)
    far = exchange_far(product)
    table = jnp.asarray(features(rows * blocks, filter_in.shape[0]))
    sines, cosines = filter_layers(
        table, filter_in, filter_in_bias, filter_mid, filter_mid_bias, filter_last, filter_last_bias)
    hidden = sines[2]
    shaped, spectrum = filter_spectra(hidden, filter_out, line(decay_rate), high, low, blocks)
    far, spectrum = after(far, spectrum)
    products = exchange_near(far)
    mixture, gated = conv_forward(meta, products, spectrum, gate_out, line(skip_gain), high, back)

    flat = lambda a: a.reshape(count, width)
    (normed2, d_down, resid, active, d_up, g_up_bias, d_resid, d_mixer, d_gated, d_conv,
     g_norm2_gain, g_norm2_shift, g_out_bias) = middle(
        meta, flat(gated), out_weight, line(out_bias), flat(tokens), flat(cotangent), line(norm2_gain),
        line(norm2_shift), up_weight, line(up_bias), down_weight, flat(gate_out), buckets)
    cube = lambda a: a.reshape(buckets, rows, width)
    seq_bits, batch_bits = index_bits("seq"), index_bits("batch")
    core, far_seq, near_batch, far_batch = seq_bits[0], seq_bits[1:], batch_bits[:1], batch_bits[1:]
    orders = [near_batch + far_seq + far_batch, far_seq + far_batch + near_batch, far_batch + near_batch + far_seq]
    barrier = lax.optimization_barrier

    def wave(chains, at):
        return [halve(parts, *order[at]) for parts, order in zip(chains, orders)]

    far = exchange_far(cube(d_conv))
    first_kept, first_sent, g_first, *first_parts = short_backward(
        meta, (mixture, cube(d_gated)), mixed, normed, conv_w, conv_b)
    g_down_bias, *stacks = weight_grads(
        meta, active, d_up, normed2, d_down, flat(gated), d_mixer, first_kept, first_sent)
    kept, sent = stacks[:3], stacks[3:]
    far, sent, active = after(far, sent, active)
    block_out = layer_output(meta, active, down_weight, line(down_bias), resid, buckets)
    grads = exchange_near(far)
    come = [xor_permute(a, *core) for a in sent]
    come, grads, block_out = barrier((come, grads, block_out))
    stack = lambda k, c: Part([(k, 0, 0), (c, 0, 0)], k.shape[0], k.shape[1])
    chains = [[stack(k, c)] for k, c in zip(kept, come)]
    chains = wave(chains, 0)
    d_product, g_skip, lags = conv_backward(meta, grads, product, spectrum, line(skip_gain), high, back)

    come, d_product, lags = barrier((waiting(chains), d_product, lags))
    arrived(chains, come)
    chains = wave(chains, 1)
    in_kept, in_sent, g_mixed, *other_parts = short_backward(meta, (d_product,), mixed, normed, conv_w, conv_b)
    (g_filter_out, g_decay, g_filter_in, g_filter_in_bias, g_filter_mid, g_filter_mid_bias,
     g_filter_last, g_filter_last_bias) = filter_backward(
        lags, back, hidden.astype(bf16), filter_out.astype(bf16), line(decay_rate), shaped, table, sines, cosines,
        filter_mid, filter_last)

    come, in_sent, g_filter_out, g_mixed = barrier((waiting(chains), in_sent, g_filter_out, g_mixed))
    arrived(chains, come)
    chains = wave(chains, 2)
    shapes = [
        (width,), (width,), (3 * width,), (3, 3 * width), (3 * width,), filter_in.shape, filter_in_bias.shape,
        filter_mid.shape, filter_mid_bias.shape, filter_last.shape, filter_last_bias.shape, filter_out.shape,
        (width,), (width,), (width,), (width,), (width,), (hidden_width,), (width,),
    ]
    layout = pack_layout(width, shapes)
    smalls = [
        g_filter_in, g_filter_in_bias, g_filter_mid, g_filter_mid_bias, g_filter_last, g_filter_last_bias,
        g_filter_out, g_decay, g_skip, g_out_bias, g_norm2_gain, g_norm2_shift, g_up_bias, g_down_bias,
    ]
    g_tokens, d_halo, in_kept, in_sent = token_grads(
        meta, g_first, g_mixed, in_weight, tokens, halo, line(norm1_gain), cube(d_resid), first_parts + other_parts,
        smalls, layout, in_kept, in_sent)

    come, in_kept, in_sent = barrier((waiting(chains), in_kept, in_sent))
    arrived(chains, come)
    in_come = xor_permute(in_sent, *core)
    for at in range(3, len(orders[0])):
        chains = wave(chains, at)
    arriving = lax.ppermute(d_halo[:, HALO - 2 :], "seq", [(i + 1, i) for i in range(blocks - 1)])
    g_tokens = g_tokens.at[:, rows - 2 :].add(arriving)
    whole_rows = in_kept.shape[1]
    order = orders[0]
    x, y, rest = near_batch[0], far_seq[0], far_seq[1:] + far_batch

    def in_sums():
        pair = [[Part([(in_kept, i, 0), (in_come, i, 0)], 1, whole_rows)] for i in range(2)]
        for steps in ((x, y), (y, x)):
            pair = [halve(parts, *step) for parts, step in zip(pair, steps)]
            arrived(pair, (yield waiting(pair)))
        joined = pair[0] + pair[1]
        for step in rest:
            joined = halve(joined, *step)
            arrived([joined], (yield waiting([joined])))
        done = jnp.concatenate([p.total(0, p.rows) for p in joined], axis=0)
        for step in reversed(rest):
            (come,) = yield [xor_permute(done, *step)]
            done = side_of(done, come, *step)
        pair = [done[:1], done[1:]]
        for steps in ((y, x), (x, y)):
            come = yield [xor_permute(a, *step) for a, step in zip(pair, steps)]
            pair = [side_of(a, c, *step) for a, c, step in zip(pair, come, steps)]
        come = yield [xor_permute(a, *core) for a in pair]
        return pair, come

    in_steps = in_sums()
    in_wait = next(in_steps)
    come, in_wait = barrier((waiting(chains), in_wait))
    arrived(chains, come)
    sums = [p.total(0, p.rows) for parts in chains for p in parts]
    both = jnp.concatenate([sums[2], sums[0][3:], sums[1][1:]], axis=0)
    gathered = lax.all_gather(both, ("seq", "batch"), axis=0)

    down = [sums[0][:3], sums[1][:1]]
    for steps in zip(reversed(orders[0]), reversed(orders[1])):
        down = [double(a, *step) for a, step in zip(down, steps)]
    grad_down_weight = spread_down(meta, down, [xor_permute(a, *core) for a in down])

    in_result, left = None, 2 * len(order) + 1
    while in_result is None:
        left -= 1
        if left == LAST_STEPS:
            in_wait, grad_down_weight = barrier((in_wait, grad_down_weight))
        if left == 2 * len(order) - 2:
            in_wait, g_tokens = barrier((in_wait, g_tokens))
        try:
            in_wait = in_steps.send(in_wait)
        except StopIteration as end:
            in_result = end.value
    in_kept, in_come = in_result
    grad_up_weight, grad_out_weight, grad_in_weight = spread(
        meta, gathered, [[core, *o] for o in orders], in_kept, in_come)
    (n1g, n1s, inb, cw, cb, fi, fib, fm, fmb, fl, flb, fo, dr, sg, ob, n2g, n2s, ub, db) = unpack(
        meta, in_kept, in_come, layout, shapes)
    return (
        cube(block_out), g_tokens, n1g, n1s, grad_in_weight, inb, cw, cb, fi, fib, fm, fmb, fl, flb, fo, dr, sg,
        grad_out_weight, ob, n2g, n2s, grad_up_weight, ub, grad_down_weight, db,
    )


def solution(mesh):
    split = P("batch", "seq", None)
    return jax.shard_map(
        shards,
        mesh=mesh,
        in_specs=(split, split, P("batch")) + (P(),) * 23,
        out_specs=(split, split) + (P(),) * 23,
        check_vma=False,
    )
```
